32 devices in a mesh: seq: 4 (over x, core), blk: 8 (over z, y).
Axes of the slice: x: 2, y: 2, z: 4, core: 2. Of those that a mesh axis runs over, the one named last changes fastest.
Arguments:
- latents: bfloat16 [4, 8192, 512], P('seq', 'blk'), may hold values from -6 to 6
- tokens: bfloat16 [4, 8192, 512], P('seq', 'blk'), may hold values from -6 to 6
- lengths: int32 [4, 4], P('seq'), may hold values from 1792 to 2048, as said below
- gain_lat: float32 [512], replicated, may hold values from 0.1 to 1.9
- gain_tok: float32 [512], replicated, may hold values from 0.1 to 1.9
- gain_mlp: float32 [512], replicated, may hold values from 0.1 to 1.9
- w_query: bfloat16 [512, 512], replicated, may hold values from -0.625 to 0.625
- w_key: bfloat16 [512, 512], replicated, may hold values from -0.25 to 0.25
- w_value: bfloat16 [512, 512], replicated, may hold values from -0.25 to 0.25
- w_out: bfloat16 [512, 512], replicated, may hold values from -0.5 to 0.5
- w_up: bfloat16 [512, 2048], replicated, may hold values from -0.25 to 0.25
- w_down: bfloat16 [2048, 512], replicated, may hold values from -0.125 to 0.125
- d_out: bfloat16 [4, 8192, 512], P('seq', 'blk'), may hold values from -6 to 6
Outputs:
- out_latents: bfloat16 [4, 8192, 512], P('seq', 'blk')
- d_latents: float32 [4, 8192, 512], P('seq', 'blk')
- d_tokens: float32 [4, 8192, 512], P('seq', 'blk')
- d_w_query: float32 [512, 512], replicated
- d_w_key: float32 [512, 512], replicated
- d_w_value: float32 [512, 512], replicated
- d_w_out: float32 [512, 512], replicated
- d_w_up: float32 [512, 2048], replicated
- d_w_down: float32 [2048, 512], replicated
- d_gain_lat: float32 [512], replicated
- d_gain_tok: float32 [512], replicated
- d_gain_mlp: float32 [512], replicated
The draws below stay inside these ranges and needn't reach their ends.
Inputs may be any that keep to these rules, and one draw needn't show every extreme that they name: Positions past the sum of a row's lengths are padding.
All inputs are finite; a program needn't handle non-finite values.
Results may differ from the reference program's by a relative error of at most 0.024.
Values may be sent and summed in bfloat16 or wider, within the bound.
No kernel may reach another device: no remote copies, remote signals or barrier semaphores. Data moves between devices by JAX's collectives and lax.ppermute only.
A program may use at most 256 MiB of HBM per device.

```python
import jax
import jax.numpy as jnp
from jax import lax

D = 512
FF = 2048
LAT = 2048
SCENES = 4
SEQS = 4
LENGTH = 8192
LATS = 8192


def draw_lengths(key, part):
    key = jax.random.fold_in(key, 11)
    keys = jax.random.split(key, 2)
    base = LENGTH // SCENES
    spread = LENGTH // (8 * SCENES)
    jitter = jax.random.randint(keys[0], (SEQS, SCENES), 0, spread + 1)
    first = jax.random.randint(keys[1], (SEQS, 1), 0, SCENES)
    places = jnp.arange(SCENES, dtype=jnp.int32)[None, :]
    jitter = jnp.where(places == first, 0, jnp.where(places == (first + 1) % SCENES, spread, jitter))
    return (base - jitter).astype(jnp.int32)


def shard_levels(own_key, shape, shards, low, high):
    level = 1.0
    for position, blocks in shards:
        heights = jax.random.uniform(jax.random.fold_in(jax.random.fold_in(own_key, 6), position), (blocks,), jnp.float32, low / len(shards), high / len(shards))
        level = level * jnp.repeat(jnp.exp(heights), shape[position] // blocks).reshape((-1,) + (1,) * (len(shape) - 1 - position))
    return level


def bell_draw(stream_key, dims, width, reach, pieces=(), held_as=jnp.bfloat16):
    entries = width * jax.random.normal(stream_key, dims, jnp.float32)
    if pieces:
        entries = entries * shard_levels(stream_key, dims, pieces, -0.22, 0.18)
    return jnp.clip(entries, -reach, reach).astype(held_as)


def setup_inputs(seed: int = 0) -> dict:
    key_of = jax.random.split(jax.random.key(seed), 14)
    return {
        "latents": bell_draw(key_of[0], (SEQS, LATS, D), 1.0, 6.0, ((0, 4), (1, 8))),
        "tokens": bell_draw(key_of[1], (SEQS, LENGTH, D), 1.0, 6.0, ((0, 4), (1, 8))),
        "lengths": draw_lengths(jax.random.fold_in(key_of[13], 71), 0),
        "gain_lat": jnp.clip(1.0 + 0.18 * jax.random.normal(key_of[3], (D,), jnp.float32), 0.1, 1.9),
        "gain_tok": jnp.clip(1.0 + 0.18 * jax.random.normal(key_of[4], (D,), jnp.float32), 0.1, 1.9),
        "gain_mlp": jnp.clip(1.0 + 0.18 * jax.random.normal(key_of[5], (D,), jnp.float32), 0.1, 1.9),
        "w_query": bell_draw(key_of[6], (D, D), (D // 6) ** -0.5, 0.625),
        "w_key": bell_draw(key_of[7], (D, D), D ** -0.5, 0.25),
        "w_value": bell_draw(key_of[8], (D, D), D ** -0.5, 0.25),
        "w_out": bell_draw(key_of[9], (D, D), (D // 4) ** -0.5, 0.5),
        "w_up": bell_draw(key_of[10], (D, FF), D ** -0.5, 0.25),
        "w_down": bell_draw(key_of[11], (FF, D), FF ** -0.5, 0.125),
        "d_out": bell_draw(key_of[12], (SEQS, LATS, D), 1.0, 6.0, ((0, 4), (1, 8))),
    }


EPSILON = 1e-05
NEGATIVE = -1e+30

@jax.custom_vjp
def low(v):
    return lax.optimization_barrier(v.astype(jnp.bfloat16)).astype(jnp.float32)

@jax.custom_vjp
def low_back(v):
    return v

def low_keep(v):
    return (low(v), None)

def low_pass(kept, grad):
    return (grad,)

def back_keep(v):
    return (v, None)

def back_low(kept, grad):
    return (low(grad),)
low.defvjp(low_keep, low_pass)
low_back.defvjp(back_keep, back_low)

def normed(values, gain):
    center = values - lax.optimization_barrier(jnp.mean(values, axis=-1, keepdims=True))
    spread = lax.optimization_barrier(jnp.mean(center * center, axis=-1, keepdims=True))
    return center * lax.rsqrt(spread + EPSILON) * gain

def product(left, right):
    return jnp.dot(left, right, precision=lax.Precision.HIGHEST)

def scene_numbers(scene_lengths):
    bounds = jnp.cumsum(scene_lengths).astype(jnp.int32)
    places = jnp.arange(LENGTH, dtype=jnp.int32)
    return lax.optimization_barrier(jnp.sum((places[:, None] >= bounds[None, :]).astype(jnp.int32), axis=1)).astype(jnp.int32)

def sequence(latent_rows, token_rows, scene_lengths, gain_lat, gain_tok, gain_mlp, w_query, w_key, w_value, w_out, w_up, w_down):
    segment = scene_numbers(scene_lengths)
    scale = D ** (-0.5)
    lat_normed = low(normed(latent_rows, gain_lat))
    query = low(low_back(product(lat_normed, w_query)))
    tok_normed = low(normed(token_rows, gain_tok))
    keys = low(low_back(product(tok_normed, w_key)))
    values = low(low_back(product(tok_normed, w_value)))

    def one_scene(query_set, scene_id):
        raw = low_back(product(query_set, keys.T)) * scale
        included = (segment == scene_id)[None, :]
        scores = jnp.where(included, raw, NEGATIVE)
        top = lax.optimization_barrier(jnp.max(scores, axis=1, keepdims=True))
        weights = jnp.where(included, jnp.exp(scores - top), 0.0)
        total = lax.optimization_barrier(jnp.sum(weights, axis=1, keepdims=True))
        return product(low(weights), values) / total
    scene_step = jax.checkpoint(one_scene)
    query_sets = jnp.transpose(query.reshape(LAT, SCENES, D), (1, 0, 2))
    attended = lax.map(lambda pair: scene_step(pair[0], pair[1]), (query_sets, jnp.arange(SCENES, dtype=jnp.int32)))
    attended = jnp.transpose(attended, (1, 0, 2)).reshape(SCENES * LAT, D)
    mixed = low(low_back(attended))
    state = latent_rows + low_back(product(mixed, w_out))
    mlp_in = low(normed(state, gain_mlp))
    inner = low(jax.nn.gelu(low_back(product(mlp_in, w_up))))
    return state + low_back(product(inner, w_down))

def reference(latents, tokens, lengths, gain_lat, gain_tok, gain_mlp, w_query, w_key, w_value, w_out, w_up, w_down, d_out):

    def whole(latent_all, token_all, g_one, g_two, g_three, m_query, m_key, m_value, m_out, m_up, m_down):
        sequence_step = jax.checkpoint(sequence)

        def one_sequence(triple):
            return sequence_step(triple[0], triple[1], triple[2], g_one, g_two, g_three, m_query, m_key, m_value, m_out, m_up, m_down)
        return lax.map(one_sequence, (latent_all, token_all, lengths))
    output, pullback = jax.vjp(whole, latents.astype(jnp.float32), tokens.astype(jnp.float32), gain_lat.astype(jnp.float32), gain_tok.astype(jnp.float32), gain_mlp.astype(jnp.float32), w_query.astype(jnp.float32), w_key.astype(jnp.float32), w_value.astype(jnp.float32), w_out.astype(jnp.float32), w_up.astype(jnp.float32), w_down.astype(jnp.float32))
    grads = pullback(d_out.astype(jnp.float32))
    return (output.astype(jnp.bfloat16), grads[0], grads[1], grads[5], grads[6], grads[7], grads[8], grads[9], grads[10], grads[2], grads[3], grads[4])
```

```python
import functools
import math

import jax
import jax.numpy as jnp
from jax import lax
from jax.experimental import pallas as pl
from jax.experimental.pallas import tpu as pltpu
from jax.sharding import PartitionSpec as P

EPSILON = 1e-05
NEGATIVE = -1e30
LOG2E = 1.4426950408889634
GELU_C = math.sqrt(2.0 / math.pi)
GELU_A = 0.044715
F32 = jnp.float32
BF16 = jnp.bfloat16
NN = (((1,), (0,)), ((), ()))
NT = (((1,), (1,)), ((), ()))
TN = (((0,), (0,)), ((), ()))
TILE = 256
VMEM_LIMIT = 60 << 20


def dot(left, right, dims=NN):
    return lax.dot_general(left, right, dims, preferred_element_type=F32)


def params():
    return pltpu.CompilerParams(vmem_limit_bytes=VMEM_LIMIT)


def whole(shape):
    zeros = (0,) * len(shape)
    return pl.BlockSpec(shape, lambda *_: zeros, pipeline_mode=pl.Buffered(1))


def norm_parts(rows):
    center = rows - jnp.mean(rows, axis=-1, keepdims=True)
    spread = jnp.mean(center * center, axis=-1, keepdims=True)
    inverse = lax.rsqrt(spread + EPSILON)
    return center * inverse, inverse


def norm_back(d_normed, unit, inverse, gain):
    d_unit = d_normed * gain
    mean_d = jnp.mean(d_unit, axis=-1, keepdims=True)
    mean_p = jnp.mean(d_unit * unit, axis=-1, keepdims=True)
    return inverse * (d_unit - mean_d - unit * mean_p)


def kv_kernel(tok_ref, gain_ref, wk_ref, wv_ref, k_ref, v_ref):
    unit, _ = norm_parts(tok_ref[...].astype(F32))
    low = (unit * gain_ref[...]).astype(BF16)
    k_ref[...] = dot(low, wk_ref[...]).astype(BF16)
    v_ref[...] = dot(low, wv_ref[...]).astype(BF16)


def keys_values(tok, gain, w_key, w_value):
    rows, width = tok.shape
    block = pl.BlockSpec((TILE, width), lambda i: (i, 0))
    shape = jax.ShapeDtypeStruct((rows, width), BF16)
    return pl.pallas_call(
        kv_kernel,
        grid=(rows // TILE,),
        in_specs=[block, whole(gain.shape), whole(w_key.shape), whole(w_value.shape)],
        out_specs=[block, block],
        out_shape=[shape, shape],
        compiler_params=params(),
        name="keys_values",
    )(tok, gain, w_key, w_value)


def forward_kernel(pieces, scale, info_ref, lat_ref, gl_ref, gm_ref, wq_ref, wo_ref, wu_ref, wd_ref, *refs):
    count = len(pieces)
    k_refs, v_refs = refs[:count], refs[count : 2 * count]
    refs = refs[2 * count :]
    q_ref, mixed_ref, mlp_ref, state_ref, inner_ref, slope_ref, out_ref, inv_ref = refs[:8]
    w_refs, refs = refs[8 : 8 + count], refs[8 + count :]
    s_refs, acc_ref = refs[:count], refs[count]
    rows = lat_ref.shape[0]
    begin, end = info_ref[0], info_ref[1]
    lat = lat_ref[...].astype(F32)
    unit, _ = norm_parts(lat)
    query = dot((unit * gl_ref[...]).astype(BF16), wq_ref[...]).astype(BF16)
    q_ref[...] = query
    top = jnp.full((8, rows), NEGATIVE, F32)
    for p in range(count):

        def scores(t, top, p=p):
            span = pl.ds(pl.multiple_of(t * TILE, TILE), TILE)
            s = dot(k_refs[p][span, :], query, NT) * (scale * LOG2E)
            place = info_ref[2 + 3 * p] + t * TILE + lax.broadcasted_iota(jnp.int32, (TILE, 1), 0)
            s = s + jnp.where((place >= begin) & (place < end), 0.0, NEGATIVE)
            s_refs[p][span, :] = s
            return jnp.maximum(top, jnp.max(s.reshape(TILE // 8, 8, rows), axis=0))

        top = lax.fori_loop(info_ref[3 + 3 * p], info_ref[4 + 3 * p], scores, top)
    top = jnp.max(top, axis=0, keepdims=True)
    total = jnp.zeros((8, rows), F32)
    acc_ref[...] = jnp.zeros_like(acc_ref)
    for p in range(count):

        def weigh(t, total, p=p):
            span = pl.ds(pl.multiple_of(t * TILE, TILE), TILE)
            w = jnp.exp2(s_refs[p][span, :] - top)
            low = w.astype(BF16)
            w_refs[p][span, :] = low
            acc_ref[...] += dot(low, v_refs[p][span, :], TN)
            return total + jnp.sum(w.reshape(TILE // 8, 8, rows), axis=0)

        total = lax.fori_loop(info_ref[3 + 3 * p], info_ref[4 + 3 * p], weigh, total)
    inverse = 1.0 / jnp.sum(total, axis=0, keepdims=True)
    inv_col = jnp.transpose(jnp.broadcast_to(inverse, (8, rows)))[:, :1]
    inv_ref[...] = jnp.broadcast_to(inv_col, inv_ref.shape)
    mixed = (acc_ref[...] * inv_col).astype(BF16)
    mixed_ref[...] = mixed
    state = lat + dot(mixed, wo_ref[...])
    state_ref[...] = state
    unit, _ = norm_parts(state)
    low = (unit * gm_ref[...]).astype(BF16)
    mlp_ref[...] = low
    out = state
    hidden = wu_ref.shape[1]
    step = min(512, hidden)
    for f in range(0, hidden, step):
        u = dot(low, wu_ref[:, f : f + step])
        square = u * u
        t = jnp.tanh(GELU_C * (u + GELU_A * (square * u)))
        half = 0.5 * (1.0 + t)
        inner = (u * half).astype(BF16)
        slope = half + (0.5 * GELU_C) * u * (1.0 - t * t) * (1.0 + 3.0 * GELU_A * square)
        inner_ref[:, f : f + step] = inner
        slope_ref[:, f : f + step] = slope.astype(BF16)
        out = out + dot(inner, wd_ref[f : f + step, :])
    out_ref[...] = out.astype(BF16)


def forward(info, lat, gl, gm, wq, wo, wu, wd, keys, values, scale):
    rows, width = lat.shape
    hidden = wu.shape[1]
    chunk = min(rows, TILE)
    pieces = [k.shape[0] for k in keys]

    def by_rows(columns):
        return pl.BlockSpec((chunk, columns), lambda i, *_: (i, 0))

    def shape(columns, dtype=BF16):
        return jax.ShapeDtypeStruct((rows, columns), dtype)

    return pl.pallas_call(
        functools.partial(forward_kernel, pieces, scale),
        grid_spec=pltpu.PrefetchScalarGridSpec(
            num_scalar_prefetch=1,
            grid=(rows // chunk,),
            in_specs=[by_rows(width)]
            + [whole(a.shape) for a in (gl, gm, wq, wo, wu, wd)]
            + [whole(a.shape) for a in (*keys, *values)],
            out_specs=[
                by_rows(width),
                by_rows(width),
                by_rows(width),
                by_rows(width),
                by_rows(hidden),
                by_rows(hidden),
                by_rows(width),
                by_rows(128),
            ]
            + [pl.BlockSpec((n, chunk), lambda i, *_: (0, i)) for n in pieces],
            scratch_shapes=[pltpu.VMEM((n, chunk), F32) for n in pieces] + [pltpu.VMEM((chunk, width), F32)],
        ),
        out_shape=[
            shape(width),
            shape(width),
            shape(width),
            shape(width, F32),
            shape(hidden),
            shape(hidden),
            shape(width),
            shape(128, F32),
        ]
        + [jax.ShapeDtypeStruct((n, rows), BF16) for n in pieces],
        compiler_params=params(),
        name="forward",
    )(info, lat, gl, gm, wq, wo, wu, wd, *keys, *values)


def mlp_back_kernel(
    chunks,
    slabs,
    cot_ref,
    slope_ref,
    state_ref,
    mixed_ref,
    mlp_ref,
    inner_ref,
    inv_ref,
    gm_ref,
    wo_ref,
    wu_ref,
    wd_ref,
    dstate_ref,
    datt_ref,
    delta_ref,
    pack_ref,
    dwo_ref,
    dgain_ref,
    dpre_ref,
    dproj_ref,
):
    i = pl.program_id(0)
    chunk = slope_ref.shape[0]
    hidden = wu_ref.shape[1]
    step = hidden // slabs

    @pl.when(i < chunks)
    def _():
        span = pl.ds(pl.multiple_of(i * chunk, chunk), chunk)
        cot = cot_ref[span, :]
        d_mlp = jnp.zeros(state_ref.shape, F32)
        for f in range(0, hidden, step):
            d_inner = dot(cot, wd_ref[f : f + step, :], NT)
            d_pre = (slope_ref[:, f : f + step].astype(F32) * d_inner).astype(BF16)
            dpre_ref[span, f : f + step] = d_pre
            d_mlp = d_mlp + dot(d_pre, wu_ref[:, f : f + step], NT)
        unit, inverse = norm_parts(state_ref[...])
        part = jnp.sum((d_mlp * unit).reshape(chunk // 8, 8, d_mlp.shape[1]), axis=0)
        dgain_ref[...] = jnp.where(i == 0, part, dgain_ref[...] + part)
        d_state = cot.astype(F32) + norm_back(d_mlp, unit, inverse, gm_ref[...])
        dstate_ref[...] = d_state
        d_proj = d_state.astype(BF16)
        dproj_ref[span, :] = d_proj
        d_att = (dot(d_proj, wo_ref[...], NT) * inv_ref[:, :1]).astype(BF16)
        datt_ref[...] = d_att
        delta = jnp.sum(d_att.astype(F32) * mixed_ref[span, :].astype(F32), axis=-1, keepdims=True)
        delta_ref[...] = jnp.transpose(jnp.broadcast_to(delta, (chunk, 128)))[:8, :]

    for j in range(slabs):

        @pl.when(i == chunks + j)
        def _(j=j):
            pack_ref[...] = dot(inner_ref[:, j * step : (j + 1) * step], cot_ref[...], TN).astype(BF16)

        @pl.when(i == chunks + slabs + j)
        def _(j=j):
            pack_ref[...] = dot(mlp_ref[...], dpre_ref[:, j * step : (j + 1) * step], TN).astype(BF16)

    @pl.when(i == chunks + 2 * slabs)
    def _():
        dwo_ref[...] = dot(mixed_ref[...], dproj_ref[...], TN).astype(BF16)


def mlp_back(cot, slope, state, mixed, mlp, inner, inv, gm, wo, wu, wd):
    rows, width = cot.shape
    hidden = wu.shape[1]
    slabs = hidden // width
    chunk = min(rows, TILE)
    chunks = rows // chunk

    def by_rows(columns):
        return pl.BlockSpec((chunk, columns), lambda i: (jnp.minimum(i, chunks - 1), 0))

    return pl.pallas_call(
        functools.partial(mlp_back_kernel, chunks, slabs),
        grid=(chunks + 2 * slabs + 1,),
        in_specs=[
            whole(cot.shape),
            by_rows(hidden),
            by_rows(width),
            whole(mixed.shape),
            whole(mlp.shape),
            whole(inner.shape),
            by_rows(128),
            whole(gm.shape),
            whole(wo.shape),
            whole(wu.shape),
            whole(wd.shape),
        ],
        out_specs=[
            by_rows(width),
            by_rows(width),
            pl.BlockSpec((8, chunk), lambda i: (0, jnp.minimum(i, chunks - 1))),
            pl.BlockSpec((width, width), lambda i: (jnp.clip(i - chunks, 0, 2 * slabs - 1), 0)),
            whole((width, width)),
            whole((8, width)),
        ],
        out_shape=[
            jax.ShapeDtypeStruct((rows, width), F32),
            jax.ShapeDtypeStruct((rows, width), BF16),
            jax.ShapeDtypeStruct((8, rows), F32),
            jax.ShapeDtypeStruct((2 * hidden, width), BF16),
            jax.ShapeDtypeStruct((width, width), BF16),
            jax.ShapeDtypeStruct((8, width), F32),
        ],
        scratch_shapes=[pltpu.VMEM((rows, hidden), BF16), pltpu.VMEM((rows, width), BF16)],
        compiler_params=params(),
        name="mlp_back",
    )(cot, slope, state, mixed, mlp, inner, inv, gm, wo, wu, wd)


def attention_back_kernel(tiles, scale, info_ref, q_ref, datt_ref, delta_ref, wk_ref, wv_ref, gain_ref, *refs):
    count = len(tiles)
    k_refs, v_refs, t_refs, w_refs = (refs[j * count : (j + 1) * count] for j in range(4))
    refs = refs[4 * count :]
    dtok_refs = refs[:count]
    dq_ref, dwk_ref, dwv_ref, dgain_ref, akey_ref, aval_ref = refs[count:]
    i = pl.program_id(0)
    width = q_ref.shape[1]

    @pl.when(i == 0)
    def _():
        dq_ref[...] = jnp.zeros_like(dq_ref)
        akey_ref[...] = jnp.zeros_like(akey_ref)
        aval_ref[...] = jnp.zeros_like(aval_ref)
        dgain_ref[...] = jnp.zeros_like(dgain_ref)

    first = 0
    for p in range(count):
        t = i - first
        inside = (t >= 0) & (t < tiles[p])
        active = inside & (t >= info_ref[3 + 3 * p]) & (t < info_ref[4 + 3 * p])

        @pl.when(active)
        def _(p=p):
            keys, weights = k_refs[p][...], w_refs[p][...]
            d_prob = dot(v_refs[p][...], datt_ref[...], NT)
            d_score = (weights.astype(F32) * (d_prob - delta_ref[:1, :])).astype(BF16)
            d_key = (dot(d_score, q_ref[...]) * scale).astype(BF16)
            d_value = dot(weights, datt_ref[...]).astype(BF16)
            dq_ref[...] += dot(d_score, keys, TN)
            unit, _ = norm_parts(t_refs[p][...].astype(F32))
            low = (unit * gain_ref[...]).astype(BF16)
            d_tok = dot(d_key, wk_ref[...], NT) + dot(d_value, wv_ref[...], NT)
            dtok_refs[p][...] = d_tok.astype(BF16)
            dgain_ref[...] += jnp.sum((d_tok * unit).reshape(TILE // 8, 8, width), axis=0)
            akey_ref[...] += dot(low, d_key, TN)
            aval_ref[...] += dot(low, d_value, TN)

        @pl.when(inside & jnp.logical_not(active))
        def _(p=p):
            dtok_refs[p][...] = jnp.zeros_like(dtok_refs[p])

        first += tiles[p]

    @pl.when(i == first - 1)
    def _():
        dwk_ref[...] = akey_ref[...].astype(BF16)
        dwv_ref[...] = aval_ref[...].astype(BF16)


def attention_back(info, q, datt, delta, wk, wv, gain, keys, values, tokens, weights, scale):
    rows, width = q.shape
    tiles = [k.shape[0] // TILE for k in keys]
    firsts = [sum(tiles[:p]) for p in range(len(tiles))]

    def tiled(p, columns):
        return pl.BlockSpec((TILE, columns), lambda i, *_: (jnp.clip(i - firsts[p], 0, tiles[p] - 1), 0))

    every = range(len(tiles))
    return pl.pallas_call(
        functools.partial(attention_back_kernel, tiles, scale),
        grid_spec=pltpu.PrefetchScalarGridSpec(
            num_scalar_prefetch=1,
            grid=(sum(tiles),),
            in_specs=[whole(a.shape) for a in (q, datt, delta, wk, wv, gain)]
            + [tiled(p, width) for _ in range(3) for p in every]
            + [tiled(p, rows) for p in every],
            out_specs=[tiled(p, width) for p in every]
            + [whole((rows, width)), whole((width, width)), whole((width, width)), whole((8, width))],
            scratch_shapes=[pltpu.VMEM((width, width), F32), pltpu.VMEM((width, width), F32)],
        ),
        out_shape=[jax.ShapeDtypeStruct(k.shape, BF16) for k in keys]
        + [
            jax.ShapeDtypeStruct((rows, width), F32),
            jax.ShapeDtypeStruct((width, width), BF16),
            jax.ShapeDtypeStruct((width, width), BF16),
            jax.ShapeDtypeStruct((8, width), F32),
        ],
        compiler_params=params(),
        name="attention_back",
    )(info, q, datt, delta, wk, wv, gain, *keys, *values, *tokens, *weights)


def latent_back_kernel(chunks, scale, dq_ref, lat_ref, dstate_ref, gain_ref, wq_ref, dlat_ref, dwq_ref, dgain_ref, acc_ref):
    i = pl.program_id(0)
    unit, inverse = norm_parts(lat_ref[...].astype(F32))
    gain = gain_ref[...]
    low = (unit * gain).astype(BF16)
    d_query = (dq_ref[...] * scale).astype(BF16)
    d_low = dot(d_query, wq_ref[...], NT)
    dlat_ref[...] = (dstate_ref[...] + norm_back(d_low, unit, inverse, gain)).astype(BF16)
    part = jnp.sum((d_low * unit).reshape(unit.shape[0] // 8, 8, unit.shape[1]), axis=0)
    dgain_ref[...] = jnp.where(i == 0, part, dgain_ref[...] + part)
    d_w = dot(low, d_query, TN)
    acc_ref[...] = jnp.where(i == 0, d_w, acc_ref[...] + d_w)

    @pl.when(i == chunks - 1)
    def _():
        dwq_ref[...] = acc_ref[...].astype(BF16)


def latent_back(dq, lat, dstate, gain, wq, scale):
    rows, width = lat.shape
    chunk = min(rows, TILE)
    block = pl.BlockSpec((chunk, width), lambda i: (i, 0))
    return pl.pallas_call(
        functools.partial(latent_back_kernel, rows // chunk, scale),
        grid=(rows // chunk,),
        in_specs=[block, block, block, whole(gain.shape), whole(wq.shape)],
        out_specs=[block, whole((width, width)), whole((8, width))],
        out_shape=[
            jax.ShapeDtypeStruct((rows, width), BF16),
            jax.ShapeDtypeStruct((width, width), BF16),
            jax.ShapeDtypeStruct((8, width), F32),
        ],
        scratch_shapes=[pltpu.VMEM((width, width), F32)],
        compiler_params=params(),
        name="latent_back",
    )(dq, lat, dstate, gain, wq)


def token_back_kernel(count, tok_ref, gain_ref, *refs):
    unit, inverse = norm_parts(tok_ref[...].astype(F32))
    total = refs[0][...].astype(F32)
    for ref in refs[1:count]:
        total = total + ref[...].astype(F32)
    refs[count][...] = norm_back(total, unit, inverse, gain_ref[...])


def token_back(tok, gain, parts):
    rows, width = tok.shape
    block = pl.BlockSpec((TILE, width), lambda i: (i, 0))
    return pl.pallas_call(
        functools.partial(token_back_kernel, len(parts)),
        grid=(rows // TILE,),
        in_specs=[block, whole(gain.shape)] + [block] * len(parts),
        out_specs=block,
        out_shape=jax.ShapeDtypeStruct((rows, width), F32),
        compiler_params=params(),
        name="token_back",
    )(tok, gain, *parts)


def exchange(value, blocks, flip):
    return lax.ppermute(value, "blk", [(i, i ^ flip) for i in range(blocks)])


def local(
    blocks, latents, tokens, lengths, gain_lat, gain_tok, gain_mlp, w_query, w_key, w_value, w_out, w_up, w_down, d_out
):
    lat, tok, cot = latents[0], tokens[0], d_out[0]
    scene_lengths = lengths[0]
    scenes = scene_lengths.shape[0]
    group = blocks // scenes
    span, width = tok.shape
    rows = lat.shape[0]
    part = rows // scenes
    scale = width ** (-0.5)
    position = lax.axis_index("blk")
    scene, member = position // group, position % group
    gl, gt, gm = (g.reshape(1, width) for g in (gain_lat, gain_tok, gain_mlp))

    order = jnp.arange(scenes, dtype=jnp.int32)
    begin = jnp.sum(jnp.where(order < scene, scene_lengths, 0))
    end = begin + jnp.sum(jnp.where(order == scene, scene_lengths, 0))

    def to_scenes(value):
        by_scene = jnp.swapaxes(value.reshape(part, scenes, width), 0, 1)
        moved = []
        for k in range(scenes):
            mine = lax.dynamic_index_in_dim(by_scene, scene ^ k, 0, keepdims=False)
            moved.append(exchange(mine, blocks, group * k) if k else mine)
        return jnp.concatenate(moved, axis=0)

    def from_scenes(value):
        moved = []
        for k in range(scenes):
            mine = value[k * part : (k + 1) * part]
            moved.append(exchange(mine, blocks, group * k) if k else mine)
        stacked = jnp.stack(moved, axis=0)
        stacked = jnp.stack([lax.dynamic_index_in_dim(stacked, scene ^ j, 0, keepdims=False) for j in range(scenes)], 1)
        return stacked.reshape(rows, width)

    lat_set = to_scenes(lat)
    pieces = [tok] + [exchange(tok, blocks, k) for k in range(1, group)]
    tail_rows = (scenes - 1) * group * span // 8
    tail_parts = []
    taken = 0
    while taken < tail_rows:
        owner = group - 1 - taken // span
        size = min(span, tail_rows - taken)
        block = pieces[0]
        for k in range(1, group):
            block = jnp.where(member == owner ^ k, pieces[k], block)
        tail_parts.insert(0, block[span - size :])
        taken += size
    tail = jnp.concatenate(tail_parts, axis=0) if len(tail_parts) > 1 else tail_parts[0]
    forward_pairs = [(i, i + group) for i in range(blocks - group)]
    tail = lax.ppermute(tail, "blk", forward_pairs)
    cot_set = to_scenes(cot)

    tok_set = [tail] + pieces[1:] + pieces[:1]
    starts = [scene * group * span - tail_rows]
    starts += [(scene * group + (member ^ k)) * span for k in [*range(1, group), 0]]
    entries = [begin, end]
    for piece, start in zip(tok_set, starts):
        tiles = piece.shape[0] // TILE
        entries += [
            start,
            jnp.clip((begin - start) // TILE, 0, tiles),
            jnp.clip((end - start + TILE - 1) // TILE, 0, tiles),
        ]
    info = jnp.stack(entries).astype(jnp.int32)

    keys, values = zip(*[keys_values(piece, gt, w_key, w_value) for piece in tok_set])
    query, mixed, mlp, state, inner, slope, out_set, inv, *weights = forward(
        info, lat_set, gl, gm, w_query, w_out, w_up, w_down, keys, values, scale
    )
    output = from_scenes(out_set)
    d_state, d_att, delta, mlp_pack, d_wo, dg_mlp = mlp_back(
        cot_set, slope, state, mixed, mlp, inner, inv, gm, w_out, w_up, w_down
    )
    *d_toks, dq, d_wk, d_wv, dg_tok = attention_back(
        info, query, d_att, delta, w_key, w_value, gt, keys, values, tok_set, weights, scale
    )
    d_lat_set, d_wq, dg_lat = latent_back(dq, lat_set, d_state, gl, w_query, scale)
    d_latents = from_scenes(d_lat_set).astype(F32)

    d_tail = lax.ppermute(d_toks[0], "blk", [(j, i) for i, j in forward_pairs])
    own_parts = [d_toks[-1]]
    returned = {k: d_toks[k] for k in range(1, group)}
    tail_own = []
    taken = 0
    while taken < tail_rows:
        owner = group - 1 - taken // span
        size = min(span, tail_rows - taken)
        chunk = d_tail[tail_rows - taken - size : tail_rows - taken]
        chunk = jnp.pad(chunk, ((span - size, 0), (0, 0)))
        tail_own.append((owner, chunk))
        taken += size
    for owner, chunk in tail_own:
        for k in range(1, group):
            returned[k] = returned[k] + jnp.where(member == owner ^ k, chunk, 0)
        own_parts.append(jnp.where(member == owner, chunk, 0))
    own_parts += [exchange(returned[k], blocks, k) for k in range(1, group)]
    d_tokens = token_back(tok, gt, own_parts)

    axes = ("seq", "blk")
    mlp_sum = lax.psum(mlp_pack, axes).astype(F32)
    small_sum = lax.psum(jnp.concatenate([d_wq, d_wk, d_wv, d_wo], axis=0), axes).astype(F32)
    gains = lax.psum(jnp.stack([jnp.sum(g, axis=0) for g in (dg_lat, dg_tok, dg_mlp)]), axes)
    hidden = w_up.shape[1]
    d_w_down = mlp_sum[:hidden]
    d_w_up = jnp.swapaxes(mlp_sum[hidden:].reshape(hidden // width, width, width), 0, 1).reshape(width, hidden)
    return (
        output[None],
        d_latents[None],
        d_tokens[None],
        small_sum[:width],
        small_sum[width : 2 * width],
        small_sum[2 * width : 3 * width],
        small_sum[3 * width :],
        d_w_up,
        d_w_down,
        gains[0],
        gains[1],
        gains[2],
    )


def solution(mesh):
    split = P("seq", "blk", None)
    in_specs = (split, split, P("seq", None)) + (P(),) * 9 + (split,)
    out_specs = (split,) * 3 + (P(),) * 9
    return jax.shard_map(
        functools.partial(local, mesh.shape["blk"]), mesh=mesh, in_specs=in_specs, out_specs=out_specs, check_vma=False
    )
```

```python
import functools
import math

import jax
import jax.numpy as jnp
from jax import lax
from jax.experimental import pallas as pl
from jax.experimental.pallas import tpu as pltpu
from jax.sharding import PartitionSpec as P

EPSILON = 1e-05
NEGATIVE = -1e30
LOG2E = 1.4426950408889634
GELU_C = math.sqrt(2.0 / math.pi)
GELU_A = 0.044715
F32 = jnp.float32
BF16 = jnp.bfloat16
NN = (((1,), (0,)), ((), ()))
NT = (((1,), (1,)), ((), ()))
TN = (((0,), (0,)), ((), ()))


def dot(left, right, dims=NN):
    return lax.dot_general(left, right, dims, preferred_element_type=F32)


def norm_parts(rows):
    center = rows - jnp.mean(rows, axis=-1, keepdims=True)
    spread = jnp.mean(center * center, axis=-1, keepdims=True)
    inverse = lax.rsqrt(spread + EPSILON)
    return center * inverse, inverse


def norm_back(d_normed, unit, inverse, gain):
    d_unit = d_normed * gain
    mean_d = jnp.mean(d_unit, axis=-1, keepdims=True)
    mean_p = jnp.mean(d_unit * unit, axis=-1, keepdims=True)
    return inverse * (d_unit - mean_d - unit * mean_p)


def vmem_call(kernel, name, outs, args, limit, scratch=(), smem=0):
    held = sum(math.prod(shape) * jnp.dtype(dtype).itemsize for shape, dtype in scratch)
    in_vmem = pl.BlockSpec(memory_space=pltpu.VMEM)
    in_smem = pl.BlockSpec(memory_space=pltpu.SMEM)
    return pl.pallas_call(
        kernel,
        in_specs=[in_smem] * smem + [in_vmem] * (len(args) - smem),
        out_specs=[in_vmem] * len(outs),
        out_shape=[jax.ShapeDtypeStruct(shape, dtype) for shape, dtype in outs],
        scratch_shapes=[pltpu.VMEM(shape, dtype) for shape, dtype in scratch],
        compiler_params=pltpu.CompilerParams(vmem_limit_bytes=(limit << 20) + held),
        cost_estimate=pl.CostEstimate(flops=0, bytes_accessed=0, transcendentals=0),
        name=name,
    )(*args)


class Flow:
    AHEAD = 5 << 20

    def __init__(self, loads, stores, semaphores):
        self.loads = loads
        self.stores = stores
        self.semaphores = semaphores
        self.started = 0
        self.waiting = set(range(len(loads)))
        self.begun = []
        self.whole = set()
        self.start_more(-1)

    def start_more(self, least):
        def size(j):
            held = self.loads[j][1]
            return math.prod(held.shape) * jnp.dtype(held.dtype).itemsize

        flying = sum(size(j) for j in self.waiting if j < self.started)
        while self.started < len(self.loads) and (self.started <= least or flying + size(self.started) <= self.AHEAD):
            flying += size(self.started)
            self.loads[self.started][2].start()
            self.started += 1

    def need(self, *refs):
        wanted = [j for j, load in enumerate(self.loads) if j in self.waiting and any(load[1] is r for r in refs)]
        for j in wanted:
            self.start_more(j)
        for j in wanted:
            self.waiting.discard(j)
            self.loads[j][2].wait()
        self.start_more(-1)

    def emit(self, ref, *where):
        for j, (out, held) in enumerate(self.stores):
            if held is ref:
                self.whole.add(j)
                source, target = (held.at[where], out.at[where]) if where else (held, out)
                copy = pltpu.make_async_copy(source, target, self.semaphores.at[len(self.begun)])
                copy.start()
                self.begun.append(copy)

    def close(self):
        self.need(*[held for _, held, _ in self.loads])
        for j, (_, held) in enumerate(self.stores):
            if j not in self.whole:
                self.emit(held)
        for copy in self.begun:
            copy.wait()


def hbm_call(kernel, name, outs, args, limit, scratch=(), smem=0, fixed_in=(), fixed_out=(), stores=None, lean=False):
    arrays = args[smem:]
    moves_in = [j for j in range(len(arrays)) if j not in fixed_in]
    moves_out = [j for j in range(len(outs)) if j not in fixed_out]
    held = [(arrays[j].shape, arrays[j].dtype) for j in moves_in] + [outs[j] for j in moves_out] + list(scratch)
    size = sum(math.prod(shape) * jnp.dtype(dtype).itemsize for shape, dtype in held)

    resident = [(arrays[j].shape, arrays[j].dtype) for j in fixed_in] + [outs[j] for j in fixed_out]
    rest = sum(math.prod(shape) * jnp.dtype(dtype).itemsize for shape, dtype in resident)
    limit = max((limit << 20) + size, 0 if lean else (62 << 20) - rest)

    def body(*refs):
        scalars, refs = refs[:smem], refs[smem:]
        ins, refs = list(refs[: len(arrays)]), refs[len(arrays) :]
        results, refs = list(refs[: len(outs)]), refs[len(outs) :]
        *kept, load_sems, store_sems = refs
        loads, kept_out = [], []
        for n, j in enumerate(moves_in):
            loads.append((ins[j], kept[n], pltpu.make_async_copy(ins[j], kept[n], load_sems.at[n])))
            ins[j] = kept[n]
        kept = kept[len(moves_in) :]
        for n, j in enumerate(moves_out):
            kept_out.append((results[j], kept[n]))
            results[j] = kept[n]
        flow = Flow(loads, kept_out, store_sems)
        kernel(flow, *scalars, *ins, *results, *kept[len(moves_out) :])
        flow.close()

    def place(count, fixed):
        return [pl.BlockSpec(memory_space=pltpu.VMEM if j in fixed else pl.ANY) for j in range(count)]

    return pl.pallas_call(
        body,
        in_specs=[pl.BlockSpec(memory_space=pltpu.SMEM)] * smem + place(len(arrays), fixed_in),
        out_specs=place(len(outs), fixed_out),
        out_shape=[jax.ShapeDtypeStruct(shape, dtype) for shape, dtype in outs],
        scratch_shapes=[pltpu.VMEM(shape, dtype) for shape, dtype in held]
        + [pltpu.SemaphoreType.DMA((max(len(moves_in), 1),)), pltpu.SemaphoreType.DMA((max(stores or len(moves_out), 1),))],
        compiler_params=pltpu.CompilerParams(vmem_limit_bytes=min(limit, 63 << 20)),
        cost_estimate=pl.CostEstimate(flops=0, bytes_accessed=0, transcendentals=0),
        name=name,
    )(*args)


def cuts(size, step):
    return [(i, min(step, size - i)) for i in range(0, size, step)]


def fold(rows):
    return jnp.sum(rows.reshape(rows.shape[0] // 8, 8, rows.shape[1]), axis=0)


def column_of(row):
    return jnp.transpose(jnp.broadcast_to(row, (8, row.shape[1])))[:, :1]


def row_of(column):
    return jnp.transpose(jnp.broadcast_to(column, (column.shape[0], 128)))[:8, :]


def join(refs, whole_ref):
    part = refs[0].shape[0]
    for j, ref in enumerate(refs):
        whole_ref[pl.ds(j * part, part), :] = ref[...]


def part_store(refs, start, value):
    part = refs[0].shape[0]
    size = min(part, value.shape[0])
    for first in range(0, value.shape[0], size):
        at = start + first
        refs[at // part][pl.ds(at % part, size), :] = value[first : first + size]


def kv_kernel(flow, tok_ref, gain_ref, wk_ref, wv_ref, k_ref, v_ref):
    flow.need(tok_ref, gain_ref, wk_ref, wv_ref)
    for start, size in cuts(tok_ref.shape[0], 256):
        rows = pl.ds(start, size)
        unit, _ = norm_parts(tok_ref[rows, :].astype(F32))
        low = (unit * gain_ref[...]).astype(BF16)
        k_ref[rows, :] = dot(low, wk_ref[...]).astype(BF16)
        v_ref[rows, :] = dot(low, wv_ref[...]).astype(BF16)
    flow.emit(k_ref)
    flow.emit(v_ref)


def keys_values(tok, gain, w_key, w_value):
    return hbm_call(kv_kernel, "keys_values", [(tok.shape, BF16)] * 2, (tok, gain, w_key, w_value), 8)


def score_piece(info_ref, p, k_ref, s_ref, query, columns, top, scale):
    begin, end = info_ref[0], info_ref[1]
    for start, size in cuts(k_ref.shape[0], 512):
        s = dot(k_ref[pl.ds(start, size), :], query, NT) * (scale * LOG2E)
        place = info_ref[2 + p] + start + lax.broadcasted_iota(jnp.int32, (size, 1), 0)
        s = s + jnp.where((place >= begin) & (place < end), 0.0, NEGATIVE)
        s_ref[pl.ds(start, size), columns] = s
        top = jnp.maximum(top, jnp.max(s.reshape(size // 8, 8, s.shape[1]), axis=0))
    return top


def weigh_piece(v_ref, s_ref, w_ref, columns, top, total, acc):
    for start, size in cuts(v_ref.shape[0], 512):
        w = jnp.exp2(s_ref[pl.ds(start, size), columns] - top)
        total = total + fold(w)
        w_ref[pl.ds(start, size), columns] = w.astype(BF16)
    part = dot(w_ref[:, columns], v_ref[...], TN)
    return total, part if acc is None else acc + part


def attend_kernel(parts, fresh, count, scale, flow, info_ref, gl_ref, wq_ref, *refs):
    new, refs = refs[: 3 * bool(fresh) + fresh], refs[3 * bool(fresh) + fresh :]
    lat_refs, refs = refs[:parts], refs[parts:]
    given = count - fresh
    k_refs, v_refs, refs = refs[:given], refs[given : 2 * given], refs[2 * given :]
    q_ref, acc_ref, top_ref, tot_ref, lat_ref = refs[:5]
    refs = refs[5:]
    k_refs, v_refs, refs = refs[:fresh] + k_refs, refs[fresh : 2 * fresh] + v_refs, refs[2 * fresh :]
    w_refs, s_refs = refs[:count], refs[count:]
    flow.need(*lat_refs, gl_ref, wq_ref)
    join(lat_refs, lat_ref)
    for j in range(fresh):
        kv_kernel(flow, new[3 + j], *new[:3], k_refs[j], v_refs[j])
    for start, size in cuts(lat_ref.shape[0], 512):
        rows = columns = pl.ds(start, size)
        unit, _ = norm_parts(lat_ref[rows, :].astype(F32))
        query = dot((unit * gl_ref[...]).astype(BF16), wq_ref[...]).astype(BF16)
        q_ref[rows, :] = query
        flow.need(*k_refs)
        top = jnp.full((8, size), NEGATIVE, F32)
        for p in range(count):
            top = score_piece(info_ref, p, k_refs[p], s_refs[p], query, columns, top, scale)
        top = jnp.max(top, axis=0, keepdims=True)
        total, acc = jnp.zeros((8, size), F32), None
        flow.need(*v_refs)
        for p in range(count):
            total, acc = weigh_piece(v_refs[p], s_refs[p], w_refs[p], columns, top, total, acc)
        acc_ref[rows, :] = acc
        if start == 0:
            flow.emit(lat_ref)
        for p in range(count):
            flow.emit(w_refs[p], slice(None), columns)
        flow.emit(acc_ref, rows)
        top_ref[:, columns] = jnp.broadcast_to(top, (8, size))
        tot_ref[:, columns] = total


def attend(info, lats, gl, wq, fresh, gt, wk, wv, keys, values, scale):
    rows, width = len(lats) * lats[0].shape[0], lats[0].shape[1]
    made = [(t.shape, BF16) for t in fresh]
    pieces = [t.shape[0] for t in (*fresh, *keys)]
    outs = [((rows, width), BF16), ((rows, width), F32), ((8, rows), F32), ((8, rows), F32), ((rows, width), BF16)]
    outs += made * 2 + [((n, rows), BF16) for n in pieces]
    new = (gt, wk, wv, *fresh) if fresh else ()
    q, acc, top, total, lat, *rest = hbm_call(
        functools.partial(attend_kernel, len(lats), len(fresh), len(pieces), scale),
        "attend",
        outs,
        (info, gl, wq, *new, *lats, *keys, *values),
        12,
        [((n, rows), F32) for n in pieces],
        smem=1,
        stores=len(outs) + (len(cuts(rows, 512)) - 1) * (len(pieces) + 1),
    )
    more = len(fresh)
    return q, acc, top, total, lat, rest[2 * more :], (*rest[:more], *keys), (*rest[more : 2 * more], *values)


def finish_kernel(
    scale, flow, info_ref, tok_ref, gt_ref, wk_ref, wv_ref, top_ref, q_ref, tot_ref, acc_ref, lat_ref, gm_ref, wo_ref, wu_ref, wd_ref,
    k_ref, v_ref, w_ref, factor_ref, mixed_ref, mlp_ref, state_ref, inner_ref, slope_ref, *refs,
):
    *out_refs, s_ref = refs
    kv_kernel(flow, tok_ref, gt_ref, wk_ref, wv_ref, k_ref, v_ref)
    flow.need(top_ref, q_ref, tot_ref, acc_ref)
    hidden = wu_ref.shape[1]
    for start, size in cuts(lat_ref.shape[0], 512):
        rows = columns = pl.ds(start, size)
        old = top_ref[:1, columns]
        top = jnp.broadcast_to(old, (8, size))
        top = score_piece(info_ref, 0, k_ref, s_ref, q_ref[rows, :], columns, top, scale)
        top = jnp.max(top, axis=0, keepdims=True)
        total, acc = weigh_piece(v_ref, s_ref, w_ref, columns, top, jnp.zeros((8, size), F32), None)
        shrink = jnp.exp2(old - top)
        total = jnp.sum(total, axis=0, keepdims=True) + jnp.sum(tot_ref[:, columns], axis=0, keepdims=True) * shrink
        inverse = 1.0 / total
        late, early = column_of(inverse), column_of(shrink * inverse)
        lane = lax.broadcasted_iota(jnp.int32, (size, 128), 1)
        factor_ref[rows, :] = jnp.where(lane == 0, late, early)
        mixed_ref[rows, :] = (acc * late + acc_ref[rows, :] * early).astype(BF16)
    flow.emit(w_ref)
    flow.need(lat_ref, wo_ref, gm_ref, wu_ref, wd_ref)
    for start, size in cuts(lat_ref.shape[0], 256):
        rows = pl.ds(start, size)
        state = lat_ref[rows, :].astype(F32) + dot(mixed_ref[rows, :], wo_ref[...])
        state_ref[rows, :] = state
        unit, _ = norm_parts(state)
        low = (unit * gm_ref[...]).astype(BF16)
        mlp_ref[rows, :] = low
        out = state
        for first, step in cuts(hidden, 512):
            some = pl.ds(first, step)
            u = dot(low, wu_ref[:, some])
            square = u * u
            t = jnp.tanh(u * (GELU_C + (GELU_C * GELU_A) * square))
            half = 0.5 + 0.5 * t
            inner = (u * half).astype(BF16)
            bend = u * ((0.5 * GELU_C) + (1.5 * GELU_C * GELU_A) * square)
            inner_ref[rows, some] = inner
            slope_ref[rows, some] = (half + bend * (1.0 - t * t)).astype(BF16)
            out = out + dot(inner, wd_ref[some, :])
        part_store(out_refs, start, out.astype(BF16))


def finish(info, parts, lat, q, acc, top, total, tail, gt, wk, wv, gm, wo, wu, wd, scale):
    rows, width = lat.shape
    hidden = wu.shape[1]
    tall = (rows, width)
    outs = [(tail.shape, BF16)] * 2 + [((tail.shape[0], rows), BF16), ((rows, 128), F32), (tall, BF16), (tall, BF16), (tall, F32)]
    outs += [((rows, hidden), BF16)] * 2 + [((rows // parts, width), BF16)] * parts
    out = hbm_call(
        functools.partial(finish_kernel, scale),
        "finish",
        outs,
        (info, tail, gt, wk, wv, top, q, total, acc, lat, gm, wo, wu, wd),
        22,
        [((tail.shape[0], rows), F32)],
        smem=1,
        fixed_out=(3, 4, 5, 6, 7, 8),
    )
    return out[:9], out[9:]


def mlp_back_kernel(
    parts, flow, info_ref, *refs,
):
    cot_refs, refs = refs[:parts], refs[parts:]
    wd_ref, slope_ref, wu_ref, state_ref, mixed_ref, factor_ref, gm_ref, wo_ref, inner_ref, mlp_ref, *refs = refs
    dstate_ref, late_ref, early_ref, dlate_ref, dearly_ref, keep_ref, send_ref, dwo_ref, dgain_ref = refs[:9]
    dpre_ref, dproj_ref, cot_ref = refs[9:]
    flow.need(*cot_refs, wd_ref)
    join(cot_refs, cot_ref)
    hidden, width = wd_ref.shape

    def pack(half, first, value):
        rows = pl.ds(first, value.shape[0])

        @pl.when(info_ref[0] == half)
        def _():
            keep_ref[rows, :] = value.astype(BF16)

        @pl.when(info_ref[0] != half)
        def _():
            send_ref[rows, :] = value.astype(BF16)

    total = jnp.zeros((8, width), F32)
    for start, size in cuts(cot_ref.shape[0], 256):
        rows = pl.ds(start, size)
        cot = cot_ref[rows, :]
        d_mlp = None
        for first, step in cuts(hidden, 512):
            some = pl.ds(first, step)
            d_inner = dot(cot, wd_ref[some, :], NT)
            d_pre = (slope_ref[rows, some].astype(F32) * d_inner).astype(BF16)
            dpre_ref[rows, some] = d_pre
            flow.need(wu_ref)
            part = dot(d_pre, wu_ref[:, some], NT)
            d_mlp = part if d_mlp is None else d_mlp + part
        flow.need(gm_ref, wo_ref)
        unit, inverse = norm_parts(state_ref[rows, :])
        total = total + fold(d_mlp * unit)
        d_state = cot.astype(F32) + norm_back(d_mlp, unit, inverse, gm_ref[...])
        dstate_ref[rows, :] = d_state
        d_proj = d_state.astype(BF16)
        dproj_ref[rows, :] = d_proj
        d_att = dot(d_proj, wo_ref[...], NT)
        mixed = mixed_ref[rows, :].astype(F32)
        for lane, part_ref, delta_ref in ((0, late_ref, dlate_ref), (1, early_ref, dearly_ref)):
            part = (d_att * factor_ref[rows, lane : lane + 1]).astype(BF16)
            part_ref[rows, :] = part
            delta = jnp.sum(part.astype(F32) * mixed, axis=-1, keepdims=True)
            delta_ref[:, rows] = row_of(delta)
    dgain_ref[...] = total
    for ref in (dstate_ref, late_ref, early_ref, dlate_ref, dearly_ref):
        flow.emit(ref)
    for first, step in cuts(hidden, 512):
        pack(0, first, dot(inner_ref[:, first : first + step], cot_ref[...], TN))
    for first, step in cuts(hidden, 512):
        pack(1, first, dot(mlp_ref[...], dpre_ref[:, first : first + step], TN))
    dwo_ref[...] = dot(mixed_ref[...], dproj_ref[...], TN).astype(BF16)


def mlp_back(info, cots, slope, state, mixed, mlp, inner, factor, gm, wo, wu, wd):
    rows, width = state.shape
    hidden = wu.shape[1]
    tall, flat = (rows, width), (8, rows)
    outs = [(tall, F32), (tall, BF16), (tall, BF16), (flat, F32), (flat, F32)]
    outs += [((hidden, width), BF16)] * 2 + [((width, width), BF16), ((8, width), F32)]
    return hbm_call(
        functools.partial(mlp_back_kernel, len(cots)),
        "mlp_back",
        outs,
        (info, *cots, wd, slope, wu, state, mixed, factor, gm, wo, inner, mlp),
        20,
        [((rows, hidden), BF16), (tall, BF16), (tall, BF16)],
        smem=1,
        fixed_in=[len(cots) + j for j in (1, 3, 4, 5, 8, 9)],
        fixed_out=range(len(outs)),
    )


def attention_back_kernel(early, start, parts, extra, scale, flow, info_ref, *refs):
    count = len(early)
    q_ref, wk_ref, wv_ref, gain_ref, *refs = refs
    grads, refs = refs[:4], refs[4:]
    v_refs, w_refs, t_refs, k_refs = (refs[j : 4 * count : 4] for j in range(4))
    refs = refs[4 * count :]
    sums, refs = refs[:start], refs[start:]
    if parts:
        lat_ref, gl_ref, wq_ref, dstate_ref, dwo_ref, dgmlp_ref, *refs = refs
    dtok_refs, refs = refs[:count], refs[count:]
    if parts:
        dlat_refs, refs = refs[:parts], refs[parts:]
        keep_ref, send_ref, dq_ref, akey_ref, aval_ref, dgain_ref, latlow_ref, dquery_ref, *refs = refs
    else:
        dq_ref, akey_ref, aval_ref, dgain_ref, *refs = refs
    dscore_ref, low_ref, dkey_ref, dval_ref, part_ref = refs
    totals = (dq_ref, akey_ref, aval_ref, dgain_ref)
    flow.need(q_ref, wk_ref, wv_ref, gain_ref)
    for p in range(count):
        size = k_refs[p].shape[0]
        datt_ref, delta_ref = grads[2 * early[p] : 2 * early[p] + 2]
        flow.need(datt_ref, delta_ref, v_refs[p], w_refs[p], t_refs[p], k_refs[p])
        begin, end, first_place = info_ref[1 + 3 * p], info_ref[2 + 3 * p], info_ref[3 + 3 * p]
        part_ref[...] = jnp.zeros_like(part_ref)
        for first, step in cuts(size, 256):
            rows = pl.ds(first, step)
            active = (first_place + first < end) & (first_place + first + step > begin)

            @pl.when(active)
            def _(p=p, rows=rows, datt_ref=datt_ref, delta_ref=delta_ref):
                d_prob = dot(v_refs[p][rows, :], datt_ref[...], NT)
                d_score = (w_refs[p][rows, :].astype(F32) * (d_prob - delta_ref[:1, :])).astype(BF16)
                dscore_ref[rows, :] = d_score
                d_key = (dot(d_score, q_ref[...]) * scale).astype(BF16)
                d_value = dot(w_refs[p][rows, :], datt_ref[...]).astype(BF16)
                dkey_ref[rows, :] = d_key
                dval_ref[rows, :] = d_value
                unit, _ = norm_parts(t_refs[p][rows, :].astype(F32))
                low_ref[rows, :] = (unit * gain_ref[...]).astype(BF16)
                d_tok = dot(d_key, wk_ref[...], NT) + dot(d_value, wv_ref[...], NT)
                dtok_refs[p][rows, :] = d_tok.astype(BF16)
                part_ref[...] += fold(d_tok * unit)

            @pl.when(jnp.logical_not(active))
            def _(p=p, rows=rows):
                for ref in (dscore_ref, dkey_ref, dval_ref, low_ref, dtok_refs[p]):
                    ref[rows, :] = jnp.zeros((rows.size, ref.shape[1]), BF16)

        flow.emit(dtok_refs[p])
        dgain = part_ref[...]
        here = pl.ds(0, size)
        news = (
            dot(dscore_ref[here, :], k_refs[p][...], TN),
            dot(low_ref[here, :], dkey_ref[here, :], TN),
            dot(low_ref[here, :], dval_ref[here, :], TN),
            dgain,
        )
        if p == 0:
            flow.need(*sums)
        for j, (ref, value) in enumerate(zip(totals, news)):
            if p == 0:
                ref[...] = value + sums[j][...] if sums else value
            else:
                ref[...] += value
    if not parts:
        return
    flow.need(lat_ref, gl_ref, wq_ref, dstate_ref, dwo_ref, dgmlp_ref)
    total = None
    width = wq_ref.shape[0]
    for first, size in cuts(lat_ref.shape[0], 256):
        rows = pl.ds(first, size)
        unit, inverse = norm_parts(lat_ref[rows, :].astype(F32))
        gain = gl_ref[...]
        latlow_ref[rows, :] = (unit * gain).astype(BF16)
        d_query = (dq_ref[rows, :] * scale).astype(BF16)
        dquery_ref[rows, :] = d_query
        d_low = dot(d_query, wq_ref[...], NT)
        part_store(dlat_refs, first, (dstate_ref[rows, :] + norm_back(d_low, unit, inverse, gain)).astype(BF16))
        part = fold(d_low * unit)
        total = part if total is None else total + part
    for ref in dlat_refs:
        flow.emit(ref)
    d_wq = dot(latlow_ref[...], dquery_ref[...], TN)
    gains = [jnp.sum(g, axis=0, keepdims=True) for g in (total, dgain_ref[...], dgmlp_ref[...])]
    line = lax.broadcasted_iota(jnp.int32, (extra, width), 0)
    block = jnp.where(line == 0, gains[0], jnp.where(line == 1, gains[1], jnp.where(line == 2, gains[2], 0.0)))
    halves = ((d_wq, akey_ref), (aval_ref, dwo_ref))
    for ref, core in ((keep_ref, info_ref[0]), (send_ref, 1 - info_ref[0])):
        ref[pl.ds(2 * width, extra), :] = block.astype(BF16)
        for h, half in enumerate(halves):

            @pl.when(core == h)
            def _(ref=ref, half=half):
                for j, piece in enumerate(half):
                    ref[pl.ds(j * width, width), :] = piece[...].astype(BF16)


def attention_back(info, q, wk, wv, gain, grads, early, values, weights, tokens, keys, sums, latents, parts, extra, scale):
    rows, width = q.shape
    square = ((width, width), F32)
    totals = [((rows, width), F32), square, square, ((8, width), F32)]
    most = max(k.shape[0] for k in keys)
    work = [((most, rows), BF16)] + [((most, width), BF16)] * 3 + [((8, width), F32)]
    outs = [(k.shape, BF16) for k in keys]
    by_piece = [a for piece in zip(values, weights, tokens, keys) for a in piece]
    args = (info, q, wk, wv, gain, *grads, *by_piece, *sums)
    if latents:
        args = (*args, *latents)
        outs += [((rows // parts, width), BF16)] * parts + [((2 * width + extra, width), BF16)] * 2
        work = totals + [((rows, width), BF16)] * 2 + work
    else:
        outs += totals
        parts = 0
    kernel = functools.partial(attention_back_kernel, early, len(sums), parts, extra, scale)
    out = hbm_call(kernel, "attention_back", outs, args, 12, work, smem=1)
    return out[: len(keys)], out[len(keys) :]


def token_back_kernel(count, flow, tok_ref, gain_ref, *refs):
    flow.need(tok_ref, gain_ref, *refs[:count])
    for start, size in cuts(tok_ref.shape[0], 256):
        rows = pl.ds(start, size)
        unit, inverse = norm_parts(tok_ref[rows, :].astype(F32))
        total = refs[0][rows, :].astype(F32)
        for ref in refs[1:count]:
            total = total + ref[rows, :].astype(F32)
        refs[count][rows, :] = norm_back(total, unit, inverse, gain_ref[...])
        flow.emit(refs[count], rows)


def token_back(tok, gain, parts):
    args = (tok, gain, *parts)
    [out] = hbm_call(functools.partial(token_back_kernel, len(parts)), "token_back", [(tok.shape, F32)], args, 8, stores=len(cuts(tok.shape[0], 256)))
    return out


def picks(shape, scenes, scene, transposed=False):
    along = lax.broadcasted_iota(jnp.int32, shape, 1 if transposed else 0)
    across = lax.broadcasted_iota(jnp.int32, shape, 0 if transposed else 1)
    return jnp.where(across == along * scenes + scene, 1.0, 0.0).astype(BF16)


def sort_kernel(flow, info_ref, rows_ref, *out_refs):
    flow.need(rows_ref)
    for k, ref in enumerate(out_refs):
        take = picks((ref.shape[0], rows_ref.shape[0]), len(out_refs), info_ref[0] ^ k)
        ref[...] = dot(take, rows_ref[...]).astype(BF16)
        flow.emit(ref)


def sort_rows(info, value, scenes):
    rows, width = value.shape
    return hbm_call(sort_kernel, "sort_rows", [((rows // scenes, width), BF16)] * scenes, (info, value), 16, smem=1)


def unsort_kernel(flow, info_ref, *refs):
    *in_refs, out_ref = refs
    flow.need(*in_refs)
    rows, part = out_ref.shape[0], in_refs[0].shape[0]
    scenes = len(in_refs)
    step = rows // scenes
    for start in range(0, rows, step):
        total = None
        for k, ref in enumerate(in_refs):
            some = part // scenes
            first = start // scenes
            put = picks((step, some), scenes, info_ref[0] ^ k, transposed=True)
            value = dot(put, ref[pl.ds(first, some), :])
            total = value if total is None else total + value
        out_ref[pl.ds(start, step), :] = total.astype(out_ref.dtype)
        flow.emit(out_ref, pl.ds(start, step))


def unsort_rows(info, parts, dtype):
    rows, width = len(parts) * parts[0].shape[0], parts[0].shape[1]
    [out] = hbm_call(unsort_kernel, "unsort_rows", [((rows, width), dtype)], (info, *parts), 16, smem=1, stores=len(parts))
    return out


def split_kernel(count, place, extra, info_ref, *refs):
    in_refs, out_refs = refs[:count], refs[count:]
    rest = None
    if extra and out_refs[-1].shape[0] == extra and len(out_refs) == 2:
        *out_refs, rest = out_refs
    body = in_refs[0].shape[0] - extra
    step = body // len(out_refs)

    def total(start, rows):
        value = in_refs[0][pl.ds(start, rows), :].astype(F32)
        for ref in in_refs[1:]:
            value = value + ref[pl.ds(start, rows), :].astype(F32)
        return value.astype(BF16)

    shared = total(body, extra) if extra else None
    for k, ref in enumerate(out_refs):
        start = (info_ref[place] ^ k) * step if len(out_refs) > 1 else 0
        ref[pl.ds(0, step), :] = total(start if isinstance(start, int) else pl.multiple_of(start, 16), step)
        if extra and rest is None:
            ref[pl.ds(step, extra), :] = shared
    if rest is not None:
        rest[...] = shared


def split_sum(info, arrays, parts, place, extra):
    rows, width = arrays[0].shape
    step = (rows - extra) // parts
    if parts > 1:
        outs = [((step + extra, width), BF16)] * parts
    else:
        outs = [((step, width), BF16)] + ([((extra, width), BF16)] if extra else [])
    kernel = functools.partial(split_kernel, len(arrays), place, extra)
    return vmem_call(kernel, "split_sum", outs, (info, *arrays), 8, smem=1)


def unpack_kernel(width, info_ref, mine_ref, other_ref, *out_refs):
    core, quad, line = info_ref[0], info_ref[1], info_ref[2]
    half = mine_ref.shape[0]
    lines = info_ref.shape[0] - 3
    block = half // (4 * lines)
    for h in range(2):
        for m in range(4):
            for z in range(lines):
                rows = pl.ds(pl.multiple_of(((quad ^ m) * lines + (line ^ z)) * block, 16), block)
                value = jnp.where(core == h, mine_ref[rows, :].astype(F32), other_ref[rows, :].astype(F32))
                at = h * half + (m * lines + z) * block
                total = 0
                for ref in out_refs:
                    tall = ref.shape[0] * (ref.shape[1] // width)
                    if total <= at < total + tall:
                        inside = at - total
                        slab, row = inside // ref.shape[0], inside % ref.shape[0]
                        ref[pl.ds(row, block), pl.ds(slab * width, width)] = value
                    total += tall


class Sums:
    def __init__(self, seqs, blocks):
        self.seqs, self.blocks = seqs, blocks
        self.lines = blocks // 2
        seq, blk = lax.axis_index("seq"), lax.axis_index("blk")
        places = [seq % 2, (seq // 2) * 2 + blk % 2, blk // 2] + [seq * 0] * self.lines
        self.info = jnp.stack(places).astype(jnp.int32)

    def flip(self, value, seq_mask, blk_mask):
        pairs = [
            (s * self.blocks + b, (s ^ seq_mask) * self.blocks + (b ^ blk_mask))
            for s in range(self.seqs)
            for b in range(self.blocks)
        ]
        return lax.ppermute(value, ("seq", "blk"), pairs)

    def to_core(self, value):
        return self.flip(value, 1, 0)

    def to_quad(self, values):
        return [self.flip(v, 2 * (k // 2), k % 2) for k, v in enumerate(values, 1)]

    def to_line(self, values):
        return [self.flip(v, 0, 2 * k) for k, v in enumerate(values, 1)]

    def add_core(self, keep, received, extra=0):
        return split_sum(self.info, [keep, received], 4, 1, extra)

    def add_quad(self, keep, received, extra=0):
        return split_sum(self.info, [keep, *received], self.lines, 2, extra)

    def add_line(self, keep, received, extra=0):
        return split_sum(self.info, [keep, *received], 1, 0, extra)

    def unpack(self, mine, other, shapes):
        outs = [(shape, F32) for shape in shapes]
        kernel = functools.partial(unpack_kernel, mine.shape[1])
        return vmem_call(kernel, "unpack", outs, (self.info, mine, other), 16, smem=1)


def after(value, *others):
    return lax.optimization_barrier((value, others))[0]


def local(
    sizes, latents, tokens, lengths, gain_lat, gain_tok, gain_mlp, w_query, w_key, w_value, w_out, w_up, w_down, d_out
):
    lat, tok, cot = latents[0], tokens[0], d_out[0]
    scene_lengths = lengths[0]
    scenes = scene_lengths.shape[0]
    seqs, blocks = sizes["seq"], sizes["blk"]
    group = blocks // scenes
    span, width = tok.shape
    hidden = w_up.shape[1]
    scale = width ** (-0.5)
    position = lax.axis_index("blk")
    scene, member = position // group, position % group
    scene_info = scene.astype(jnp.int32).reshape(1)
    gl, gt, gm = (g.reshape(1, width) for g in (gain_lat, gain_tok, gain_mlp))
    sums = Sums(seqs, blocks)

    def exchange(value, mask):
        return sums.flip(value, 0, mask)

    def across(values):
        return [exchange(v, group * k) if k else v for k, v in enumerate(values)]

    order = jnp.arange(scenes, dtype=jnp.int32)
    begin = jnp.sum(jnp.where(order < scene, scene_lengths, 0))
    end = begin + jnp.sum(jnp.where(order == scene, scene_lengths, 0))
    base = scene * group * span
    tail_rows = (scenes - 1) * group * span // 8
    starts = [base + (member ^ k) * span for k in [*range(1, group), 0]]
    main_info = jnp.stack([begin, end, *starts]).astype(jnp.int32)
    tail_info = jnp.stack([begin, end, base - tail_rows]).astype(jnp.int32)

    lat_parts = sort_rows(scene_info, lat, scenes)
    others = [exchange(tok, k) for k in range(1, group)]
    lat_in = across(lat_parts)
    cot_parts = sort_rows(scene_info, after(cot, lat_parts), scenes)
    own_kv = keys_values(after(tok, cot_parts), gt, w_key, w_value)
    lat_in, others, cot_parts, own_kv, main_info, tail_info = lax.optimization_barrier(
        (lat_in, others, cot_parts, own_kv, main_info, tail_info)
    )
    cot_near = exchange(cot_parts[1], group)

    pieces = [tok, *others]
    lowest = (group * span - tail_rows) // span
    needed = []
    for owner in range(lowest, group):
        block = pieces[owner]
        for m in range(1, group):
            block = jnp.where(member == m, pieces[owner ^ m], block)
        needed.append(block)
    needed = jnp.concatenate(needed, axis=0) if len(needed) > 1 else needed[0]
    pairs = [(i, i + group) for i in range(blocks - group)]
    sent = needed[needed.shape[0] - tail_rows :]
    tail = lax.ppermute(sent, "blk", pairs)
    fresh = list(others) if group == 2 else []
    given = [own_kv] if fresh else [keys_values(piece, gt, w_key, w_value) for piece in others] + [own_kv]
    made_keys, made_values = zip(*given)
    query, acc, top, total, lat_set, weights, keys, values = attend(
        main_info, lat_in, gl, w_query, after(fresh, sent), gt, w_key, w_value, made_keys, made_values, scale
    )
    tail, query, cot_parts, cot_near = lax.optimization_barrier((tail, query, cot_parts, cot_near))

    cot_in = [cot_parts[0], cot_near, *[exchange(cot_parts[k], group * k) for k in range(2, scenes)]]
    saved, out_parts = finish(
        tail_info, scenes, lat_set, query, acc, top, total, tail, gt, w_key, w_value, gm, w_out, w_up, w_down, scale
    )
    tail_key, tail_value, tail_weight, factor, mixed, mlp, state, inner, slope = saved
    cot_in, out_parts, slope = lax.optimization_barrier((cot_in, out_parts, slope))
    out_back = across(out_parts)
    d_state, d_late, d_early, late, early_delta, keep, send, d_wo, dg_mlp = mlp_back(
        sums.info, cot_in, slope, state, mixed, mlp, inner, factor, gm, w_out, w_up, w_down
    )

    out_back, keep, send, d_early, d_late = lax.optimization_barrier((out_back, keep, send, d_early, d_late))
    received = sums.to_core(send)
    keep, *sends = sums.add_core(keep, received)
    received = sums.to_quad(sends)
    pieces = [(0, tail_value, tail_weight, tail, tail_key, tail_info)]
    for j, piece in enumerate((*others, tok)):
        pieces.append((1, values[j], weights[j], piece, keys[j], jnp.stack([begin, end, starts[j]]).astype(jnp.int32)))
    calls, size = [[]], 0
    for piece in pieces:
        if calls[-1] and size + piece[1].shape[0] > 3 * span:
            calls.append([])
            size = 0
        calls[-1].append(piece)
        size += piece[1].shape[0]
    extra = 16
    d_toks, kept = [], []
    for j, call in enumerate(calls):
        early, some_values, some_weights, some_tokens, some_keys, places = zip(*call)
        places = jnp.concatenate([sums.info[:1], *places])
        latents = (lat_set, gl, w_query, d_state, d_wo, dg_mlp) if j == len(calls) - 1 else ()
        grads = (d_late, late, after(d_early, keep), early_delta)
        some, kept = attention_back(
            places, query, w_key, w_value, gt, grads, early, some_values, some_weights, some_tokens, some_keys, kept,
            latents, scenes, extra, scale,
        )
        d_toks += some
    received, d_toks, kept = lax.optimization_barrier((received, d_toks, kept))
    d_tail, *returned, own = d_toks
    d_tail = lax.ppermute(d_tail, "blk", [(j, i) for i, j in pairs])
    *d_lat_parts, small_keep, small_send = kept

    small_got = sums.to_core(small_send)
    keep, *sends = sums.add_quad(keep, received)
    received = sums.to_line(sends)
    returned = dict(enumerate(returned, 1))
    own_tail = []
    for owner in range(lowest, group):
        start = owner * span - (group * span - tail_rows)
        chunk = after(d_tail, keep)[max(start, 0) : start + span]
        chunk = jnp.pad(chunk, ((span - chunk.shape[0], 0), (0, 0)))
        for k in range(1, group):
            returned[k] = returned[k] + jnp.where(member == owner ^ k, chunk, 0)
        own_tail.append(jnp.where(member == owner, chunk, 0))
    small_got, returned = lax.optimization_barrier((small_got, returned))
    returned = [exchange(returned[k], k) for k in range(1, group)]
    small_keep, *small_sends = sums.add_core(small_keep, small_got, extra)
    small_got = sums.to_quad(small_sends)
    output = unsort_rows(scene_info, after(out_back, small_sends), BF16)
    [shard] = sums.add_line(keep, after(received, output))
    received = sums.to_line([shard] * (sums.lines - 1))
    small_got, returned, received = lax.optimization_barrier((small_got, returned, received))
    block = jnp.concatenate([shard, *received], axis=0)
    received = sums.to_quad([block] * 3)
    small_keep, *small_sends = sums.add_quad(small_keep, after(small_got, block), extra)
    small_got = sums.to_line(small_sends)
    small_shard, gains = sums.add_line(small_keep, small_got, extra)
    small_got = sums.to_line([small_shard] * (sums.lines - 1))
    d_lat_back = across(after(d_lat_parts, small_shard))
    d_tokens = token_back(tok, gt, [own, *own_tail, *after(returned, small_shard)])
    small_block = jnp.concatenate([small_shard, *after(small_got, d_tokens)], axis=0)
    small_got = sums.to_quad([small_block] * 3)
    received, d_lat_back, small_block = lax.optimization_barrier((received, d_lat_back, small_block))
    mine = jnp.concatenate([block, *received], axis=0)
    other = sums.to_core(mine)
    d_latents = unsort_rows(scene_info, after(d_lat_back, mine), F32)
    small_mine = jnp.concatenate([small_block, *after(small_got, d_latents)], axis=0)
    small_other = sums.to_core(small_mine)
    d_w_down, d_w_up = sums.unpack(mine, after(other, small_mine), [(hidden, width), (width, hidden)])
    squares = sums.unpack(small_mine, after(small_other, d_w_up), [(width, width)] * 4)
    gains = gains.astype(F32)
    return (output[None], d_latents[None], d_tokens[None], *squares, d_w_up, d_w_down, gains[0], gains[1], gains[2])


def solution(mesh):
    split = P("seq", "blk", None)
    in_specs = (split, split, P("seq", None)) + (P(),) * 9 + (split,)
    out_specs = (split,) * 3 + (P(),) * 9
    return jax.shard_map(
        functools.partial(local, dict(mesh.shape)), mesh=mesh, in_specs=in_specs, out_specs=out_specs, check_vma=False
    )
```

```python
import functools
import math

import jax
import jax.numpy as jnp
from jax import lax
from jax.experimental import pallas as pl
from jax.experimental.pallas import tpu as pltpu
from jax.sharding import PartitionSpec as P

EPSILON = 1e-05
NEGATIVE = -1e30
LOG2E = 1.4426950408889634
GELU_C = math.sqrt(2.0 / math.pi)
GELU_A = 0.044715
F32 = jnp.float32
BF16 = jnp.bfloat16
NN = (((1,), (0,)), ((), ()))
NT = (((1,), (1,)), ((), ()))
TN = (((0,), (0,)), ((), ()))


def dot(left, right, dims=NN):
    return lax.dot_general(left, right, dims, preferred_element_type=F32)


def norm_parts(rows):
    center = rows - jnp.mean(rows, axis=-1, keepdims=True)
    spread = jnp.mean(center * center, axis=-1, keepdims=True)
    inverse = lax.rsqrt(spread + EPSILON)
    return center * inverse, inverse


def norm_back(d_normed, unit, inverse, gain):
    d_unit = d_normed * gain
    mean_d = jnp.mean(d_unit, axis=-1, keepdims=True)
    mean_p = jnp.mean(d_unit * unit, axis=-1, keepdims=True)
    return inverse * (d_unit - mean_d - unit * mean_p)


def vmem_call(kernel, name, outs, args, limit, scratch=(), smem=0):
    held = sum(math.prod(shape) * jnp.dtype(dtype).itemsize for shape, dtype in scratch)
    in_vmem = pl.BlockSpec(memory_space=pltpu.VMEM)
    in_smem = pl.BlockSpec(memory_space=pltpu.SMEM)
    return pl.pallas_call(
        kernel,
        in_specs=[in_smem] * smem + [in_vmem] * (len(args) - smem),
        out_specs=[in_vmem] * len(outs),
        out_shape=[jax.ShapeDtypeStruct(shape, dtype) for shape, dtype in outs],
        scratch_shapes=[pltpu.VMEM(shape, dtype) for shape, dtype in scratch],
        compiler_params=pltpu.CompilerParams(vmem_limit_bytes=(limit << 20) + held),
        cost_estimate=pl.CostEstimate(flops=0, bytes_accessed=0, transcendentals=0),
        name=name,
    )(*args)


class Flow:
    AHEAD = 64 << 20

    def __init__(self, loads, stores, semaphores):
        self.loads = loads
        self.stores = stores
        self.semaphores = semaphores
        self.started = 0
        self.waiting = set(range(len(loads)))
        self.begun = []
        self.whole = set()
        self.start_more(-1)

    def start_more(self, least):
        def size(j):
            held = self.loads[j][1]
            return math.prod(held.shape) * jnp.dtype(held.dtype).itemsize

        flying = sum(size(j) for j in self.waiting if j < self.started)
        while self.started < len(self.loads) and (self.started <= least or flying + size(self.started) <= self.AHEAD):
            flying += size(self.started)
            self.loads[self.started][2].start()
            self.started += 1

    def need(self, *refs):
        wanted = [j for j, load in enumerate(self.loads) if j in self.waiting and any(load[1] is r for r in refs)]
        for j in wanted:
            self.start_more(j)
        for j in wanted:
            self.waiting.discard(j)
            self.loads[j][2].wait()
        self.start_more(-1)

    def emit(self, ref, *where):
        for j, (out, held) in enumerate(self.stores):
            if held is ref:
                self.whole.add(j)
                source, target = (held.at[where], out.at[where]) if where else (held, out)
                copy = pltpu.make_async_copy(source, target, self.semaphores.at[len(self.begun)])
                copy.start()
                self.begun.append(copy)

    def close(self):
        self.need(*[held for _, held, _ in self.loads])
        for j, (_, held) in enumerate(self.stores):
            if j not in self.whole:
                self.emit(held)
        for copy in self.begun:
            copy.wait()


def hbm_call(kernel, name, outs, args, limit, scratch=(), smem=0, fixed_in=(), fixed_out=(), stores=None):
    arrays = args[smem:]
    moves_in = [j for j in range(len(arrays)) if j not in fixed_in]
    moves_out = [j for j in range(len(outs)) if j not in fixed_out]
    held = [(arrays[j].shape, arrays[j].dtype) for j in moves_in] + [outs[j] for j in moves_out] + list(scratch)
    size = sum(math.prod(shape) * jnp.dtype(dtype).itemsize for shape, dtype in held)

    resident = [(arrays[j].shape, arrays[j].dtype) for j in fixed_in] + [outs[j] for j in fixed_out]
    rest = sum(math.prod(shape) * jnp.dtype(dtype).itemsize for shape, dtype in resident)
    limit = max((limit << 20) + size, (63 << 20) - rest)

    def body(*refs):
        scalars, refs = refs[:smem], refs[smem:]
        ins, refs = list(refs[: len(arrays)]), refs[len(arrays) :]
        results, refs = list(refs[: len(outs)]), refs[len(outs) :]
        *kept, load_sems, store_sems = refs
        loads, kept_out = [], []
        for n, j in enumerate(moves_in):
            loads.append((ins[j], kept[n], pltpu.make_async_copy(ins[j], kept[n], load_sems.at[n])))
            ins[j] = kept[n]
        kept = kept[len(moves_in) :]
        for n, j in enumerate(moves_out):
            kept_out.append((results[j], kept[n]))
            results[j] = kept[n]
        flow = Flow(loads, kept_out, store_sems)
        kernel(flow, *scalars, *ins, *results, *kept[len(moves_out) :])
        flow.close()

    def place(count, fixed):
        return [pl.BlockSpec(memory_space=pltpu.VMEM if j in fixed else pl.ANY) for j in range(count)]

    return pl.pallas_call(
        body,
        in_specs=[pl.BlockSpec(memory_space=pltpu.SMEM)] * smem + place(len(arrays), fixed_in),
        out_specs=place(len(outs), fixed_out),
        out_shape=[jax.ShapeDtypeStruct(shape, dtype) for shape, dtype in outs],
        scratch_shapes=[pltpu.VMEM(shape, dtype) for shape, dtype in held]
        + [pltpu.SemaphoreType.DMA((max(len(moves_in), 1),)), pltpu.SemaphoreType.DMA((max(stores or len(moves_out), 1),))],
        compiler_params=pltpu.CompilerParams(vmem_limit_bytes=min(limit, 63 << 20)),
        cost_estimate=pl.CostEstimate(flops=0, bytes_accessed=0, transcendentals=0),
        name=name,
    )(*args)


def cuts(size, step):
    return [(i, min(step, size - i)) for i in range(0, size, step)]


def fold(rows):
    return jnp.sum(rows.reshape(rows.shape[0] // 8, 8, rows.shape[1]), axis=0)


def column_of(row):
    return jnp.transpose(jnp.broadcast_to(row, (8, row.shape[1])))[:, :1]


def row_of(column):
    return jnp.transpose(jnp.broadcast_to(column, (column.shape[0], 128)))[:8, :]


def join(refs, whole_ref):
    part = refs[0].shape[0]
    for j, ref in enumerate(refs):
        whole_ref[pl.ds(j * part, part), :] = ref[...]


def line_store(ref, scenes, scene, start, value):
    part = ref.shape[0] // scenes
    size = min(part, value.shape[0])
    for first in range(0, value.shape[0], size):
        at = start + first
        place = (scene ^ (at // part)) * part + at % part
        ref[pl.ds(pl.multiple_of(place, 16), size), :] = value[first : first + size]


def part_store(refs, start, value):
    part = refs[0].shape[0]
    size = min(part, value.shape[0])
    for first in range(0, value.shape[0], size):
        at = start + first
        refs[at // part][pl.ds(at % part, size), :] = value[first : first + size]


def kv_kernel(flow, tok_ref, gain_ref, wk_ref, wv_ref, k_ref, v_ref):
    flow.need(tok_ref, gain_ref, wk_ref, wv_ref)
    for start, size in cuts(tok_ref.shape[0], 256):
        rows = pl.ds(start, size)
        unit, _ = norm_parts(tok_ref[rows, :].astype(F32))
        low = (unit * gain_ref[...]).astype(BF16)
        k_ref[rows, :] = dot(low, wk_ref[...]).astype(BF16)
        v_ref[rows, :] = dot(low, wv_ref[...]).astype(BF16)
    flow.emit(k_ref)
    flow.emit(v_ref)


def keys_values(tok, gain, w_key, w_value):
    return hbm_call(kv_kernel, "keys_values", [(tok.shape, BF16)] * 2, (tok, gain, w_key, w_value), 8)


def score_piece(info_ref, p, k_ref, s_ref, query, columns, top, scale):
    begin, end = info_ref[0], info_ref[1]
    for start, size in cuts(k_ref.shape[0], 512):
        s = dot(k_ref[pl.ds(start, size), :], query, NT) * (scale * LOG2E)
        place = info_ref[2 + p] + start + lax.broadcasted_iota(jnp.int32, (size, 1), 0)
        s = s + jnp.where((place >= begin) & (place < end), 0.0, NEGATIVE)
        s_ref[pl.ds(start, size), columns] = s
        top = jnp.maximum(top, jnp.max(s.reshape(size // 8, 8, s.shape[1]), axis=0))
    return top


def weigh_piece(v_ref, s_ref, w_ref, columns, top, total, acc):
    for start, size in cuts(v_ref.shape[0], 512):
        w = jnp.exp2(s_ref[pl.ds(start, size), columns] - top)
        total = total + fold(w)
        w_ref[pl.ds(start, size), columns] = w.astype(BF16)
    part = dot(w_ref[:, columns], v_ref[...], TN)
    return total, part if acc is None else acc + part


def attend_kernel(parts, fresh, count, scale, flow, info_ref, gl_ref, wq_ref, *refs):
    new, refs = refs[: 3 * bool(fresh) + fresh], refs[3 * bool(fresh) + fresh :]
    lat_refs, refs = refs[:parts], refs[parts:]
    given = count - fresh
    k_refs, v_refs, refs = refs[:given], refs[given : 2 * given], refs[2 * given :]
    q_ref, acc_ref, top_ref, tot_ref, lat_ref = refs[:5]
    refs = refs[5:]
    k_refs, v_refs, refs = refs[:fresh] + k_refs, refs[fresh : 2 * fresh] + v_refs, refs[2 * fresh :]
    w_refs, s_refs = refs[:count], refs[count:]
    flow.need(*lat_refs, gl_ref, wq_ref)
    join(lat_refs, lat_ref)
    for j in range(fresh):
        kv_kernel(flow, new[3 + j], *new[:3], k_refs[j], v_refs[j])
    for start, size in cuts(lat_ref.shape[0], 512):
        rows = columns = pl.ds(start, size)
        unit, _ = norm_parts(lat_ref[rows, :].astype(F32))
        query = dot((unit * gl_ref[...]).astype(BF16), wq_ref[...]).astype(BF16)
        q_ref[rows, :] = query
        flow.need(*k_refs)
        top = jnp.full((8, size), NEGATIVE, F32)
        for p in range(count):
            top = score_piece(info_ref, p, k_refs[p], s_refs[p], query, columns, top, scale)
        top = jnp.max(top, axis=0, keepdims=True)
        total, acc = jnp.zeros((8, size), F32), None
        flow.need(*v_refs)
        for p in range(count):
            total, acc = weigh_piece(v_refs[p], s_refs[p], w_refs[p], columns, top, total, acc)
        acc_ref[rows, :] = acc
        if start == 0:
            flow.emit(lat_ref)
        for p in range(count):
            flow.emit(w_refs[p], slice(None), columns)
        flow.emit(acc_ref, rows)
        top_ref[:, columns] = jnp.broadcast_to(top, (8, size))
        tot_ref[:, columns] = total


def attend(info, lats, gl, wq, fresh, gt, wk, wv, keys, values, scale):
    rows, width = len(lats) * lats[0].shape[0], lats[0].shape[1]
    made = [(t.shape, BF16) for t in fresh]
    pieces = [t.shape[0] for t in (*fresh, *keys)]
    outs = [((rows, width), BF16), ((rows, width), F32), ((8, rows), F32), ((8, rows), F32), ((rows, width), BF16)]
    outs += made * 2 + [((n, rows), BF16) for n in pieces]
    new = (gt, wk, wv, *fresh) if fresh else ()
    q, acc, top, total, lat, *rest = hbm_call(
        functools.partial(attend_kernel, len(lats), len(fresh), len(pieces), scale),
        "attend",
        outs,
        (info, gl, wq, *new, *lats, *keys, *values),
        12,
        [((n, rows), F32) for n in pieces],
        smem=1,
        stores=len(outs) + (len(cuts(rows, 512)) - 1) * (len(pieces) + 1),
        fixed_out=(2, 3),
    )
    more = len(fresh)
    return q, acc, top, total, lat, rest[2 * more :], (*rest[:more], *keys), (*rest[more : 2 * more], *values)


def finish_kernel(
    scale, flow, info_ref, tok_ref, gt_ref, wk_ref, wv_ref, top_ref, q_ref, tot_ref, acc_ref, lat_ref, gm_ref, wo_ref, wu_ref, wd_ref,
    k_ref, v_ref, w_ref, factor_ref, mixed_ref, mlp_ref, state_ref, inner_ref, slope_ref, *refs,
):
    *out_refs, s_ref = refs
    kv_kernel(flow, tok_ref, gt_ref, wk_ref, wv_ref, k_ref, v_ref)
    flow.need(top_ref, q_ref, tot_ref, acc_ref)
    hidden = wu_ref.shape[1]
    for start, size in cuts(lat_ref.shape[0], 512):
        rows = columns = pl.ds(start, size)
        old = top_ref[:1, columns]
        top = jnp.broadcast_to(old, (8, size))
        top = score_piece(info_ref, 0, k_ref, s_ref, q_ref[rows, :], columns, top, scale)
        top = jnp.max(top, axis=0, keepdims=True)
        total, acc = weigh_piece(v_ref, s_ref, w_ref, columns, top, jnp.zeros((8, size), F32), None)
        shrink = jnp.exp2(old - top)
        total = jnp.sum(total, axis=0, keepdims=True) + jnp.sum(tot_ref[:, columns], axis=0, keepdims=True) * shrink
        inverse = 1.0 / total
        late, early = column_of(inverse), column_of(shrink * inverse)
        lane = lax.broadcasted_iota(jnp.int32, (size, 128), 1)
        factor_ref[rows, :] = jnp.where(lane == 0, late, early)
        mixed_ref[rows, :] = (acc * late + acc_ref[rows, :] * early).astype(BF16)
    flow.emit(w_ref)
    flow.need(lat_ref, wo_ref, gm_ref, wu_ref, wd_ref)
    for start, size in cuts(lat_ref.shape[0], 256):
        rows = pl.ds(start, size)
        state = lat_ref[rows, :].astype(F32) + dot(mixed_ref[rows, :], wo_ref[...])
        state_ref[rows, :] = state
        unit, _ = norm_parts(state)
        low = (unit * gm_ref[...]).astype(BF16)
        mlp_ref[rows, :] = low
        out = state
        for first, step in cuts(hidden, 512):
            some = pl.ds(first, step)
            u = dot(low, wu_ref[:, some])
            square = u * u
            t = jnp.tanh(u * (GELU_C + (GELU_C * GELU_A) * square))
            half = 0.5 + 0.5 * t
            inner = (u * half).astype(BF16)
            bend = u * ((0.5 * GELU_C) + (1.5 * GELU_C * GELU_A) * square)
            inner_ref[rows, some] = inner
            slope_ref[rows, some] = (half + bend * (1.0 - t * t)).astype(BF16)
            out = out + dot(inner, wd_ref[some, :])
        part_store(out_refs, start, out.astype(BF16))


def finish(info, parts, lat, q, acc, top, total, tail, gt, wk, wv, gm, wo, wu, wd, scale):
    rows, width = lat.shape
    hidden = wu.shape[1]
    tall = (rows, width)
    outs = [(tail.shape, BF16)] * 2 + [((tail.shape[0], rows), BF16), ((rows, 128), F32), (tall, BF16), (tall, BF16), (tall, F32)]
    outs += [((rows, hidden), BF16)] * 2 + [((rows // parts, width), BF16)] * parts
    out = hbm_call(
        functools.partial(finish_kernel, scale),
        "finish",
        outs,
        (info, tail, gt, wk, wv, top, q, total, acc, lat, gm, wo, wu, wd),
        22,
        [((tail.shape[0], rows), F32)],
        smem=1,
        fixed_in=(4, 6),
        fixed_out=(3, 4, 5, 6, 7, 8),
    )
    return out[:9], out[9:]


def mlp_back_kernel(
    parts, flow, info_ref, *refs,
):
    cot_refs, refs = refs[:parts], refs[parts:]
    wd_ref, slope_ref, wu_ref, state_ref, mixed_ref, factor_ref, gm_ref, wo_ref, inner_ref, mlp_ref, *refs = refs
    dstate_ref, late_ref, early_ref, dlate_ref, dearly_ref, keep_ref, send_ref, dwo_ref, dgain_ref = refs[:9]
    dpre_ref, dproj_ref, cot_ref = refs[9:]
    flow.need(*cot_refs, wd_ref)
    join(cot_refs, cot_ref)
    hidden, width = wd_ref.shape

    def pack(half, first, value):
        rows = pl.ds(first, value.shape[0])

        @pl.when(info_ref[0] == half)
        def _():
            keep_ref[rows, :] = value.astype(BF16)

        @pl.when(info_ref[0] != half)
        def _():
            send_ref[rows, :] = value.astype(BF16)

    total = jnp.zeros((8, width), F32)
    for start, size in cuts(cot_ref.shape[0], 256):
        rows = pl.ds(start, size)
        cot = cot_ref[rows, :]
        d_mlp = None
        for first, step in cuts(hidden, 512):
            some = pl.ds(first, step)
            d_inner = dot(cot, wd_ref[some, :], NT)
            d_pre = (slope_ref[rows, some].astype(F32) * d_inner).astype(BF16)
            dpre_ref[rows, some] = d_pre
            flow.need(wu_ref)
            part = dot(d_pre, wu_ref[:, some], NT)
            d_mlp = part if d_mlp is None else d_mlp + part
        flow.need(gm_ref, wo_ref)
        unit, inverse = norm_parts(state_ref[rows, :])
        total = total + fold(d_mlp * unit)
        d_state = cot.astype(F32) + norm_back(d_mlp, unit, inverse, gm_ref[...])
        dstate_ref[rows, :] = d_state
        d_proj = d_state.astype(BF16)
        dproj_ref[rows, :] = d_proj
        d_att = dot(d_proj, wo_ref[...], NT)
        mixed = mixed_ref[rows, :].astype(F32)
        for lane, part_ref, delta_ref in ((0, late_ref, dlate_ref), (1, early_ref, dearly_ref)):
            part = (d_att * factor_ref[rows, lane : lane + 1]).astype(BF16)
            part_ref[rows, :] = part
            delta = jnp.sum(part.astype(F32) * mixed, axis=-1, keepdims=True)
            delta_ref[:, rows] = row_of(delta)
    dgain_ref[...] = total
    for ref in (dstate_ref, late_ref, early_ref, dlate_ref, dearly_ref):
        flow.emit(ref)
    for first, step in cuts(hidden, 512):
        pack(0, first, dot(inner_ref[:, first : first + step], cot_ref[...], TN))
    for first, step in cuts(hidden, 512):
        pack(1, first, dot(mlp_ref[...], dpre_ref[:, first : first + step], TN))
    dwo_ref[...] = dot(mixed_ref[...], dproj_ref[...], TN).astype(BF16)


def mlp_back(info, cots, slope, state, mixed, mlp, inner, factor, gm, wo, wu, wd):
    rows, width = state.shape
    hidden = wu.shape[1]
    tall, flat = (rows, width), (8, rows)
    outs = [(tall, F32), (tall, BF16), (tall, BF16), (flat, F32), (flat, F32)]
    outs += [((hidden, width), BF16)] * 2 + [((width, width), BF16), ((8, width), F32)]
    return hbm_call(
        functools.partial(mlp_back_kernel, len(cots)),
        "mlp_back",
        outs,
        (info, *cots, wd, slope, wu, state, mixed, factor, gm, wo, inner, mlp),
        20,
        [((rows, hidden), BF16), (tall, BF16), (tall, BF16)],
        smem=1,
        fixed_in=[len(cots) + j for j in (1, 3, 4, 5, 8, 9)],
        fixed_out=range(3, len(outs)),
    )


def attention_back_kernel(count, start, parts, extra, scale, flow, info_ref, *refs):
    q_ref, wk_ref, wv_ref, gain_ref, *refs = refs
    datt_ref, delta_ref, *refs = refs
    v_refs, w_refs, t_refs, k_refs = (refs[j : 4 * count : 4] for j in range(4))
    refs = refs[4 * count :]
    sums, refs = refs[:start], refs[start:]
    if parts:
        lat_ref, gl_ref, wq_ref, dstate_ref, dwo_ref, dgmlp_ref, *refs = refs
    dtok_refs, refs = refs[:count], refs[count:]
    if parts:
        dlat_ref, *refs = refs
        keep_ref, send_ref, dq_ref, akey_ref, aval_ref, dgain_ref, latlow_ref, dquery_ref, *refs = refs
    else:
        dq_ref, akey_ref, aval_ref, dgain_ref, *refs = refs
    dscore_ref, low_ref, dkey_ref, dval_ref, part_ref = refs
    totals = (dq_ref, akey_ref, aval_ref, dgain_ref)
    flow.need(q_ref, wk_ref, wv_ref, gain_ref)
    for p in range(count):
        size = k_refs[p].shape[0]
        flow.need(datt_ref, delta_ref, v_refs[p], w_refs[p], t_refs[p], k_refs[p])
        begin, end, first_place = info_ref[1 + 3 * p], info_ref[2 + 3 * p], info_ref[3 + 3 * p]
        part_ref[...] = jnp.zeros_like(part_ref)
        for first, step in cuts(size, 256):
            rows = pl.ds(first, step)
            active = (first_place + first < end) & (first_place + first + step > begin)

            @pl.when(active)
            def _(p=p, rows=rows):
                d_prob = dot(v_refs[p][rows, :], datt_ref[...], NT)
                d_score = (w_refs[p][rows, :].astype(F32) * (d_prob - delta_ref[:1, :])).astype(BF16)
                dscore_ref[rows, :] = d_score
                d_key = (dot(d_score, q_ref[...]) * scale).astype(BF16)
                d_value = dot(w_refs[p][rows, :], datt_ref[...]).astype(BF16)
                dkey_ref[rows, :] = d_key
                dval_ref[rows, :] = d_value
                unit, _ = norm_parts(t_refs[p][rows, :].astype(F32))
                low_ref[rows, :] = (unit * gain_ref[...]).astype(BF16)
                d_tok = dot(d_key, wk_ref[...], NT) + dot(d_value, wv_ref[...], NT)
                dtok_refs[p][rows, :] = d_tok.astype(BF16)
                part_ref[...] += fold(d_tok * unit)

            @pl.when(jnp.logical_not(active))
            def _(p=p, rows=rows):
                for ref in (dscore_ref, dkey_ref, dval_ref, low_ref, dtok_refs[p]):
                    ref[rows, :] = jnp.zeros((rows.size, ref.shape[1]), BF16)

        flow.emit(dtok_refs[p])
        dgain = part_ref[...]
        here = pl.ds(0, size)
        news = (
            dot(dscore_ref[here, :], k_refs[p][...], TN),
            dot(low_ref[here, :], dkey_ref[here, :], TN),
            dot(low_ref[here, :], dval_ref[here, :], TN),
            dgain,
        )
        if p == 0:
            flow.need(*sums)
        for j, (ref, value) in enumerate(zip(totals, news)):
            if p == 0:
                ref[...] = value + sums[j][...] if sums else value
            else:
                ref[...] += value
    if not parts:
        return
    flow.need(lat_ref, gl_ref, wq_ref, dstate_ref, dwo_ref, dgmlp_ref)
    total = None
    width = wq_ref.shape[0]
    for first, size in cuts(lat_ref.shape[0], 256):
        rows = pl.ds(first, size)
        unit, inverse = norm_parts(lat_ref[rows, :].astype(F32))
        gain = gl_ref[...]
        latlow_ref[rows, :] = (unit * gain).astype(BF16)
        d_query = (dq_ref[rows, :] * scale).astype(BF16)
        dquery_ref[rows, :] = d_query
        d_low = dot(d_query, wq_ref[...], NT)
        line_store(dlat_ref, parts, info_ref[1 + 3 * count], first, (dstate_ref[rows, :] + norm_back(d_low, unit, inverse, gain)).astype(BF16))
        part = fold(d_low * unit)
        total = part if total is None else total + part
    flow.emit(dlat_ref)
    d_wq = dot(latlow_ref[...], dquery_ref[...], TN)
    gains = [jnp.sum(g, axis=0, keepdims=True) for g in (total, dgain_ref[...], dgmlp_ref[...])]
    line = lax.broadcasted_iota(jnp.int32, (extra, width), 0)
    block = jnp.where(line == 0, gains[0], jnp.where(line == 1, gains[1], jnp.where(line == 2, gains[2], 0.0)))
    halves = ((d_wq, akey_ref), (aval_ref, dwo_ref))
    for ref, core in ((keep_ref, info_ref[0]), (send_ref, 1 - info_ref[0])):
        ref[pl.ds(2 * width, extra), :] = block.astype(BF16)
        for h, half in enumerate(halves):

            @pl.when(core == h)
            def _(ref=ref, half=half):
                for j, piece in enumerate(half):
                    ref[pl.ds(j * width, width), :] = piece[...].astype(BF16)


def attention_back(info, q, wk, wv, gain, grads, values, weights, tokens, keys, sums, latents, parts, extra, scale):
    rows, width = q.shape
    square = ((width, width), F32)
    totals = [((rows, width), F32), square, square, ((8, width), F32)]
    most = max(k.shape[0] for k in keys)
    work = [((most, rows), BF16)] + [((most, width), BF16)] * 3 + [((8, width), F32)]
    outs = [(k.shape, BF16) for k in keys]
    by_piece = [a for piece in zip(values, weights, tokens, keys) for a in piece]
    args = (info, q, wk, wv, gain, *grads, *by_piece, *sums)
    if latents:
        args = (*args, *latents)
        outs += [((rows, width), BF16)] + [((2 * width + extra, width), BF16)] * 2
        work = totals + [((rows, width), BF16)] * 2 + work
    else:
        outs += totals
        parts = 0
    kernel = functools.partial(attention_back_kernel, len(keys), len(sums), parts, extra, scale)
    first = 6 + 4 * len(keys)
    fixed_in = [5] + [first + j for j in range(len(sums))]
    fixed_out = [] if latents else [len(keys) + j for j in range(4)]
    if latents:
        fixed_in.append(first + len(sums) + len(latents) - 1)
    out = hbm_call(kernel, "attention_back", outs, args, 12, work, 1, fixed_in, fixed_out)
    return out[: len(keys)], out[len(keys) :]


def token_back_kernel(count, flow, tok_ref, gain_ref, *refs):
    flow.need(tok_ref, gain_ref, *refs[:count])
    for start, size in cuts(tok_ref.shape[0], 256):
        rows = pl.ds(start, size)
        unit, inverse = norm_parts(tok_ref[rows, :].astype(F32))
        total = refs[0][rows, :].astype(F32)
        for ref in refs[1:count]:
            total = total + ref[rows, :].astype(F32)
        refs[count][rows, :] = norm_back(total, unit, inverse, gain_ref[...])
        flow.emit(refs[count], rows)


def token_back(tok, gain, parts):
    args = (tok, gain, *parts)
    [out] = hbm_call(functools.partial(token_back_kernel, len(parts)), "token_back", [(tok.shape, F32)], args, 8, stores=len(cuts(tok.shape[0], 256)))
    return out


def picks(shape, scenes, scene, transposed=False):
    along = lax.broadcasted_iota(jnp.int32, shape, 1 if transposed else 0)
    across = lax.broadcasted_iota(jnp.int32, shape, 0 if transposed else 1)
    return jnp.where(across == along * scenes + scene, 1.0, 0.0).astype(BF16)


def sort_kernel(flow, info_ref, rows_ref, *out_refs):
    flow.need(rows_ref)
    for k, ref in enumerate(out_refs):
        take = picks((ref.shape[0], rows_ref.shape[0]), len(out_refs), info_ref[0] ^ k)
        ref[...] = dot(take, rows_ref[...]).astype(BF16)
        flow.emit(ref)


def sort_rows(info, value, scenes):
    rows, width = value.shape
    return hbm_call(sort_kernel, "sort_rows", [((rows // scenes, width), BF16)] * scenes, (info, value), 16, smem=1)


def unsort_kernel(scenes, flow, info_ref, *refs):
    *in_refs, out_ref = refs
    flow.need(*in_refs)
    if len(in_refs) == 1:
        size = out_ref.shape[0] // scenes
        in_refs = [in_refs[0].at[pl.ds(k * size, size)] for k in range(scenes)]
    rows, part = out_ref.shape[0], in_refs[0].shape[0]
    step = rows // scenes
    for start in range(0, rows, step):
        total = None
        for k, ref in enumerate(in_refs):
            some = part // scenes
            first = start // scenes
            put = picks((step, some), scenes, info_ref[0] ^ k, transposed=True)
            value = dot(put, ref[pl.ds(first, some), :])
            total = value if total is None else total + value
        out_ref[pl.ds(start, step), :] = total.astype(out_ref.dtype)
        flow.emit(out_ref, pl.ds(start, step))


def unsort_rows(info, parts, scenes, dtype):
    rows, width = sum(p.shape[0] for p in parts), parts[0].shape[1]
    kernel = functools.partial(unsort_kernel, scenes)
    [out] = hbm_call(kernel, "unsort_rows", [((rows, width), dtype)], (info, *parts), 16, smem=1, stores=scenes)
    return out


def split_kernel(count, place, extra, info_ref, *refs):
    in_refs, out_refs = refs[:count], refs[count:]
    rest = None
    if extra and out_refs[-1].shape[0] == extra and len(out_refs) == 2:
        *out_refs, rest = out_refs
    body = in_refs[0].shape[0] - extra
    step = body // len(out_refs)

    def total(start, rows):
        value = in_refs[0][pl.ds(start, rows), :].astype(F32)
        for ref in in_refs[1:]:
            value = value + ref[pl.ds(start, rows), :].astype(F32)
        return value.astype(BF16)

    shared = total(body, extra) if extra else None
    for k, ref in enumerate(out_refs):
        start = (info_ref[place] ^ k) * step if len(out_refs) > 1 else 0
        ref[pl.ds(0, step), :] = total(start if isinstance(start, int) else pl.multiple_of(start, 16), step)
        if extra and rest is None:
            ref[pl.ds(step, extra), :] = shared
    if rest is not None:
        rest[...] = shared


def split_sum(info, arrays, parts, place, extra):
    rows, width = arrays[0].shape
    step = (rows - extra) // parts
    if parts > 1:
        outs = [((step + extra, width), BF16)] * parts
    else:
        outs = [((step, width), BF16)] + ([((extra, width), BF16)] if extra else [])
    kernel = functools.partial(split_kernel, len(arrays), place, extra)
    return vmem_call(kernel, "split_sum", outs, (info, *arrays), 8, smem=1)


def unpack_kernel(width, count, crossed, info_ref, *refs):
    core, quad, line = info_ref[0], info_ref[1], info_ref[2]
    out_refs, (mine_ref, other_ref) = refs[2 * count : -2], refs[-2:]
    join(refs[:count], mine_ref)
    join(refs[count : 2 * count], other_ref)
    half = mine_ref.shape[0]
    lines = info_ref.shape[0] - 3
    block = half // (4 * lines)
    for h in range(2):
        for m in range(4):
            for z in range(lines):
                chip, spot = quad ^ m, line ^ z
                if crossed:
                    late = spot // (lines // 2)
                    chip = jnp.where(late == 0, chip, (chip % 2) * 2 + chip // 2)
                    spot = (late * 4 + chip) * (lines // 2) + spot % (lines // 2)
                else:
                    spot = chip * lines + spot
                rows = pl.ds(pl.multiple_of(spot * block, 16), block)
                value = jnp.where(core == h, mine_ref[rows, :].astype(F32), other_ref[rows, :].astype(F32))
                at = h * half + (m * lines + z) * block
                total = 0
                for ref in out_refs:
                    tall = ref.shape[0] * (ref.shape[1] // width)
                    if total <= at < total + tall:
                        inside = at - total
                        slab, row = inside // ref.shape[0], inside % ref.shape[0]
                        ref[pl.ds(row, block), pl.ds(slab * width, width)] = value
                    total += tall


class Sums:
    def __init__(self, seqs, blocks):
        self.seqs, self.blocks = seqs, blocks
        self.lines = blocks // 2
        seq, blk = lax.axis_index("seq"), lax.axis_index("blk")
        places = [seq % 2, (seq // 2) * 2 + blk % 2, blk // 2] + [seq * 0] * self.lines
        self.info = jnp.stack(places).astype(jnp.int32)

    def flip(self, value, seq_mask, blk_mask):
        pairs = [
            (s * self.blocks + b, (s ^ seq_mask) * self.blocks + (b ^ blk_mask))
            for s in range(self.seqs)
            for b in range(self.blocks)
        ]
        return lax.ppermute(value, ("seq", "blk"), pairs)

    def to_core(self, value):
        return self.flip(value, 1, 0)

    def to_quad(self, values):
        return [self.flip(v, 2 * (k // 2), k % 2) for k, v in enumerate(values, 1)]

    def to_line(self, values):
        return [self.flip(v, 0, 2 * k) for k, v in enumerate(values, 1)]

    def add_core(self, keep, received, extra=0):
        return split_sum(self.info, [keep, received], 4, 1, extra)

    def add_quad(self, keep, received, extra=0):
        return split_sum(self.info, [keep, *received], self.lines, 2, extra)

    def add_line(self, keep, received, extra=0):
        return split_sum(self.info, [keep, *received], 1, 0, extra)

    def unpack(self, mine, other, shapes, crossed=False):
        outs = [(shape, F32) for shape in shapes]
        rows, width = mine[0].shape
        kernel = functools.partial(unpack_kernel, width, len(mine), crossed)
        work = [((rows * len(mine), width), BF16)] * 2
        return vmem_call(kernel, "unpack", outs, (self.info, *mine, *other), 16, work, smem=1)


def after(value, *others):
    return lax.optimization_barrier((value, others))[0]


def local(
    sizes, latents, tokens, lengths, gain_lat, gain_tok, gain_mlp, w_query, w_key, w_value, w_out, w_up, w_down, d_out
):
    lat, tok, cot = latents[0], tokens[0], d_out[0]
    scene_lengths = lengths[0]
    scenes = scene_lengths.shape[0]
    seqs, blocks = sizes["seq"], sizes["blk"]
    group = blocks // scenes
    span, width = tok.shape
    hidden = w_up.shape[1]
    scale = width ** (-0.5)
    position = lax.axis_index("blk")
    scene, member = position // group, position % group
    scene_info = scene.astype(jnp.int32).reshape(1)
    gl, gt, gm = (g.reshape(1, width) for g in (gain_lat, gain_tok, gain_mlp))
    lines = [[m + group * k for k in range(scenes)] for m in range(group)]
    sums = Sums(seqs, blocks)

    def exchange(value, mask):
        return sums.flip(value, 0, mask)

    def across(values):
        return [exchange(v, group * k) if k else v for k, v in enumerate(values)]

    order = jnp.arange(scenes, dtype=jnp.int32)
    begin = jnp.sum(jnp.where(order < scene, scene_lengths, 0))
    end = begin + jnp.sum(jnp.where(order == scene, scene_lengths, 0))
    base = scene * group * span
    tail_rows = (scenes - 1) * group * span // 8
    starts = [base + (member ^ k) * span for k in [*range(1, group), 0]]
    main_info = jnp.stack([begin, end, *starts]).astype(jnp.int32)
    tail_info = jnp.stack([begin, end, base - tail_rows]).astype(jnp.int32)

    lat_parts = sort_rows(scene_info, lat, scenes)
    others = [exchange(tok, k) for k in range(1, group)]
    lat_in = across(lat_parts)
    cot_parts = sort_rows(scene_info, after(cot, lat_parts), scenes)
    own_kv = keys_values(after(tok, cot_parts), gt, w_key, w_value)
    lat_in, others, cot_parts, own_kv, main_info, tail_info = lax.optimization_barrier(
        (lat_in, others, cot_parts, own_kv, main_info, tail_info)
    )
    cot_near = exchange(cot_parts[1], group)

    pieces = [tok, *others]
    lowest = (group * span - tail_rows) // span
    needed = []
    for owner in range(lowest, group):
        block = pieces[owner]
        for m in range(1, group):
            block = jnp.where(member == m, pieces[owner ^ m], block)
        needed.append(block)
    needed = jnp.concatenate(needed, axis=0) if len(needed) > 1 else needed[0]
    pairs = [(i, i + group) for i in range(blocks - group)]
    sent = needed[needed.shape[0] - tail_rows :]
    tail = lax.ppermute(sent, "blk", pairs)
    fresh = list(others) if group == 2 else []
    given = [own_kv] if fresh else [keys_values(piece, gt, w_key, w_value) for piece in others] + [own_kv]
    made_keys, made_values = zip(*given)
    query, acc, top, total, lat_set, weights, keys, values = attend(
        main_info, lat_in, gl, w_query, after(fresh, sent), gt, w_key, w_value, made_keys, made_values, scale
    )
    tail, query, cot_parts, cot_near = lax.optimization_barrier((tail, query, cot_parts, cot_near))

    cot_in = [cot_parts[0], cot_near, *[exchange(cot_parts[k], group * k) for k in range(2, scenes)]]
    saved, out_parts = finish(
        tail_info, scenes, lat_set, query, acc, top, total, tail, gt, w_key, w_value, gm, w_out, w_up, w_down, scale
    )
    tail_key, tail_value, tail_weight, factor, mixed, mlp, state, inner, slope = saved
    cot_in, out_parts, slope = lax.optimization_barrier((cot_in, out_parts, slope))
    out_back = across(out_parts)
    d_state, d_late, d_early, late, early_delta, keep, send, d_wo, dg_mlp = mlp_back(
        sums.info, cot_in, slope, state, mixed, mlp, inner, factor, gm, w_out, w_up, w_down
    )

    out_back, keep, send, d_early, d_late = lax.optimization_barrier((out_back, keep, send, d_early, d_late))
    received = sums.to_core(send)
    pieces = [(tail_value, tail_weight, tail, tail_key, tail_info)]
    for j, piece in enumerate((*others, tok)):
        pieces.append((values[j], weights[j], piece, keys[j], jnp.stack([begin, end, starts[j]]).astype(jnp.int32)))
    calls, size = [pieces[:1], []], 0
    for piece in pieces[1:]:
        if calls[-1] and size + piece[0].shape[0] > 3 * span:
            calls.append([])
            size = 0
        calls[-1].append(piece)
        size += piece[0].shape[0]
    extra = 16
    d_toks, kept = [], []
    for j, call in enumerate(calls):
        some_values, some_weights, some_tokens, some_keys, places = zip(*call)
        places = jnp.concatenate([sums.info[:1], *places, scene_info])
        latents = (lat_set, gl, w_query, d_state, d_wo, dg_mlp) if j == len(calls) - 1 else ()
        grads = (d_early, early_delta) if j else (d_late, late)
        some, kept = attention_back(
            places, query, w_key, w_value, gt, grads, some_values, some_weights, some_tokens, some_keys, kept,
            latents, scenes, extra, scale,
        )
        d_toks += some
        if j == 0:
            received, d_toks, kept = lax.optimization_barrier((received, d_toks, kept))
            keep, *sends = sums.add_core(keep, received)
            d_early = after(d_early, keep)
            received = sums.to_quad(sends)
            d_tail = lax.ppermute(d_toks[0], "blk", [(j, i) for i, j in pairs])
    received, d_tail, d_toks, kept = lax.optimization_barrier((received, d_tail, d_toks, kept))
    _, *returned, own = d_toks
    d_lat_set, small_keep, small_send = kept

    returned = dict(enumerate(returned, 1))
    own_tail = []
    for owner in range(lowest, group):
        start = owner * span - (group * span - tail_rows)
        chunk = d_tail[max(start, 0) : start + span]
        chunk = jnp.pad(chunk, ((span - chunk.shape[0], 0), (0, 0)))
        for k in range(1, group):
            returned[k] = returned[k] + jnp.where(member == owner ^ k, chunk, 0)
        own_tail.append(jnp.where(member == owner, chunk, 0))
    small_got = sums.to_core(small_send)
    keep, *sends = sums.add_quad(keep, received)
    received = sums.to_line(sends)
    returned = [exchange(after(returned[k], keep), k) for k in range(1, group)]
    output = unsort_rows(scene_info, after(out_back, keep), scenes, BF16)
    small_got, received, output = lax.optimization_barrier((small_got, received, output))
    [shard] = sums.add_line(keep, received)
    small_keep, *small_sends = sums.add_core(small_keep, small_got, extra)
    small_got = sums.to_quad(small_sends)
    block = shard
    for j in range(sums.lines.bit_length() - 1):
        far = sums.flip(block, 0, 2 << j)
        if j == sums.lines.bit_length() - 2:
            small_got, far = lax.optimization_barrier((small_got, far))
        block = jnp.concatenate([block, far], axis=0)
    half = block.shape[0] // 2
    near_a, near_b = block[:half], block[half:]
    far_a, far_b = sums.flip(near_a, 0, 1), sums.flip(near_b, 2, 0)
    small_keep, *small_sends = sums.add_quad(small_keep, small_got, extra)
    small_got = sums.to_line(small_sends)
    small_got, far_a, far_b, returned = lax.optimization_barrier((small_got, far_a, far_b, returned))
    two_a, two_b = jnp.concatenate([near_a, far_a], axis=0), jnp.concatenate([near_b, far_b], axis=0)
    last_a, last_b = sums.flip(two_a, 2, 0), sums.flip(two_b, 0, 1)
    small_shard, gains = sums.add_line(small_keep, small_got, extra)
    small_block = small_shard
    for j in range(sums.lines.bit_length() - 1):
        far = sums.flip(small_block, 0, 2 << j)
        if j == sums.lines.bit_length() - 2:
            d_tokens = token_back(tok, gt, [own, *own_tail, *after(returned, small_block)])
            far = after(far, d_tokens)
        small_block = jnp.concatenate([small_block, far], axis=0)
    last_a, last_b, small_block = lax.optimization_barrier((last_a, last_b, small_block))
    d_lat_back = lax.all_to_all(after(d_lat_set, small_block), "blk", 0, 0, axis_index_groups=lines, tiled=True)
    small_got = sums.to_quad([small_block] * 3)
    mine = [two_a, last_a, two_b, last_b]
    other = [sums.to_core(v) for v in mine]
    d_w_down, d_w_up = sums.unpack(mine, other, [(hidden, width), (width, hidden)], crossed=True)
    small_got, d_lat_back, d_w_up = lax.optimization_barrier((small_got, d_lat_back, d_w_up))
    small_mine = [jnp.concatenate([small_block, *small_got], axis=0)]
    small_other = [sums.to_core(small_mine[0])]
    d_latents = unsort_rows(0 * scene_info, [after(d_lat_back, small_mine)], scenes, F32)
    squares = sums.unpack(small_mine, after(small_other, d_latents), [(width, width)] * 4)
    gains = gains.astype(F32)
    return (output[None], d_latents[None], d_tokens[None], *squares, d_w_up, d_w_down, gains[0], gains[1], gains[2])


def solution(mesh):
    split = P("seq", "blk", None)
    in_specs = (split, split, P("seq", None)) + (P(),) * 9 + (split,)
    out_specs = (split,) * 3 + (P(),) * 9
    return jax.shard_map(
        functools.partial(local, dict(mesh.shape)), mesh=mesh, in_specs=in_specs, out_specs=out_specs, check_vma=False
    )
```

```python
import functools
import math

import jax
import jax.numpy as jnp
from jax import lax
from jax.experimental import pallas as pl
from jax.experimental.pallas import tpu as pltpu
from jax.sharding import PartitionSpec as P

EPSILON = 1e-05
NEGATIVE = -1e30
ROOM = (64 << 20) - (160 << 10)
LOG2E = 1.4426950408889634
GELU_C = math.sqrt(2.0 / math.pi)
GELU_A = 0.044715
F32 = jnp.float32
BF16 = jnp.bfloat16
NN = (((1,), (0,)), ((), ()))
NT = (((1,), (1,)), ((), ()))
TN = (((0,), (0,)), ((), ()))


def dot(left, right, dims=NN):
    return lax.dot_general(left, right, dims, preferred_element_type=F32)


def norm_parts(rows):
    center = rows - jnp.mean(rows, axis=-1, keepdims=True)
    spread = jnp.mean(center * center, axis=-1, keepdims=True)
    inverse = lax.rsqrt(spread + EPSILON)
    return center * inverse, inverse


def norm_back(d_normed, unit, inverse, gain):
    d_unit = d_normed * gain
    mean_d = jnp.mean(d_unit, axis=-1, keepdims=True)
    mean_p = jnp.mean(d_unit * unit, axis=-1, keepdims=True)
    return inverse * (d_unit - mean_d - unit * mean_p)


def vmem_call(kernel, name, outs, args, limit, scratch=(), smem=0):
    held = sum(math.prod(shape) * jnp.dtype(dtype).itemsize for shape, dtype in scratch)
    in_vmem = pl.BlockSpec(memory_space=pltpu.VMEM)
    in_smem = pl.BlockSpec(memory_space=pltpu.SMEM)
    return pl.pallas_call(
        kernel,
        in_specs=[in_smem] * smem + [in_vmem] * (len(args) - smem),
        out_specs=[in_vmem] * len(outs),
        out_shape=[jax.ShapeDtypeStruct(shape, dtype) for shape, dtype in outs],
        scratch_shapes=[pltpu.VMEM(shape, dtype) for shape, dtype in scratch],
        compiler_params=pltpu.CompilerParams(vmem_limit_bytes=(limit << 20) + held),
        cost_estimate=pl.CostEstimate(flops=0, bytes_accessed=0, transcendentals=0),
        name=name,
    )(*args)


class Flow:
    AHEAD = 64 << 20

    def __init__(self, loads, stores, semaphores):
        self.loads = loads
        self.stores = stores
        self.semaphores = semaphores
        self.started = 0
        self.waiting = set(range(len(loads)))
        self.begun = []
        self.whole = set()
        self.start_more(-1)

    def start_more(self, least):
        def size(j):
            held = self.loads[j][1]
            return math.prod(held.shape) * jnp.dtype(held.dtype).itemsize

        flying = sum(size(j) for j in self.waiting if j < self.started)
        while self.started < len(self.loads) and (self.started <= least or flying + size(self.started) <= self.AHEAD):
            flying += size(self.started)
            self.loads[self.started][2].start()
            self.started += 1

    def need(self, *refs):
        wanted = [j for j, load in enumerate(self.loads) if j in self.waiting and any(load[1] is r for r in refs)]
        for j in wanted:
            self.start_more(j)
        for j in wanted:
            self.waiting.discard(j)
            self.loads[j][2].wait()
        self.start_more(-1)

    def emit(self, ref, *where):
        for j, (out, held) in enumerate(self.stores):
            if held is ref:
                self.whole.add(j)
                source, target = (held.at[where], out.at[where]) if where else (held, out)
                copy = pltpu.make_async_copy(source, target, self.semaphores.at[len(self.begun)])
                copy.start()
                self.begun.append(copy)

    def close(self):
        self.need(*[held for _, held, _ in self.loads])
        for j, (_, held) in enumerate(self.stores):
            if j not in self.whole:
                self.emit(held)
        for copy in self.begun:
            copy.wait()


def hbm_call(kernel, name, outs, args, limit, scratch=(), smem=0, fixed_in=(), fixed_out=(), stores=None):
    arrays = args[smem:]
    moves_in = [j for j in range(len(arrays)) if j not in fixed_in]
    moves_out = [j for j in range(len(outs)) if j not in fixed_out]
    held = [(arrays[j].shape, arrays[j].dtype) for j in moves_in] + [outs[j] for j in moves_out] + list(scratch)
    size = sum(math.prod(shape) * jnp.dtype(dtype).itemsize for shape, dtype in held)

    resident = [(arrays[j].shape, arrays[j].dtype) for j in fixed_in] + [outs[j] for j in fixed_out]
    rest = sum(math.prod(shape) * jnp.dtype(dtype).itemsize for shape, dtype in resident)
    limit = max((limit << 20) + size, ROOM - rest)

    def body(*refs):
        scalars, refs = refs[:smem], refs[smem:]
        ins, refs = list(refs[: len(arrays)]), refs[len(arrays) :]
        results, refs = list(refs[: len(outs)]), refs[len(outs) :]
        *kept, load_sems, store_sems = refs
        loads, kept_out = [], []
        for n, j in enumerate(moves_in):
            loads.append((ins[j], kept[n], pltpu.make_async_copy(ins[j], kept[n], load_sems.at[n])))
            ins[j] = kept[n]
        kept = kept[len(moves_in) :]
        for n, j in enumerate(moves_out):
            kept_out.append((results[j], kept[n]))
            results[j] = kept[n]
        flow = Flow(loads, kept_out, store_sems)
        kernel(flow, *scalars, *ins, *results, *kept[len(moves_out) :])
        flow.close()

    def place(count, fixed):
        return [pl.BlockSpec(memory_space=pltpu.VMEM if j in fixed else pl.ANY) for j in range(count)]

    return pl.pallas_call(
        body,
        in_specs=[pl.BlockSpec(memory_space=pltpu.SMEM)] * smem + place(len(arrays), fixed_in),
        out_specs=place(len(outs), fixed_out),
        out_shape=[jax.ShapeDtypeStruct(shape, dtype) for shape, dtype in outs],
        scratch_shapes=[pltpu.VMEM(shape, dtype) for shape, dtype in held]
        + [pltpu.SemaphoreType.DMA((max(len(moves_in), 1),)), pltpu.SemaphoreType.DMA((max(stores or len(moves_out), 1),))],
        compiler_params=pltpu.CompilerParams(vmem_limit_bytes=min(limit, ROOM)),
        cost_estimate=pl.CostEstimate(flops=0, bytes_accessed=0, transcendentals=0),
        name=name,
    )(*args)


def cuts(size, step):
    return [(i, min(step, size - i)) for i in range(0, size, step)]


def fold(rows):
    return jnp.sum(rows.reshape(rows.shape[0] // 8, 8, rows.shape[1]), axis=0)


def column_of(row):
    return jnp.transpose(jnp.broadcast_to(row, (8, row.shape[1])))[:, :1]


def row_of(column):
    return jnp.transpose(jnp.broadcast_to(column, (column.shape[0], 128)))[:8, :]


def join(refs, whole_ref):
    part = refs[0].shape[0]
    for j, ref in enumerate(refs):
        whole_ref[pl.ds(j * part, part), :] = ref[...]


def line_store(ref, scenes, scene, start, value):
    part = ref.shape[0] // scenes
    size = min(part, value.shape[0])
    for first in range(0, value.shape[0], size):
        at = start + first
        place = (scene ^ (at // part)) * part + at % part
        ref[pl.ds(pl.multiple_of(place, 16), size), :] = value[first : first + size]


def part_store(refs, start, value):
    part = refs[0].shape[0]
    size = min(part, value.shape[0])
    for first in range(0, value.shape[0], size):
        at = start + first
        refs[at // part][pl.ds(at % part, size), :] = value[first : first + size]


def kv_kernel(flow, tok_ref, gain_ref, wk_ref, wv_ref, k_ref, v_ref):
    flow.need(tok_ref, gain_ref, wk_ref, wv_ref)
    for start, size in cuts(tok_ref.shape[0], 256):
        rows = pl.ds(start, size)
        unit, _ = norm_parts(tok_ref[rows, :].astype(F32))
        low = (unit * gain_ref[...]).astype(BF16)
        k_ref[rows, :] = dot(low, wk_ref[...]).astype(BF16)
        v_ref[rows, :] = dot(low, wv_ref[...]).astype(BF16)
    flow.emit(k_ref)
    flow.emit(v_ref)


def keys_values(tok, gain, w_key, w_value):
    return hbm_call(kv_kernel, "keys_values", [(tok.shape, BF16)] * 2, (tok, gain, w_key, w_value), 8)


def score_piece(info_ref, p, k_ref, s_ref, query, columns, top, scale):
    begin, end = info_ref[0], info_ref[1]
    for start, size in cuts(k_ref.shape[0], 512):
        s = dot(k_ref[pl.ds(start, size), :], query, NT) * (scale * LOG2E)
        place = info_ref[2 + p] + start + lax.broadcasted_iota(jnp.int32, (size, 1), 0)
        s = s + jnp.where((place >= begin) & (place < end), 0.0, NEGATIVE)
        s_ref[pl.ds(start, size), columns] = s
        top = jnp.maximum(top, jnp.max(s.reshape(size // 8, 8, s.shape[1]), axis=0))
    return top


def weigh_piece(v_ref, s_ref, w_ref, columns, top, total, acc):
    for start, size in cuts(v_ref.shape[0], 512):
        w = jnp.exp2(s_ref[pl.ds(start, size), columns] - top)
        total = total + fold(w)
        w_ref[pl.ds(start, size), columns] = w.astype(BF16)
    part = dot(w_ref[:, columns], v_ref[...], TN)
    return total, part if acc is None else acc + part


def attend_kernel(parts, fresh, count, scale, flow, info_ref, gl_ref, wq_ref, *refs):
    new, refs = refs[: 3 * bool(fresh) + fresh], refs[3 * bool(fresh) + fresh :]
    lat_refs, refs = refs[:parts], refs[parts:]
    given = count - fresh
    k_refs, v_refs, refs = refs[:given], refs[given : 2 * given], refs[2 * given :]
    q_ref, acc_ref, top_ref, tot_ref, lat_ref = refs[:5]
    refs = refs[5:]
    k_refs, v_refs, refs = refs[:fresh] + k_refs, refs[fresh : 2 * fresh] + v_refs, refs[2 * fresh :]
    w_refs, s_refs = refs[:count], refs[count:]
    flow.need(*lat_refs, gl_ref, wq_ref)
    join(lat_refs, lat_ref)
    for j in range(fresh):
        kv_kernel(flow, new[3 + j], *new[:3], k_refs[j], v_refs[j])
    for start, size in cuts(lat_ref.shape[0], 512):
        rows = columns = pl.ds(start, size)
        unit, _ = norm_parts(lat_ref[rows, :].astype(F32))
        query = dot((unit * gl_ref[...]).astype(BF16), wq_ref[...]).astype(BF16)
        q_ref[rows, :] = query
        flow.need(*k_refs)
        top = jnp.full((8, size), NEGATIVE, F32)
        for p in range(count):
            top = score_piece(info_ref, p, k_refs[p], s_refs[p], query, columns, top, scale)
        top = jnp.max(top, axis=0, keepdims=True)
        total, acc = jnp.zeros((8, size), F32), None
        flow.need(*v_refs)
        for p in range(count):
            total, acc = weigh_piece(v_refs[p], s_refs[p], w_refs[p], columns, top, total, acc)
        acc_ref[rows, :] = acc
        if start == 0:
            flow.emit(lat_ref)
        for p in range(count):
            flow.emit(w_refs[p], slice(None), columns)
        flow.emit(acc_ref, rows)
        top_ref[:, columns] = jnp.broadcast_to(top, (8, size))
        tot_ref[:, columns] = total


def attend(info, lats, gl, wq, fresh, gt, wk, wv, keys, values, scale):
    rows, width = len(lats) * lats[0].shape[0], lats[0].shape[1]
    made = [(t.shape, BF16) for t in fresh]
    pieces = [t.shape[0] for t in (*fresh, *keys)]
    outs = [((rows, width), BF16), ((rows, width), F32), ((8, rows), F32), ((8, rows), F32), ((rows, width), BF16)]
    outs += made * 2 + [((n, rows), BF16) for n in pieces]
    new = (gt, wk, wv, *fresh) if fresh else ()
    q, acc, top, total, lat, *rest = hbm_call(
        functools.partial(attend_kernel, len(lats), len(fresh), len(pieces), scale),
        "attend",
        outs,
        (info, gl, wq, *new, *lats, *keys, *values),
        12,
        [((n, rows), F32) for n in pieces],
        smem=1,
        stores=len(outs) + (len(cuts(rows, 512)) - 1) * (len(pieces) + 1),
    )
    more = len(fresh)
    return q, acc, top, total, lat, rest[2 * more :], (*rest[:more], *keys), (*rest[more : 2 * more], *values)


def finish_kernel(
    scale, flow, info_ref, tok_ref, gt_ref, wk_ref, wv_ref, top_ref, q_ref, tot_ref, acc_ref, lat_ref, gm_ref, wo_ref, wu_ref, wd_ref,
    k_ref, v_ref, w_ref, factor_ref, mixed_ref, mlp_ref, state_ref, inner_ref, slope_ref, *refs,
):
    *out_refs, s_ref = refs
    kv_kernel(flow, tok_ref, gt_ref, wk_ref, wv_ref, k_ref, v_ref)
    flow.need(top_ref, q_ref, tot_ref, acc_ref)
    hidden = wu_ref.shape[1]
    for start, size in cuts(lat_ref.shape[0], 512):
        rows = columns = pl.ds(start, size)
        old = top_ref[:1, columns]
        top = jnp.broadcast_to(old, (8, size))
        top = score_piece(info_ref, 0, k_ref, s_ref, q_ref[rows, :], columns, top, scale)
        top = jnp.max(top, axis=0, keepdims=True)
        total, acc = weigh_piece(v_ref, s_ref, w_ref, columns, top, jnp.zeros((8, size), F32), None)
        shrink = jnp.exp2(old - top)
        total = jnp.sum(total, axis=0, keepdims=True) + jnp.sum(tot_ref[:, columns], axis=0, keepdims=True) * shrink
        inverse = 1.0 / total
        late, early = column_of(inverse), column_of(shrink * inverse)
        lane = lax.broadcasted_iota(jnp.int32, (size, 128), 1)
        factor_ref[rows, :] = jnp.where(lane == 0, late, early)
        mixed_ref[rows, :] = (acc * late + acc_ref[rows, :] * early).astype(BF16)
    for ref in (w_ref, factor_ref, mixed_ref):
        flow.emit(ref)
    flow.need(lat_ref, wo_ref, gm_ref, wu_ref, wd_ref)
    for start, size in cuts(lat_ref.shape[0], 256):
        rows = pl.ds(start, size)
        state = lat_ref[rows, :].astype(F32) + dot(mixed_ref[rows, :], wo_ref[...])
        state_ref[rows, :] = state
        unit, _ = norm_parts(state)
        low = (unit * gm_ref[...]).astype(BF16)
        mlp_ref[rows, :] = low
        out = state
        for first, step in cuts(hidden, 512):
            some = pl.ds(first, step)
            u = dot(low, wu_ref[:, some])
            square = u * u
            t = jnp.tanh(u * (GELU_C + (GELU_C * GELU_A) * square))
            half = 0.5 + 0.5 * t
            inner = (u * half).astype(BF16)
            bend = u * ((0.5 * GELU_C) + (1.5 * GELU_C * GELU_A) * square)
            inner_ref[rows, some] = inner
            slope_ref[rows, some] = (half + bend * (1.0 - t * t)).astype(BF16)
            out = out + dot(inner, wd_ref[some, :])
        part_store(out_refs, start, out.astype(BF16))
        for ref in (state_ref, mlp_ref, inner_ref, slope_ref):
            flow.emit(ref, rows)


def finish(info, parts, lat, q, acc, top, total, tail, gt, wk, wv, gm, wo, wu, wd, scale):
    rows, width = lat.shape
    hidden = wu.shape[1]
    tall = (rows, width)
    outs = [(tail.shape, BF16)] * 2 + [((tail.shape[0], rows), BF16), ((rows, 128), F32), (tall, BF16), (tall, BF16), (tall, F32)]
    outs += [((rows, hidden), BF16)] * 2 + [((rows // parts, width), BF16)] * parts
    out = hbm_call(
        functools.partial(finish_kernel, scale),
        "finish",
        outs,
        (info, tail, gt, wk, wv, top, q, total, acc, lat, gm, wo, wu, wd),
        22,
        [((tail.shape[0], rows), F32)],
        smem=1,
        stores=len(outs) + 4 * (len(cuts(rows, 256)) - 1),
    )
    return out[:9], out[9:]


def mlp_back_kernel(
    parts, flow, info_ref, *refs,
):
    cot_refs, refs = refs[:parts], refs[parts:]
    wd_ref, slope_ref, wu_ref, state_ref, mixed_ref, factor_ref, gm_ref, wo_ref, inner_ref, mlp_ref, *refs = refs
    dstate_ref, late_ref, early_ref, dlate_ref, dearly_ref, keep_ref, send_ref, dwo_ref, dgain_ref = refs[:9]
    dpre_ref, dproj_ref, cot_ref = refs[9:]
    flow.need(*cot_refs, wd_ref, slope_ref)
    join(cot_refs, cot_ref)
    hidden, width = wd_ref.shape

    def pack(half, first, value):
        rows = pl.ds(first, value.shape[0])

        @pl.when(info_ref[0] == half)
        def _():
            keep_ref[rows, :] = value.astype(BF16)

        @pl.when(info_ref[0] != half)
        def _():
            send_ref[rows, :] = value.astype(BF16)

    total = jnp.zeros((8, width), F32)
    for start, size in cuts(cot_ref.shape[0], 256):
        rows = pl.ds(start, size)
        cot = cot_ref[rows, :]
        d_mlp = None
        for first, step in cuts(hidden, 512):
            some = pl.ds(first, step)
            d_inner = dot(cot, wd_ref[some, :], NT)
            d_pre = (slope_ref[rows, some].astype(F32) * d_inner).astype(BF16)
            dpre_ref[rows, some] = d_pre
            flow.need(wu_ref)
            part = dot(d_pre, wu_ref[:, some], NT)
            d_mlp = part if d_mlp is None else d_mlp + part
        flow.need(gm_ref, wo_ref, state_ref, mixed_ref, factor_ref)
        unit, inverse = norm_parts(state_ref[rows, :])
        total = total + fold(d_mlp * unit)
        d_state = cot.astype(F32) + norm_back(d_mlp, unit, inverse, gm_ref[...])
        dstate_ref[rows, :] = d_state
        d_proj = d_state.astype(BF16)
        dproj_ref[rows, :] = d_proj
        d_att = dot(d_proj, wo_ref[...], NT)
        mixed = mixed_ref[rows, :].astype(F32)
        for lane, part_ref, delta_ref in ((0, late_ref, dlate_ref), (1, early_ref, dearly_ref)):
            part = (d_att * factor_ref[rows, lane : lane + 1]).astype(BF16)
            part_ref[rows, :] = part
            delta = jnp.sum(part.astype(F32) * mixed, axis=-1, keepdims=True)
            delta_ref[:, rows] = row_of(delta)
    dgain_ref[...] = total
    for ref in (dstate_ref, late_ref, early_ref, dlate_ref, dearly_ref):
        flow.emit(ref)
    flow.need(inner_ref, mlp_ref)
    for first, step in cuts(hidden, 512):
        pack(0, first, dot(inner_ref[:, first : first + step], cot_ref[...], TN))
    for first, step in cuts(hidden, 512):
        pack(1, first, dot(mlp_ref[...], dpre_ref[:, first : first + step], TN))
    dwo_ref[...] = dot(mixed_ref[...], dproj_ref[...], TN).astype(BF16)


def mlp_back(info, cots, slope, state, mixed, mlp, inner, factor, gm, wo, wu, wd):
    rows, width = state.shape
    hidden = wu.shape[1]
    tall, flat = (rows, width), (8, rows)
    outs = [(tall, F32), (tall, BF16), (tall, BF16), (flat, F32), (flat, F32)]
    outs += [((hidden, width), BF16)] * 2 + [((width, width), BF16), ((8, width), F32)]
    return hbm_call(
        functools.partial(mlp_back_kernel, len(cots)),
        "mlp_back",
        outs,
        (info, *cots, wd, slope, wu, state, mixed, factor, gm, wo, inner, mlp),
        20,
        [((rows, hidden), BF16), (tall, BF16), (tall, BF16)],
        smem=1,
    )


def attention_back_kernel(count, start, parts, extra, scale, flow, info_ref, *refs):
    q_ref, wk_ref, wv_ref, gain_ref, *refs = refs
    datt_ref, delta_ref, *refs = refs
    v_refs, w_refs, t_refs, k_refs = (refs[j : 4 * count : 4] for j in range(4))
    refs = refs[4 * count :]
    sums, refs = refs[:start], refs[start:]
    if parts:
        lat_ref, gl_ref, wq_ref, dstate_ref, dwo_ref, dgmlp_ref, *refs = refs
    dtok_refs, refs = refs[:count], refs[count:]
    if parts:
        dlat_ref, *refs = refs
        keep_ref, send_ref, dq_ref, akey_ref, aval_ref, dgain_ref, latlow_ref, dquery_ref, *refs = refs
    else:
        dq_ref, akey_ref, aval_ref, dgain_ref, *refs = refs
    dscore_ref, low_ref, dkey_ref, dval_ref, part_ref = refs
    totals = (dq_ref, akey_ref, aval_ref, dgain_ref)
    flow.need(q_ref, wk_ref, wv_ref, gain_ref)
    for p in range(count):
        size = k_refs[p].shape[0]
        flow.need(datt_ref, delta_ref, v_refs[p], w_refs[p], t_refs[p], k_refs[p])
        begin, end, first_place = info_ref[1 + 3 * p], info_ref[2 + 3 * p], info_ref[3 + 3 * p]
        part_ref[...] = jnp.zeros_like(part_ref)
        for first, step in cuts(size, 256):
            rows = pl.ds(first, step)
            active = (first_place + first < end) & (first_place + first + step > begin)

            @pl.when(active)
            def _(p=p, rows=rows):
                d_prob = dot(v_refs[p][rows, :], datt_ref[...], NT)
                d_score = (w_refs[p][rows, :].astype(F32) * (d_prob - delta_ref[:1, :])).astype(BF16)
                dscore_ref[rows, :] = d_score
                d_key = (dot(d_score, q_ref[...]) * scale).astype(BF16)
                d_value = dot(w_refs[p][rows, :], datt_ref[...]).astype(BF16)
                dkey_ref[rows, :] = d_key
                dval_ref[rows, :] = d_value
                unit, _ = norm_parts(t_refs[p][rows, :].astype(F32))
                low_ref[rows, :] = (unit * gain_ref[...]).astype(BF16)
                d_tok = dot(d_key, wk_ref[...], NT) + dot(d_value, wv_ref[...], NT)
                dtok_refs[p][rows, :] = d_tok.astype(BF16)
                part_ref[...] += fold(d_tok * unit)

            @pl.when(jnp.logical_not(active))
            def _(p=p, rows=rows):
                for ref in (dscore_ref, dkey_ref, dval_ref, low_ref, dtok_refs[p]):
                    ref[rows, :] = jnp.zeros((rows.size, ref.shape[1]), BF16)

        flow.emit(dtok_refs[p])
        dgain = part_ref[...]
        here = pl.ds(0, size)
        news = (
            dot(dscore_ref[here, :], k_refs[p][...], TN),
            dot(low_ref[here, :], dkey_ref[here, :], TN),
            dot(low_ref[here, :], dval_ref[here, :], TN),
            dgain,
        )
        if p == 0:
            flow.need(*sums)
        for j, (ref, value) in enumerate(zip(totals, news)):
            if p == 0:
                ref[...] = value + sums[j][...] if sums else value
            else:
                ref[...] += value
    if not parts:
        return
    flow.need(lat_ref, gl_ref, wq_ref, dstate_ref, dwo_ref, dgmlp_ref)
    total = None
    width = wq_ref.shape[0]
    for first, size in cuts(lat_ref.shape[0], 256):
        rows = pl.ds(first, size)
        unit, inverse = norm_parts(lat_ref[rows, :].astype(F32))
        gain = gl_ref[...]
        latlow_ref[rows, :] = (unit * gain).astype(BF16)
        d_query = (dq_ref[rows, :] * scale).astype(BF16)
        dquery_ref[rows, :] = d_query
        d_low = dot(d_query, wq_ref[...], NT)
        line_store(dlat_ref, parts, info_ref[1 + 3 * count], first, (dstate_ref[rows, :] + norm_back(d_low, unit, inverse, gain)).astype(BF16))
        part = fold(d_low * unit)
        total = part if total is None else total + part
    flow.emit(dlat_ref)
    d_wq = dot(latlow_ref[...], dquery_ref[...], TN)
    gains = [jnp.sum(g, axis=0, keepdims=True) for g in (total, dgain_ref[...], dgmlp_ref[...])]
    line = lax.broadcasted_iota(jnp.int32, (extra, width), 0)
    block = jnp.where(line == 0, gains[0], jnp.where(line == 1, gains[1], jnp.where(line == 2, gains[2], 0.0)))
    halves = ((d_wq, akey_ref), (aval_ref, dwo_ref))
    for ref, core in ((keep_ref, info_ref[0]), (send_ref, 1 - info_ref[0])):
        ref[pl.ds(2 * width, extra), :] = block.astype(BF16)
        for h, half in enumerate(halves):

            @pl.when(core == h)
            def _(ref=ref, half=half):
                for j, piece in enumerate(half):
                    ref[pl.ds(j * width, width), :] = piece[...].astype(BF16)


def attention_back(info, q, wk, wv, gain, grads, values, weights, tokens, keys, sums, latents, parts, extra, scale):
    rows, width = q.shape
    square = ((width, width), F32)
    totals = [((rows, width), F32), square, square, ((8, width), F32)]
    most = max(k.shape[0] for k in keys)
    work = [((most, rows), BF16)] + [((most, width), BF16)] * 3 + [((8, width), F32)]
    outs = [(k.shape, BF16) for k in keys]
    by_piece = [a for piece in zip(values, weights, tokens, keys) for a in piece]
    args = (info, q, wk, wv, gain, *grads, *by_piece, *sums)
    if latents:
        args = (*args, *latents)
        outs += [((rows, width), BF16)] + [((2 * width + extra, width), BF16)] * 2
        work = totals + [((rows, width), BF16)] * 2 + work
    else:
        outs += totals
        parts = 0
    kernel = functools.partial(attention_back_kernel, len(keys), len(sums), parts, extra, scale)
    out = hbm_call(kernel, "attention_back", outs, args, 12, work, smem=1)
    return out[: len(keys)], out[len(keys) :]


def token_back_kernel(count, flow, tok_ref, gain_ref, *refs):
    flow.need(tok_ref, gain_ref, *refs[:count])
    for start, size in cuts(tok_ref.shape[0], 256):
        rows = pl.ds(start, size)
        unit, inverse = norm_parts(tok_ref[rows, :].astype(F32))
        total = refs[0][rows, :].astype(F32)
        for ref in refs[1:count]:
            total = total + ref[rows, :].astype(F32)
        refs[count][rows, :] = norm_back(total, unit, inverse, gain_ref[...])
        flow.emit(refs[count], rows)


def token_back(tok, gain, parts):
    args = (tok, gain, *parts)
    [out] = hbm_call(functools.partial(token_back_kernel, len(parts)), "token_back", [(tok.shape, F32)], args, 8, stores=len(cuts(tok.shape[0], 256)))
    return out


def picks(shape, scenes, scene, transposed=False):
    along = lax.broadcasted_iota(jnp.int32, shape, 1 if transposed else 0)
    across = lax.broadcasted_iota(jnp.int32, shape, 0 if transposed else 1)
    return jnp.where(across == along * scenes + scene, 1.0, 0.0).astype(BF16)


def sort_kernel(flow, info_ref, rows_ref, *out_refs):
    flow.need(rows_ref)
    for k, ref in enumerate(out_refs):
        take = picks((ref.shape[0], rows_ref.shape[0]), len(out_refs), info_ref[0] ^ k)
        ref[...] = dot(take, rows_ref[...]).astype(BF16)
        flow.emit(ref)


def sort_rows(info, value, scenes):
    rows, width = value.shape
    return hbm_call(sort_kernel, "sort_rows", [((rows // scenes, width), BF16)] * scenes, (info, value), 16, smem=1)


def unsort_kernel(scenes, flow, info_ref, *refs):
    *in_refs, out_ref = refs
    flow.need(*in_refs)
    if len(in_refs) == 1:
        size = out_ref.shape[0] // scenes
        in_refs = [in_refs[0].at[pl.ds(k * size, size)] for k in range(scenes)]
    rows, part = out_ref.shape[0], in_refs[0].shape[0]
    step = rows // scenes
    for start in range(0, rows, step):
        total = None
        for k, ref in enumerate(in_refs):
            some = part // scenes
            first = start // scenes
            put = picks((step, some), scenes, info_ref[0] ^ k, transposed=True)
            value = dot(put, ref[pl.ds(first, some), :])
            total = value if total is None else total + value
        out_ref[pl.ds(start, step), :] = total.astype(out_ref.dtype)
        flow.emit(out_ref, pl.ds(start, step))


def unsort_rows(info, parts, scenes, dtype):
    rows, width = sum(p.shape[0] for p in parts), parts[0].shape[1]
    kernel = functools.partial(unsort_kernel, scenes)
    [out] = hbm_call(kernel, "unsort_rows", [((rows, width), dtype)], (info, *parts), 16, smem=1, stores=scenes)
    return out


def split_kernel(count, place, extra, info_ref, *refs):
    in_refs, out_refs = refs[:count], refs[count:]
    rest = None
    if extra and out_refs[-1].shape[0] == extra and len(out_refs) == 2:
        *out_refs, rest = out_refs
    body = in_refs[0].shape[0] - extra
    step = body // len(out_refs)

    def total(start, rows):
        value = in_refs[0][pl.ds(start, rows), :].astype(F32)
        for ref in in_refs[1:]:
            value = value + ref[pl.ds(start, rows), :].astype(F32)
        return value.astype(BF16)

    shared = total(body, extra) if extra else None
    for k, ref in enumerate(out_refs):
        start = (info_ref[place] ^ k) * step if len(out_refs) > 1 else 0
        ref[pl.ds(0, step), :] = total(start if isinstance(start, int) else pl.multiple_of(start, 16), step)
        if extra and rest is None:
            ref[pl.ds(step, extra), :] = shared
    if rest is not None:
        rest[...] = shared


def split_sum(info, arrays, parts, place, extra):
    rows, width = arrays[0].shape
    step = (rows - extra) // parts
    if parts > 1:
        outs = [((step + extra, width), BF16)] * parts
    else:
        outs = [((step, width), BF16)] + ([((extra, width), BF16)] if extra else [])
    kernel = functools.partial(split_kernel, len(arrays), place, extra)
    return vmem_call(kernel, "split_sum", outs, (info, *arrays), 8, smem=1)


def unpack_kernel(width, count, crossed, info_ref, *refs):
    core, quad, line = info_ref[0], info_ref[1], info_ref[2]
    out_refs, (mine_ref, other_ref) = refs[2 * count : -2], refs[-2:]
    join(refs[:count], mine_ref)
    join(refs[count : 2 * count], other_ref)
    half = mine_ref.shape[0]
    lines = info_ref.shape[0] - 3
    block = half // (4 * lines)
    for h in range(2):
        for m in range(4):
            for z in range(lines):
                chip, spot = quad ^ m, line ^ z
                if crossed:
                    late = spot // (lines // 2)
                    chip = jnp.where(late == 0, chip, (chip % 2) * 2 + chip // 2)
                    spot = (late * 4 + chip) * (lines // 2) + spot % (lines // 2)
                else:
                    spot = chip * lines + spot
                rows = pl.ds(pl.multiple_of(spot * block, 16), block)
                value = jnp.where(core == h, mine_ref[rows, :].astype(F32), other_ref[rows, :].astype(F32))
                at = h * half + (m * lines + z) * block
                total = 0
                for ref in out_refs:
                    tall = ref.shape[0] * (ref.shape[1] // width)
                    if total <= at < total + tall:
                        inside = at - total
                        slab, row = inside // ref.shape[0], inside % ref.shape[0]
                        ref[pl.ds(row, block), pl.ds(slab * width, width)] = value
                    total += tall


class Sums:
    def __init__(self, seqs, blocks):
        self.seqs, self.blocks = seqs, blocks
        self.lines = blocks // 2
        seq, blk = lax.axis_index("seq"), lax.axis_index("blk")
        places = [seq % 2, (seq // 2) * 2 + blk % 2, blk // 2] + [seq * 0] * self.lines
        self.info = jnp.stack(places).astype(jnp.int32)

    def flip(self, value, seq_mask, blk_mask):
        pairs = [
            (s * self.blocks + b, (s ^ seq_mask) * self.blocks + (b ^ blk_mask))
            for s in range(self.seqs)
            for b in range(self.blocks)
        ]
        return lax.ppermute(value, ("seq", "blk"), pairs)

    def to_core(self, value):
        return self.flip(value, 1, 0)

    def to_quad(self, values):
        return [self.flip(v, 2 * (k // 2), k % 2) for k, v in enumerate(values, 1)]

    def to_line(self, values):
        return [self.flip(v, 0, 2 * k) for k, v in enumerate(values, 1)]

    def add_core(self, keep, received, extra=0):
        return split_sum(self.info, [keep, received], 4, 1, extra)

    def add_quad(self, keep, received, extra=0):
        return split_sum(self.info, [keep, *received], self.lines, 2, extra)

    def add_line(self, keep, received, extra=0):
        return split_sum(self.info, [keep, *received], 1, 0, extra)

    def unpack(self, mine, other, shapes, crossed=False):
        outs = [(shape, F32) for shape in shapes]
        rows, width = mine[0].shape
        kernel = functools.partial(unpack_kernel, width, len(mine), crossed)
        work = [((rows * len(mine), width), BF16)] * 2
        return vmem_call(kernel, "unpack", outs, (self.info, *mine, *other), 16, work, smem=1)


def after(value, *others):
    return lax.optimization_barrier((value, others))[0]


def local(
    sizes, latents, tokens, lengths, gain_lat, gain_tok, gain_mlp, w_query, w_key, w_value, w_out, w_up, w_down, d_out
):
    lat, tok, cot = latents[0], tokens[0], d_out[0]
    scene_lengths = lengths[0]
    scenes = scene_lengths.shape[0]
    seqs, blocks = sizes["seq"], sizes["blk"]
    group = blocks // scenes
    span, width = tok.shape
    hidden = w_up.shape[1]
    scale = width ** (-0.5)
    position = lax.axis_index("blk")
    scene, member = position // group, position % group
    scene_info = scene.astype(jnp.int32).reshape(1)
    gl, gt, gm = (g.reshape(1, width) for g in (gain_lat, gain_tok, gain_mlp))
    lines = [[m + group * k for k in range(scenes)] for m in range(group)]
    sums = Sums(seqs, blocks)

    def exchange(value, mask):
        return sums.flip(value, 0, mask)

    def across(values):
        return [exchange(v, group * k) if k else v for k, v in enumerate(values)]

    order = jnp.arange(scenes, dtype=jnp.int32)
    begin = jnp.sum(jnp.where(order < scene, scene_lengths, 0))
    end = begin + jnp.sum(jnp.where(order == scene, scene_lengths, 0))
    base = scene * group * span
    tail_rows = (scenes - 1) * group * span // 8
    starts = [base + (member ^ k) * span for k in [*range(1, group), 0]]
    main_info = jnp.stack([begin, end, *starts]).astype(jnp.int32)
    tail_info = jnp.stack([begin, end, base - tail_rows]).astype(jnp.int32)
    calls, size = [[0], []], 0
    for j in range(1, group + 1):
        if calls[-1] and size + span > 3 * span:
            calls.append([])
            size = 0
        calls[-1].append(j)
        size += span
    core = lax.axis_index("seq") % 2
    places = []
    for call in calls:
        spots = [v for j in call for v in (begin, end, (base - tail_rows, *starts)[j])]
        places.append(jnp.stack([core, *spots, scene]).astype(jnp.int32))

    lat_parts = sort_rows(scene_info, lat, scenes)
    others = [exchange(tok, k) for k in range(1, group)]
    lat_in = across(lat_parts)
    cot_parts = sort_rows(scene_info, after(cot, lat_parts), scenes)
    own_kv = keys_values(after(tok, cot_parts), gt, w_key, w_value)
    lat_in, others, cot_parts, own_kv, main_info, tail_info, places = lax.optimization_barrier(
        (lat_in, others, cot_parts, own_kv, main_info, tail_info, places)
    )
    cot_near = exchange(cot_parts[1], group)

    pieces = [tok, *others]
    lowest = (group * span - tail_rows) // span
    needed = []
    for owner in range(lowest, group):
        block = pieces[owner]
        for m in range(1, group):
            block = jnp.where(member == m, pieces[owner ^ m], block)
        needed.append(block)
    needed = jnp.concatenate(needed, axis=0) if len(needed) > 1 else needed[0]
    pairs = [(i, i + group) for i in range(blocks - group)]
    sent = needed[needed.shape[0] - tail_rows :]
    tail = lax.ppermute(sent, "blk", pairs)
    fresh = list(others) if group == 2 else []
    given = [own_kv] if fresh else [keys_values(piece, gt, w_key, w_value) for piece in others] + [own_kv]
    made_keys, made_values = zip(*given)
    query, acc, top, total, lat_set, weights, keys, values = attend(
        main_info, lat_in, gl, w_query, after(fresh, sent), gt, w_key, w_value, made_keys, made_values, scale
    )
    tail, query, cot_parts, cot_near = lax.optimization_barrier((tail, query, cot_parts, cot_near))

    cot_in = [cot_parts[0], cot_near, *[exchange(cot_parts[k], group * k) for k in range(2, scenes)]]
    saved, out_parts = finish(
        tail_info, scenes, lat_set, query, acc, top, total, tail, gt, w_key, w_value, gm, w_out, w_up, w_down, scale
    )
    tail_key, tail_value, tail_weight, factor, mixed, mlp, state, inner, slope = saved
    cot_in, out_parts, slope = lax.optimization_barrier((cot_in, out_parts, slope))
    out_back = across(out_parts)
    d_state, d_late, d_early, late, early_delta, keep, send, d_wo, dg_mlp = mlp_back(
        sums.info, cot_in, slope, state, mixed, mlp, inner, factor, gm, w_out, w_up, w_down
    )

    out_back, keep, send, d_early, d_late = lax.optimization_barrier((out_back, keep, send, d_early, d_late))
    received = sums.to_core(send)
    pieces = [(tail_value, tail_weight, tail, tail_key)]
    pieces += [(values[j], weights[j], piece, keys[j]) for j, piece in enumerate((*others, tok))]
    extra = 16
    d_toks, kept = [], []
    for j, call in enumerate(calls):
        some_values, some_weights, some_tokens, some_keys = zip(*[pieces[p] for p in call])
        latents = (lat_set, gl, w_query, d_state, d_wo, dg_mlp) if j == len(calls) - 1 else ()
        grads = (d_early, early_delta) if j else (d_late, late)
        some, kept = attention_back(
            places[j], query, w_key, w_value, gt, grads, some_values, some_weights, some_tokens, some_keys, kept,
            latents, scenes, extra, scale,
        )
        d_toks += some
        if j == 0:
            received, d_toks, kept = lax.optimization_barrier((received, d_toks, kept))
            keep, *sends = sums.add_core(keep, received)
            d_early = after(d_early, keep)
            received = sums.to_quad(sends)
            d_tail = lax.ppermute(d_toks[0], "blk", [(j, i) for i, j in pairs])
    received, d_tail, d_toks, kept = lax.optimization_barrier((received, d_tail, d_toks, kept))
    _, *returned, own = d_toks
    d_lat_set, small_keep, small_send = kept

    returned = dict(enumerate(returned, 1))
    own_tail = []
    for owner in range(lowest, group):
        start = owner * span - (group * span - tail_rows)
        chunk = d_tail[max(start, 0) : start + span]
        chunk = jnp.pad(chunk, ((span - chunk.shape[0], 0), (0, 0)))
        for k in range(1, group):
            returned[k] = returned[k] + jnp.where(member == owner ^ k, chunk, 0)
        own_tail.append(jnp.where(member == owner, chunk, 0))
    small_got = sums.to_core(small_send)
    keep, *sends = sums.add_quad(keep, received)
    received = sums.to_line(sends)
    returned = [exchange(after(returned[k], keep), k) for k in range(1, group)]
    output = unsort_rows(scene_info, after(out_back, keep), scenes, BF16)
    small_got, received, output = lax.optimization_barrier((small_got, received, output))
    [shard] = sums.add_line(keep, received)
    small_keep, *small_sends = sums.add_core(small_keep, small_got, extra)
    small_got = sums.to_quad(small_sends)
    block = shard
    for j in range(sums.lines.bit_length() - 1):
        far = sums.flip(block, 0, 2 << j)
        if j == sums.lines.bit_length() - 2:
            small_got, far = lax.optimization_barrier((small_got, far))
        block = jnp.concatenate([block, far], axis=0)
    half = block.shape[0] // 2
    near_a, near_b = block[:half], block[half:]
    far_a, far_b = sums.flip(near_a, 0, 1), sums.flip(near_b, 2, 0)
    small_keep, *small_sends = sums.add_quad(small_keep, small_got, extra)
    small_got = sums.to_line(small_sends)
    small_got, far_a, far_b, returned = lax.optimization_barrier((small_got, far_a, far_b, returned))
    two_a, two_b = jnp.concatenate([near_a, far_a], axis=0), jnp.concatenate([near_b, far_b], axis=0)
    last_a, last_b = sums.flip(two_a, 2, 0), sums.flip(two_b, 0, 1)
    small_shard, gains = sums.add_line(small_keep, small_got, extra)
    small_block = small_shard
    for j in range(sums.lines.bit_length() - 1):
        far = sums.flip(small_block, 0, 2 << j)
        if j == sums.lines.bit_length() - 2:
            leaving = after(d_lat_set, small_block)
            d_lat_back = lax.all_to_all(leaving, "blk", 0, 0, axis_index_groups=lines, tiled=True)
            d_tokens = token_back(tok, gt, [own, *own_tail, *after(returned, small_block)])
            far = after(far, d_tokens)
        small_block = jnp.concatenate([small_block, far], axis=0)
    last_a, last_b, small_block = lax.optimization_barrier((last_a, last_b, small_block))
    small_got = sums.to_quad([small_block] * 3)
    mine = [two_a, last_a, two_b, last_b]
    other = [sums.to_core(v) for v in mine]
    d_w_down, d_w_up = sums.unpack(mine, other, [(hidden, width), (width, hidden)], crossed=True)
    small_got, d_lat_back, d_w_up = lax.optimization_barrier((small_got, d_lat_back, d_w_up))
    small_mine = [small_block, *small_got]
    small_other = [sums.to_core(v) for v in small_mine]
    d_latents = unsort_rows(0 * scene_info, [after(d_lat_back, small_mine)], scenes, F32)
    squares = sums.unpack(small_mine, after(small_other, d_latents), [(width, width)] * 4)
    gains = gains.astype(F32)
    return (output[None], d_latents[None], d_tokens[None], *squares, d_w_up, d_w_down, gains[0], gains[1], gains[2])


def solution(mesh):
    split = P("seq", "blk", None)
    in_specs = (split, split, P("seq", None)) + (P(),) * 9 + (split,)
    out_specs = (split,) * 3 + (P(),) * 9
    return jax.shard_map(
        functools.partial(local, dict(mesh.shape)), mesh=mesh, in_specs=in_specs, out_specs=out_specs, check_vma=False
    )
```

```python
import functools
import math

import jax
import jax.numpy as jnp
from jax import lax
from jax.experimental import pallas as pl
from jax.experimental.pallas import tpu as pltpu
from jax.sharding import PartitionSpec as P

EPSILON = 1e-05
NEGATIVE = -1e30
ROOM = (64 << 20) - (160 << 10)
LOG2E = 1.4426950408889634
GELU_C = math.sqrt(2.0 / math.pi)
GELU_A = 0.044715
F32 = jnp.float32
BF16 = jnp.bfloat16
NN = (((1,), (0,)), ((), ()))
NT = (((1,), (1,)), ((), ()))
TN = (((0,), (0,)), ((), ()))


def dot(left, right, dims=NN):
    return lax.dot_general(left, right, dims, preferred_element_type=F32)


def norm_parts(rows):
    center = rows - jnp.mean(rows, axis=-1, keepdims=True)
    spread = jnp.mean(center * center, axis=-1, keepdims=True)
    inverse = lax.rsqrt(spread + EPSILON)
    return center * inverse, inverse


def norm_back(d_normed, unit, inverse, gain):
    d_unit = d_normed * gain
    mean_d = jnp.mean(d_unit, axis=-1, keepdims=True)
    mean_p = jnp.mean(d_unit * unit, axis=-1, keepdims=True)
    return inverse * (d_unit - mean_d - unit * mean_p)


def vmem_call(kernel, name, outs, args, limit, scratch=(), smem=0):
    held = sum(math.prod(shape) * jnp.dtype(dtype).itemsize for shape, dtype in scratch)
    in_vmem = pl.BlockSpec(memory_space=pltpu.VMEM)
    in_smem = pl.BlockSpec(memory_space=pltpu.SMEM)
    return pl.pallas_call(
        kernel,
        in_specs=[in_smem] * smem + [in_vmem] * (len(args) - smem),
        out_specs=[in_vmem] * len(outs),
        out_shape=[jax.ShapeDtypeStruct(shape, dtype) for shape, dtype in outs],
        scratch_shapes=[pltpu.VMEM(shape, dtype) for shape, dtype in scratch],
        compiler_params=pltpu.CompilerParams(vmem_limit_bytes=(limit << 20) + held),
        cost_estimate=pl.CostEstimate(flops=0, bytes_accessed=0, transcendentals=0),
        name=name,
    )(*args)


class Flow:
    AHEAD = 64 << 20

    def __init__(self, loads, stores, semaphores):
        self.loads = loads
        self.stores = stores
        self.semaphores = semaphores
        self.started = 0
        self.waiting = set(range(len(loads)))
        self.begun = []
        self.whole = set()
        self.start_more(-1)

    def start_more(self, least):
        def size(j):
            held = self.loads[j][1]
            return math.prod(held.shape) * jnp.dtype(held.dtype).itemsize

        flying = sum(size(j) for j in self.waiting if j < self.started)
        while self.started < len(self.loads) and (self.started <= least or flying + size(self.started) <= self.AHEAD):
            flying += size(self.started)
            self.loads[self.started][2].start()
            self.started += 1

    def need(self, *refs):
        wanted = [j for j, load in enumerate(self.loads) if j in self.waiting and any(load[1] is r for r in refs)]
        for j in wanted:
            self.start_more(j)
        for j in wanted:
            self.waiting.discard(j)
            self.loads[j][2].wait()
        self.start_more(-1)

    def emit(self, ref, *where):
        for j, (out, held) in enumerate(self.stores):
            if held is ref:
                self.whole.add(j)
                source, target = (held.at[where], out.at[where]) if where else (held, out)
                copy = pltpu.make_async_copy(source, target, self.semaphores.at[len(self.begun)])
                copy.start()
                self.begun.append(copy)

    def close(self):
        self.need(*[held for _, held, _ in self.loads])
        for j, (_, held) in enumerate(self.stores):
            if j not in self.whole:
                self.emit(held)
        for copy in self.begun:
            copy.wait()


def hbm_call(kernel, name, outs, args, limit, scratch=(), smem=0, fixed_in=(), fixed_out=(), stores=None):
    arrays = args[smem:]
    moves_in = [j for j in range(len(arrays)) if j not in fixed_in]
    moves_out = [j for j in range(len(outs)) if j not in fixed_out]
    held = [(arrays[j].shape, arrays[j].dtype) for j in moves_in] + [outs[j] for j in moves_out] + list(scratch)
    size = sum(math.prod(shape) * jnp.dtype(dtype).itemsize for shape, dtype in held)

    resident = [(arrays[j].shape, arrays[j].dtype) for j in fixed_in] + [outs[j] for j in fixed_out]
    rest = sum(math.prod(shape) * jnp.dtype(dtype).itemsize for shape, dtype in resident)
    limit = max((limit << 20) + size, ROOM - rest)

    def body(*refs):
        scalars, refs = refs[:smem], refs[smem:]
        ins, refs = list(refs[: len(arrays)]), refs[len(arrays) :]
        results, refs = list(refs[: len(outs)]), refs[len(outs) :]
        *kept, load_sems, store_sems = refs
        loads, kept_out = [], []
        for n, j in enumerate(moves_in):
            loads.append((ins[j], kept[n], pltpu.make_async_copy(ins[j], kept[n], load_sems.at[n])))
            ins[j] = kept[n]
        kept = kept[len(moves_in) :]
        for n, j in enumerate(moves_out):
            kept_out.append((results[j], kept[n]))
            results[j] = kept[n]
        flow = Flow(loads, kept_out, store_sems)
        kernel(flow, *scalars, *ins, *results, *kept[len(moves_out) :])
        flow.close()

    def place(count, fixed):
        return [pl.BlockSpec(memory_space=pltpu.VMEM if j in fixed else pl.ANY) for j in range(count)]

    return pl.pallas_call(
        body,
        in_specs=[pl.BlockSpec(memory_space=pltpu.SMEM)] * smem + place(len(arrays), fixed_in),
        out_specs=place(len(outs), fixed_out),
        out_shape=[jax.ShapeDtypeStruct(shape, dtype) for shape, dtype in outs],
        scratch_shapes=[pltpu.VMEM(shape, dtype) for shape, dtype in held]
        + [pltpu.SemaphoreType.DMA((max(len(moves_in), 1),)), pltpu.SemaphoreType.DMA((max(stores or len(moves_out), 1),))],
        compiler_params=pltpu.CompilerParams(vmem_limit_bytes=min(limit, ROOM)),
        cost_estimate=pl.CostEstimate(flops=0, bytes_accessed=0, transcendentals=0),
        name=name,
    )(*args)


def cuts(size, step):
    return [(i, min(step, size - i)) for i in range(0, size, step)]


def fold(rows):
    return jnp.sum(rows.reshape(rows.shape[0] // 8, 8, rows.shape[1]), axis=0)


def column_of(row):
    return jnp.transpose(jnp.broadcast_to(row, (8, row.shape[1])))[:, :1]


def row_of(column):
    return jnp.transpose(jnp.broadcast_to(column, (column.shape[0], 128)))[:8, :]


def join(refs, whole_ref):
    part = refs[0].shape[0]
    for j, ref in enumerate(refs):
        whole_ref[pl.ds(j * part, part), :] = ref[...]


def line_store(ref, scenes, scene, start, value):
    part = ref.shape[0] // scenes
    size = min(part, value.shape[0])
    for first in range(0, value.shape[0], size):
        at = start + first
        place = (scene ^ (at // part)) * part + at % part
        ref[pl.ds(pl.multiple_of(place, 16), size), :] = value[first : first + size]


def part_store(refs, start, value):
    part = refs[0].shape[0]
    size = min(part, value.shape[0])
    for first in range(0, value.shape[0], size):
        at = start + first
        refs[at // part][pl.ds(at % part, size), :] = value[first : first + size]


def kv_kernel(flow, tok_ref, gain_ref, wk_ref, wv_ref, k_ref, v_ref):
    flow.need(tok_ref, gain_ref, wk_ref, wv_ref)
    for start, size in cuts(tok_ref.shape[0], 256):
        rows = pl.ds(start, size)
        unit, _ = norm_parts(tok_ref[rows, :].astype(F32))
        low = (unit * gain_ref[...]).astype(BF16)
        k_ref[rows, :] = dot(low, wk_ref[...]).astype(BF16)
        v_ref[rows, :] = dot(low, wv_ref[...]).astype(BF16)
    flow.emit(k_ref)
    flow.emit(v_ref)


def keys_values(tok, gain, w_key, w_value):
    return hbm_call(kv_kernel, "keys_values", [(tok.shape, BF16)] * 2, (tok, gain, w_key, w_value), 8)


def score_piece(info_ref, p, k_ref, s_ref, query, columns, top, scale):
    begin, end = info_ref[0], info_ref[1]
    for start, size in cuts(k_ref.shape[0], 512):
        s = dot(k_ref[pl.ds(start, size), :], query, NT) * (scale * LOG2E)
        place = info_ref[2 + p] + start + lax.broadcasted_iota(jnp.int32, (size, 1), 0)
        s = s + jnp.where((place >= begin) & (place < end), 0.0, NEGATIVE)
        s_ref[pl.ds(start, size), columns] = s
        top = jnp.maximum(top, jnp.max(s.reshape(size // 8, 8, s.shape[1]), axis=0))
    return top


def weigh_piece(v_ref, s_ref, w_ref, columns, top, total, acc):
    for start, size in cuts(v_ref.shape[0], 512):
        w = jnp.exp2(s_ref[pl.ds(start, size), columns] - top)
        total = total + fold(w)
        w_ref[pl.ds(start, size), columns] = w.astype(BF16)
    part = dot(w_ref[:, columns], v_ref[...], TN)
    return total, part if acc is None else acc + part


def attend_kernel(parts, fresh, count, scale, flow, info_ref, gl_ref, wq_ref, *refs):
    new, refs = refs[: 3 * bool(fresh) + fresh], refs[3 * bool(fresh) + fresh :]
    lat_refs, refs = refs[:parts], refs[parts:]
    given = count - fresh
    k_refs, v_refs, refs = refs[:given], refs[given : 2 * given], refs[2 * given :]
    q_ref, acc_ref, top_ref, tot_ref, lat_ref = refs[:5]
    refs = refs[5:]
    k_refs, v_refs, refs = refs[:fresh] + k_refs, refs[fresh : 2 * fresh] + v_refs, refs[2 * fresh :]
    w_refs, s_refs = refs[:count], refs[count:]
    flow.need(*lat_refs, gl_ref, wq_ref)
    join(lat_refs, lat_ref)
    for j in range(fresh):
        kv_kernel(flow, new[3 + j], *new[:3], k_refs[j], v_refs[j])
    for start, size in cuts(lat_ref.shape[0], 512):
        rows = columns = pl.ds(start, size)
        unit, _ = norm_parts(lat_ref[rows, :].astype(F32))
        query = dot((unit * gl_ref[...]).astype(BF16), wq_ref[...]).astype(BF16)
        q_ref[rows, :] = query
        flow.need(*k_refs)
        top = jnp.full((8, size), NEGATIVE, F32)
        for p in range(count):
            top = score_piece(info_ref, p, k_refs[p], s_refs[p], query, columns, top, scale)
        top = jnp.max(top, axis=0, keepdims=True)
        total, acc = jnp.zeros((8, size), F32), None
        flow.need(*v_refs)
        for p in range(count):
            total, acc = weigh_piece(v_refs[p], s_refs[p], w_refs[p], columns, top, total, acc)
        acc_ref[rows, :] = acc
        if start == 0:
            flow.emit(lat_ref)
        for p in range(count):
            flow.emit(w_refs[p], slice(None), columns)
        flow.emit(acc_ref, rows)
        top_ref[:, columns] = jnp.broadcast_to(top, (8, size))
        tot_ref[:, columns] = total


def attend(info, lats, gl, wq, fresh, gt, wk, wv, keys, values, scale):
    rows, width = len(lats) * lats[0].shape[0], lats[0].shape[1]
    made = [(t.shape, BF16) for t in fresh]
    pieces = [t.shape[0] for t in (*fresh, *keys)]
    outs = [((rows, width), BF16), ((rows, width), F32), ((8, rows), F32), ((8, rows), F32), ((rows, width), BF16)]
    outs += made * 2 + [((n, rows), BF16) for n in pieces]
    new = (gt, wk, wv, *fresh) if fresh else ()
    q, acc, top, total, lat, *rest = hbm_call(
        functools.partial(attend_kernel, len(lats), len(fresh), len(pieces), scale),
        "attend",
        outs,
        (info, gl, wq, *new, *lats, *keys, *values),
        12,
        [((n, rows), F32) for n in pieces],
        smem=1,
        stores=len(outs) + (len(cuts(rows, 512)) - 1) * (len(pieces) + 1),
    )
    more = len(fresh)
    return q, acc, top, total, lat, rest[2 * more :], (*rest[:more], *keys), (*rest[more : 2 * more], *values)


def finish_kernel(
    scale, flow, info_ref, tok_ref, gt_ref, wk_ref, wv_ref, top_ref, q_ref, tot_ref, acc_ref, lat_ref, gm_ref, wo_ref, wu_ref, wd_ref,
    k_ref, v_ref, w_ref, factor_ref, mixed_ref, mlp_ref, state_ref, inner_ref, slope_ref, *refs,
):
    *out_refs, s_ref = refs
    kv_kernel(flow, tok_ref, gt_ref, wk_ref, wv_ref, k_ref, v_ref)
    flow.need(top_ref, q_ref, tot_ref, acc_ref)
    hidden = wu_ref.shape[1]
    for start, size in cuts(lat_ref.shape[0], 512):
        rows = columns = pl.ds(start, size)
        old = top_ref[:1, columns]
        top = jnp.broadcast_to(old, (8, size))
        top = score_piece(info_ref, 0, k_ref, s_ref, q_ref[rows, :], columns, top, scale)
        top = jnp.max(top, axis=0, keepdims=True)
        total, acc = weigh_piece(v_ref, s_ref, w_ref, columns, top, jnp.zeros((8, size), F32), None)
        shrink = jnp.exp2(old - top)
        total = jnp.sum(total, axis=0, keepdims=True) + jnp.sum(tot_ref[:, columns], axis=0, keepdims=True) * shrink
        inverse = 1.0 / total
        late, early = column_of(inverse), column_of(shrink * inverse)
        lane = lax.broadcasted_iota(jnp.int32, (size, 128), 1)
        factor_ref[rows, :] = jnp.where(lane == 0, late, early)
        mixed_ref[rows, :] = (acc * late + acc_ref[rows, :] * early).astype(BF16)
    for ref in (w_ref, factor_ref, mixed_ref):
        flow.emit(ref)
    flow.need(lat_ref, wo_ref, gm_ref, wu_ref, wd_ref)
    for start, size in cuts(lat_ref.shape[0], 256):
        rows = pl.ds(start, size)
        state = lat_ref[rows, :].astype(F32) + dot(mixed_ref[rows, :], wo_ref[...])
        state_ref[rows, :] = state
        unit, _ = norm_parts(state)
        low = (unit * gm_ref[...]).astype(BF16)
        mlp_ref[rows, :] = low
        out = state
        for first, step in cuts(hidden, 512):
            some = pl.ds(first, step)
            u = dot(low, wu_ref[:, some])
            square = u * u
            t = jnp.tanh(u * (GELU_C + (GELU_C * GELU_A) * square))
            half = 0.5 + 0.5 * t
            inner = (u * half).astype(BF16)
            bend = u * ((0.5 * GELU_C) + (1.5 * GELU_C * GELU_A) * square)
            inner_ref[rows, some] = inner
            slope_ref[rows, some] = (half + bend * (1.0 - t * t)).astype(BF16)
            out = out + dot(inner, wd_ref[some, :])
        part_store(out_refs, start, out.astype(BF16))
        for ref in (state_ref, mlp_ref, inner_ref, slope_ref):
            flow.emit(ref, rows)


def finish(info, parts, lat, q, acc, top, total, tail, gt, wk, wv, gm, wo, wu, wd, scale):
    rows, width = lat.shape
    hidden = wu.shape[1]
    tall = (rows, width)
    outs = [(tail.shape, BF16)] * 2 + [((tail.shape[0], rows), BF16), ((rows, 128), F32), (tall, BF16), (tall, BF16), (tall, F32)]
    outs += [((rows, hidden), BF16)] * 2 + [((rows // parts, width), BF16)] * parts
    out = hbm_call(
        functools.partial(finish_kernel, scale),
        "finish",
        outs,
        (info, tail, gt, wk, wv, top, q, total, acc, lat, gm, wo, wu, wd),
        22,
        [((tail.shape[0], rows), F32)],
        smem=1,
        stores=len(outs) + 4 * (len(cuts(rows, 256)) - 1),
    )
    return out[:9], out[9:]


def mlp_back_kernel(
    parts, flow, info_ref, *refs,
):
    cot_refs, refs = refs[:parts], refs[parts:]
    wd_ref, slope_ref, wu_ref, state_ref, mixed_ref, factor_ref, gm_ref, wo_ref, inner_ref, mlp_ref, *refs = refs
    dstate_ref, late_ref, early_ref, dlate_ref, dearly_ref, keep_ref, send_ref, dwo_ref, dgain_ref = refs[:9]
    dpre_ref, dproj_ref, cot_ref = refs[9:]
    flow.need(*cot_refs, wd_ref, slope_ref)
    join(cot_refs, cot_ref)
    hidden, width = wd_ref.shape

    def pack(half, first, value):
        rows = pl.ds(first, value.shape[0])

        @pl.when(info_ref[0] == half)
        def _():
            keep_ref[rows, :] = value.astype(BF16)

        @pl.when(info_ref[0] != half)
        def _():
            send_ref[rows, :] = value.astype(BF16)

    total = jnp.zeros((8, width), F32)
    for start, size in cuts(cot_ref.shape[0], 256):
        rows = pl.ds(start, size)
        cot = cot_ref[rows, :]
        d_mlp = None
        for first, step in cuts(hidden, 512):
            some = pl.ds(first, step)
            d_inner = dot(cot, wd_ref[some, :], NT)
            d_pre = (slope_ref[rows, some].astype(F32) * d_inner).astype(BF16)
            dpre_ref[rows, some] = d_pre
            flow.need(wu_ref)
            part = dot(d_pre, wu_ref[:, some], NT)
            d_mlp = part if d_mlp is None else d_mlp + part
        flow.need(gm_ref, wo_ref, state_ref, mixed_ref, factor_ref)
        unit, inverse = norm_parts(state_ref[rows, :])
        total = total + fold(d_mlp * unit)
        d_state = cot.astype(F32) + norm_back(d_mlp, unit, inverse, gm_ref[...])
        dstate_ref[rows, :] = d_state
        d_proj = d_state.astype(BF16)
        dproj_ref[rows, :] = d_proj
        d_att = dot(d_proj, wo_ref[...], NT)
        mixed = mixed_ref[rows, :].astype(F32)
        for lane, part_ref, delta_ref in ((0, late_ref, dlate_ref), (1, early_ref, dearly_ref)):
            part = (d_att * factor_ref[rows, lane : lane + 1]).astype(BF16)
            part_ref[rows, :] = part
            delta = jnp.sum(part.astype(F32) * mixed, axis=-1, keepdims=True)
            delta_ref[:, rows] = row_of(delta)
    dgain_ref[...] = total
    for ref in (dstate_ref, late_ref, early_ref, dlate_ref, dearly_ref):
        flow.emit(ref)
    flow.need(inner_ref, mlp_ref)
    for first, step in cuts(hidden, 512):
        pack(0, first, dot(inner_ref[:, first : first + step], cot_ref[...], TN))
    for first, step in cuts(hidden, 512):
        pack(1, first, dot(mlp_ref[...], dpre_ref[:, first : first + step], TN))
    dwo_ref[...] = dot(mixed_ref[...], dproj_ref[...], TN).astype(BF16)


def mlp_back(info, cots, slope, state, mixed, mlp, inner, factor, gm, wo, wu, wd):
    rows, width = state.shape
    hidden = wu.shape[1]
    tall, flat = (rows, width), (8, rows)
    outs = [(tall, F32), (tall, BF16), (tall, BF16), (flat, F32), (flat, F32)]
    outs += [((hidden, width), BF16)] * 2 + [((width, width), BF16), ((8, width), F32)]
    return hbm_call(
        functools.partial(mlp_back_kernel, len(cots)),
        "mlp_back",
        outs,
        (info, *cots, wd, slope, wu, state, mixed, factor, gm, wo, inner, mlp),
        20,
        [((rows, hidden), BF16), (tall, BF16), (tall, BF16)],
        smem=1,
    )


def attention_back_kernel(count, start, parts, extra, scale, flow, info_ref, *refs):
    q_ref, wk_ref, wv_ref, gain_ref, *refs = refs
    datt_ref, delta_ref, *refs = refs
    v_refs, w_refs, t_refs, k_refs = (refs[j : 4 * count : 4] for j in range(4))
    refs = refs[4 * count :]
    sums, refs = refs[:start], refs[start:]
    if parts:
        lat_ref, gl_ref, wq_ref, dstate_ref, dwo_ref, dgmlp_ref, *refs = refs
    dtok_refs, refs = refs[:count], refs[count:]
    if parts:
        dlat_ref, *refs = refs
        keep_ref, send_ref, dq_ref, akey_ref, aval_ref, dgain_ref, latlow_ref, dquery_ref, *refs = refs
    else:
        dq_ref, akey_ref, aval_ref, dgain_ref, *refs = refs
    dscore_ref, low_ref, dkey_ref, dval_ref, part_ref = refs
    totals = (dq_ref, akey_ref, aval_ref, dgain_ref)
    flow.need(q_ref, wk_ref, wv_ref, gain_ref)
    for p in range(count):
        size = k_refs[p].shape[0]
        flow.need(datt_ref, delta_ref, v_refs[p], w_refs[p], t_refs[p], k_refs[p])
        begin, end, first_place = info_ref[1 + 3 * p], info_ref[2 + 3 * p], info_ref[3 + 3 * p]
        part_ref[...] = jnp.zeros_like(part_ref)
        for first, step in cuts(size, 256):
            rows = pl.ds(first, step)
            active = (first_place + first < end) & (first_place + first + step > begin)

            @pl.when(active)
            def _(p=p, rows=rows):
                d_prob = dot(v_refs[p][rows, :], datt_ref[...], NT)
                d_score = (w_refs[p][rows, :].astype(F32) * (d_prob - delta_ref[:1, :])).astype(BF16)
                dscore_ref[rows, :] = d_score
                d_key = (dot(d_score, q_ref[...]) * scale).astype(BF16)
                d_value = dot(w_refs[p][rows, :], datt_ref[...]).astype(BF16)
                dkey_ref[rows, :] = d_key
                dval_ref[rows, :] = d_value
                unit, _ = norm_parts(t_refs[p][rows, :].astype(F32))
                low_ref[rows, :] = (unit * gain_ref[...]).astype(BF16)
                d_tok = dot(d_key, wk_ref[...], NT) + dot(d_value, wv_ref[...], NT)
                dtok_refs[p][rows, :] = d_tok.astype(BF16)
                part_ref[...] += fold(d_tok * unit)

            @pl.when(jnp.logical_not(active))
            def _(p=p, rows=rows):
                for ref in (dscore_ref, dkey_ref, dval_ref, low_ref, dtok_refs[p]):
                    ref[rows, :] = jnp.zeros((rows.size, ref.shape[1]), BF16)

        flow.emit(dtok_refs[p])
        dgain = part_ref[...]
        here = pl.ds(0, size)
        news = (
            dot(dscore_ref[here, :], k_refs[p][...], TN),
            dot(low_ref[here, :], dkey_ref[here, :], TN),
            dot(low_ref[here, :], dval_ref[here, :], TN),
            dgain,
        )
        if p == 0:
            flow.need(*sums)
        for j, (ref, value) in enumerate(zip(totals, news)):
            if p == 0:
                ref[...] = value + sums[j][...] if sums else value
            else:
                ref[...] += value
    if not parts:
        return
    flow.need(lat_ref, gl_ref, wq_ref, dstate_ref, dwo_ref, dgmlp_ref)
    total = None
    width = wq_ref.shape[0]
    for first, size in cuts(lat_ref.shape[0], 256):
        rows = pl.ds(first, size)
        unit, inverse = norm_parts(lat_ref[rows, :].astype(F32))
        gain = gl_ref[...]
        latlow_ref[rows, :] = (unit * gain).astype(BF16)
        d_query = (dq_ref[rows, :] * scale).astype(BF16)
        dquery_ref[rows, :] = d_query
        d_low = dot(d_query, wq_ref[...], NT)
        line_store(dlat_ref, parts, info_ref[1 + 3 * count], first, (dstate_ref[rows, :] + norm_back(d_low, unit, inverse, gain)).astype(BF16))
        part = fold(d_low * unit)
        total = part if total is None else total + part
    flow.emit(dlat_ref)
    d_wq = dot(latlow_ref[...], dquery_ref[...], TN)
    gains = [jnp.sum(g, axis=0, keepdims=True) for g in (total, dgain_ref[...], dgmlp_ref[...])]
    line = lax.broadcasted_iota(jnp.int32, (extra, width), 0)
    block = jnp.where(line == 0, gains[0], jnp.where(line == 1, gains[1], jnp.where(line == 2, gains[2], 0.0)))
    halves = ((d_wq, akey_ref), (aval_ref, dwo_ref))
    for ref, core in ((keep_ref, info_ref[0]), (send_ref, 1 - info_ref[0])):
        ref[pl.ds(2 * width, extra), :] = block.astype(BF16)
        for h, half in enumerate(halves):

            @pl.when(core == h)
            def _(ref=ref, half=half):
                for j, piece in enumerate(half):
                    ref[pl.ds(j * width, width), :] = piece[...].astype(BF16)


def attention_back(info, q, wk, wv, gain, grads, values, weights, tokens, keys, sums, latents, parts, extra, scale):
    rows, width = q.shape
    square = ((width, width), F32)
    totals = [((rows, width), F32), square, square, ((8, width), F32)]
    most = max(k.shape[0] for k in keys)
    work = [((most, rows), BF16)] + [((most, width), BF16)] * 3 + [((8, width), F32)]
    outs = [(k.shape, BF16) for k in keys]
    by_piece = [a for piece in zip(values, weights, tokens, keys) for a in piece]
    args = (info, q, wk, wv, gain, *grads, *by_piece, *sums)
    if latents:
        args = (*args, *latents)
        outs += [((rows, width), BF16)] + [((2 * width + extra, width), BF16)] * 2
        work = totals + [((rows, width), BF16)] * 2 + work
    else:
        outs += totals
        parts = 0
    kernel = functools.partial(attention_back_kernel, len(keys), len(sums), parts, extra, scale)
    out = hbm_call(kernel, "attention_back", outs, args, 12, work, smem=1)
    return out[: len(keys)], out[len(keys) :]


def token_back_kernel(count, flow, tok_ref, gain_ref, *refs):
    flow.need(tok_ref, gain_ref, *refs[:count])
    for start, size in cuts(tok_ref.shape[0], 256):
        rows = pl.ds(start, size)
        unit, inverse = norm_parts(tok_ref[rows, :].astype(F32))
        total = refs[0][rows, :].astype(F32)
        for ref in refs[1:count]:
            total = total + ref[rows, :].astype(F32)
        refs[count][rows, :] = norm_back(total, unit, inverse, gain_ref[...])
        flow.emit(refs[count], rows)


def token_back(tok, gain, parts):
    args = (tok, gain, *parts)
    [out] = hbm_call(functools.partial(token_back_kernel, len(parts)), "token_back", [(tok.shape, F32)], args, 8, stores=len(cuts(tok.shape[0], 256)))
    return out


def picks(shape, scenes, scene, transposed=False):
    along = lax.broadcasted_iota(jnp.int32, shape, 1 if transposed else 0)
    across = lax.broadcasted_iota(jnp.int32, shape, 0 if transposed else 1)
    return jnp.where(across == along * scenes + scene, 1.0, 0.0).astype(BF16)


def sort_kernel(flow, info_ref, rows_ref, *out_refs):
    flow.need(rows_ref)
    for k, ref in enumerate(out_refs):
        scenes, some = len(out_refs), ref.shape[0] // len(out_refs)
        take = picks((some, some * scenes), scenes, info_ref[0] ^ k)
        for first in range(0, ref.shape[0], some):
            given = rows_ref[pl.ds(first * scenes, some * scenes), :]
            ref[pl.ds(first, some), :] = dot(take, given).astype(BF16)
        flow.emit(ref)


def sort_rows(info, value, scenes):
    rows, width = value.shape
    return hbm_call(sort_kernel, "sort_rows", [((rows // scenes, width), BF16)] * scenes, (info, value), 16, smem=1)


def unsort_kernel(scenes, flow, info_ref, *refs):
    *in_refs, out_ref = refs
    flow.need(*in_refs)
    if len(in_refs) == 1:
        size = out_ref.shape[0] // scenes
        in_refs = [in_refs[0].at[pl.ds(k * size, size)] for k in range(scenes)]
    rows, part = out_ref.shape[0], in_refs[0].shape[0]
    step = rows // scenes
    for start in range(0, rows, step):
        total = None
        for k, ref in enumerate(in_refs):
            some = part // scenes
            first = start // scenes
            put = picks((step, some), scenes, info_ref[0] ^ k, transposed=True)
            value = dot(put, ref[pl.ds(first, some), :])
            total = value if total is None else total + value
        out_ref[pl.ds(start, step), :] = total.astype(out_ref.dtype)
        flow.emit(out_ref, pl.ds(start, step))


def unsort_rows(info, parts, scenes, dtype):
    rows, width = sum(p.shape[0] for p in parts), parts[0].shape[1]
    kernel = functools.partial(unsort_kernel, scenes)
    [out] = hbm_call(kernel, "unsort_rows", [((rows, width), dtype)], (info, *parts), 16, smem=1, stores=scenes)
    return out


def split_kernel(count, place, extra, info_ref, *refs):
    in_refs, out_refs = refs[:count], refs[count:]
    rest = None
    if extra and out_refs[-1].shape[0] == extra and len(out_refs) == 2:
        *out_refs, rest = out_refs
    body = in_refs[0].shape[0] - extra
    step = body // len(out_refs)

    def total(start, rows):
        value = in_refs[0][pl.ds(start, rows), :].astype(F32)
        for ref in in_refs[1:]:
            value = value + ref[pl.ds(start, rows), :].astype(F32)
        return value.astype(BF16)

    shared = total(body, extra) if extra else None
    for k, ref in enumerate(out_refs):
        start = (info_ref[place] ^ k) * step if len(out_refs) > 1 else 0
        ref[pl.ds(0, step), :] = total(start if isinstance(start, int) else pl.multiple_of(start, 16), step)
        if extra and rest is None:
            ref[pl.ds(step, extra), :] = shared
    if rest is not None:
        rest[...] = shared


def split_sum(info, arrays, parts, place, extra):
    rows, width = arrays[0].shape
    step = (rows - extra) // parts
    if parts > 1:
        outs = [((step + extra, width), BF16)] * parts
    else:
        outs = [((step, width), BF16)] + ([((extra, width), BF16)] if extra else [])
    kernel = functools.partial(split_kernel, len(arrays), place, extra)
    return vmem_call(kernel, "split_sum", outs, (info, *arrays), 8, smem=1)


def unpack_kernel(width, count, crossed, info_ref, *refs):
    core, quad, line = info_ref[0], info_ref[1], info_ref[2]
    out_refs, (mine_ref, other_ref) = refs[2 * count : -2], refs[-2:]
    join(refs[:count], mine_ref)
    join(refs[count : 2 * count], other_ref)
    half = mine_ref.shape[0]
    lines = info_ref.shape[0] - 3
    block = half // (4 * lines)
    for h in range(2):
        for m in range(4):
            for z in range(lines):
                chip, spot = quad ^ m, line ^ z
                if crossed:
                    late = spot // (lines // 2)
                    chip = jnp.where(late == 0, chip, (chip % 2) * 2 + chip // 2)
                    spot = (late * 4 + chip) * (lines // 2) + spot % (lines // 2)
                else:
                    spot = chip * lines + spot
                rows = pl.ds(pl.multiple_of(spot * block, 16), block)
                value = jnp.where(core == h, mine_ref[rows, :].astype(F32), other_ref[rows, :].astype(F32))
                at = h * half + (m * lines + z) * block
                total = 0
                for ref in out_refs:
                    tall = ref.shape[0] * (ref.shape[1] // width)
                    if total <= at < total + tall:
                        inside = at - total
                        slab, row = inside // ref.shape[0], inside % ref.shape[0]
                        ref[pl.ds(row, block), pl.ds(slab * width, width)] = value
                    total += tall


class Sums:
    def __init__(self, seqs, blocks):
        self.seqs, self.blocks = seqs, blocks
        self.lines = blocks // 2
        seq, blk = lax.axis_index("seq"), lax.axis_index("blk")
        places = [seq % 2, (seq // 2) * 2 + blk % 2, blk // 2] + [seq * 0] * self.lines
        self.info = jnp.stack(places).astype(jnp.int32)

    def flip(self, value, seq_mask, blk_mask):
        pairs = [
            (s * self.blocks + b, (s ^ seq_mask) * self.blocks + (b ^ blk_mask))
            for s in range(self.seqs)
            for b in range(self.blocks)
        ]
        return lax.ppermute(value, ("seq", "blk"), pairs)

    def to_core(self, value):
        return self.flip(value, 1, 0)

    def to_quad(self, values):
        return [self.flip(v, 2 * (k // 2), k % 2) for k, v in enumerate(values, 1)]

    def to_line(self, values):
        return [self.flip(v, 0, 2 * k) for k, v in enumerate(values, 1)]

    def add_core(self, keep, received, extra=0):
        return split_sum(self.info, [keep, received], 4, 1, extra)

    def add_quad(self, keep, received, extra=0):
        return split_sum(self.info, [keep, *received], self.lines, 2, extra)

    def add_line(self, keep, received, extra=0):
        return split_sum(self.info, [keep, *received], 1, 0, extra)

    def unpack(self, mine, other, shapes, crossed=False):
        outs = [(shape, F32) for shape in shapes]
        rows, width = mine[0].shape
        kernel = functools.partial(unpack_kernel, width, len(mine), crossed)
        work = [((rows * len(mine), width), BF16)] * 2
        return vmem_call(kernel, "unpack", outs, (self.info, *mine, *other), 16, work, smem=1)


def after(value, *others):
    return lax.optimization_barrier((value, others))[0]


def local(
    sizes, latents, tokens, lengths, gain_lat, gain_tok, gain_mlp, w_query, w_key, w_value, w_out, w_up, w_down, d_out
):
    lat, tok, cot = latents[0], tokens[0], d_out[0]
    scene_lengths = lengths[0]
    scenes = scene_lengths.shape[0]
    seqs, blocks = sizes["seq"], sizes["blk"]
    group = blocks // scenes
    span, width = tok.shape
    hidden = w_up.shape[1]
    scale = width ** (-0.5)
    position = lax.axis_index("blk")
    scene, member = position // group, position % group
    scene_info = scene.astype(jnp.int32).reshape(1)
    gl, gt, gm = (g.reshape(1, width) for g in (gain_lat, gain_tok, gain_mlp))
    lines = [[m + group * k for k in range(scenes)] for m in range(group)]
    sums = Sums(seqs, blocks)

    def exchange(value, mask):
        return sums.flip(value, 0, mask)

    def across(values):
        return [exchange(v, group * k) if k else v for k, v in enumerate(values)]

    order = jnp.arange(scenes, dtype=jnp.int32)
    begin = jnp.sum(jnp.where(order < scene, scene_lengths, 0))
    end = begin + jnp.sum(jnp.where(order == scene, scene_lengths, 0))
    base = scene * group * span
    tail_rows = (scenes - 1) * group * span // 8
    starts = [base + (member ^ k) * span for k in [*range(1, group), 0]]
    main_info = jnp.stack([begin, end, *starts]).astype(jnp.int32)
    tail_info = jnp.stack([begin, end, base - tail_rows]).astype(jnp.int32)
    calls, size = [[0], []], 0
    for j in range(1, group + 1):
        if calls[-1] and size + span > 3 * span:
            calls.append([])
            size = 0
        calls[-1].append(j)
        size += span
    core = lax.axis_index("seq") % 2
    places = []
    for call in calls:
        spots = [v for j in call for v in (begin, end, (base - tail_rows, *starts)[j])]
        places.append(jnp.stack([core, *spots, scene]).astype(jnp.int32))

    lat_parts = sort_rows(scene_info, lat, scenes)
    others = [exchange(tok, k) for k in range(1, group)]
    lat_in = across(lat_parts)
    cot_parts = sort_rows(scene_info, after(cot, lat_parts), scenes)
    own_kv = keys_values(after(tok, cot_parts), gt, w_key, w_value)
    lat_in, others, cot_parts, own_kv, main_info, tail_info, places = lax.optimization_barrier(
        (lat_in, others, cot_parts, own_kv, main_info, tail_info, places)
    )
    cot_near = exchange(cot_parts[1], group)

    pieces = [tok, *others]
    lowest = (group * span - tail_rows) // span
    needed = []
    for owner in range(lowest, group):
        block = pieces[owner]
        for m in range(1, group):
            block = jnp.where(member == m, pieces[owner ^ m], block)
        needed.append(block)
    needed = jnp.concatenate(needed, axis=0) if len(needed) > 1 else needed[0]
    pairs = [(i, i + group) for i in range(blocks - group)]
    sent = needed[needed.shape[0] - tail_rows :]
    tail = lax.ppermute(sent, "blk", pairs)
    fresh = list(others) if group == 2 else []
    given = [own_kv] if fresh else [keys_values(piece, gt, w_key, w_value) for piece in others] + [own_kv]
    made_keys, made_values = zip(*given)
    query, acc, top, total, lat_set, weights, keys, values = attend(
        main_info, lat_in, gl, w_query, after(fresh, sent), gt, w_key, w_value, made_keys, made_values, scale
    )
    tail, query, cot_parts, cot_near = lax.optimization_barrier((tail, query, cot_parts, cot_near))

    cot_in = [cot_parts[0], cot_near, *[exchange(cot_parts[k], group * k) for k in range(2, scenes)]]
    saved, out_parts = finish(
        tail_info, scenes, lat_set, query, acc, top, total, tail, gt, w_key, w_value, gm, w_out, w_up, w_down, scale
    )
    tail_key, tail_value, tail_weight, factor, mixed, mlp, state, inner, slope = saved
    cot_in, out_parts, slope = lax.optimization_barrier((cot_in, out_parts, slope))
    out_back = across(out_parts)
    d_state, d_late, d_early, late, early_delta, keep, send, d_wo, dg_mlp = mlp_back(
        sums.info, cot_in, slope, state, mixed, mlp, inner, factor, gm, w_out, w_up, w_down
    )

    out_back, keep, send, d_early, d_late = lax.optimization_barrier((out_back, keep, send, d_early, d_late))
    received = sums.to_core(send)
    pieces = [(tail_value, tail_weight, tail, tail_key)]
    pieces += [(values[j], weights[j], piece, keys[j]) for j, piece in enumerate((*others, tok))]
    extra = 16
    d_toks, kept = [], []
    for j, call in enumerate(calls):
        some_values, some_weights, some_tokens, some_keys = zip(*[pieces[p] for p in call])
        latents = (lat_set, gl, w_query, d_state, d_wo, dg_mlp) if j == len(calls) - 1 else ()
        grads = (d_early, early_delta) if j else (d_late, late)
        some, kept = attention_back(
            places[j], query, w_key, w_value, gt, grads, some_values, some_weights, some_tokens, some_keys, kept,
            latents, scenes, extra, scale,
        )
        d_toks += some
        if j == 0:
            received, d_toks, kept = lax.optimization_barrier((received, d_toks, kept))
            keep, *sends = sums.add_core(keep, received)
            d_early = after(d_early, keep)
            received = sums.to_quad(sends)
            d_tail = lax.ppermute(d_toks[0], "blk", [(j, i) for i, j in pairs])
    received, d_tail, d_toks, kept = lax.optimization_barrier((received, d_tail, d_toks, kept))
    _, *returned, own = d_toks
    d_lat_set, small_keep, small_send = kept

    returned = dict(enumerate(returned, 1))
    own_tail = []
    for owner in range(lowest, group):
        start = owner * span - (group * span - tail_rows)
        chunk = d_tail[max(start, 0) : start + span]
        chunk = jnp.pad(chunk, ((span - chunk.shape[0], 0), (0, 0)))
        for k in range(1, group):
            returned[k] = returned[k] + jnp.where(member == owner ^ k, chunk, 0)
        own_tail.append(jnp.where(member == owner, chunk, 0))
    small_got = sums.to_core(small_send)
    keep, *sends = sums.add_quad(keep, received)
    received = sums.to_line(sends)
    returned = [exchange(after(returned[k], keep), k) for k in range(1, group)]
    output = unsort_rows(scene_info, after(out_back, keep), scenes, BF16)
    small_got, received, output = lax.optimization_barrier((small_got, received, output))
    [shard] = sums.add_line(keep, received)
    small_keep, *small_sends = sums.add_core(small_keep, small_got, extra)
    small_got = sums.to_quad(small_sends)
    block = shard
    for j in range(sums.lines.bit_length() - 1):
        far = sums.flip(block, 0, 2 << j)
        if j == sums.lines.bit_length() - 2:
            small_got, far = lax.optimization_barrier((small_got, far))
        block = jnp.concatenate([block, far], axis=0)
    half = block.shape[0] // 2
    near_a, near_b = block[:half], block[half:]
    far_a, far_b = sums.flip(near_a, 0, 1), sums.flip(near_b, 2, 0)
    small_keep, *small_sends = sums.add_quad(small_keep, small_got, extra)
    small_got = sums.to_line(small_sends)
    small_got, far_a, far_b, returned = lax.optimization_barrier((small_got, far_a, far_b, returned))
    two_a, two_b = jnp.concatenate([near_a, far_a], axis=0), jnp.concatenate([near_b, far_b], axis=0)
    last_a, last_b = sums.flip(two_a, 2, 0), sums.flip(two_b, 0, 1)
    small_shard, gains = sums.add_line(small_keep, small_got, extra)
    small_block = small_shard
    for j in range(sums.lines.bit_length() - 1):
        far = sums.flip(small_block, 0, 2 << j)
        if j == sums.lines.bit_length() - 2:
            d_tokens = token_back(tok, gt, [own, *own_tail, *after(returned, small_block)])
            far = after(far, d_tokens)
        small_block = jnp.concatenate([small_block, far], axis=0)
    other_a, other_b = sums.to_core(two_a), sums.to_core(two_b)
    last_a, last_b, small_block, other_a, other_b = lax.optimization_barrier(
        (last_a, last_b, small_block, other_a, other_b)
    )
    leaving = after(d_lat_set, small_block)
    d_lat_back = lax.all_to_all(leaving, "blk", 0, 0, axis_index_groups=lines, tiled=True)
    small_got = sums.to_quad([small_block] * 3)
    mine = [two_a, last_a, two_b, last_b]
    other = [other_a, sums.to_core(last_a), other_b, sums.to_core(last_b)]
    d_w_down, d_w_up = sums.unpack(mine, other, [(hidden, width), (width, hidden)], crossed=True)
    small_got, d_lat_back, d_w_up = lax.optimization_barrier((small_got, d_lat_back, d_w_up))
    small_mine = [small_block, *small_got]
    small_other = [sums.to_core(v) for v in small_mine]
    d_latents = unsort_rows(0 * scene_info, [after(d_lat_back, small_mine)], scenes, F32)
    squares = sums.unpack(small_mine, after(small_other, d_latents), [(width, width)] * 4)
    gains = gains.astype(F32)
    return (output[None], d_latents[None], d_tokens[None], *squares, d_w_up, d_w_down, gains[0], gains[1], gains[2])


def solution(mesh):
    split = P("seq", "blk", None)
    in_specs = (split, split, P("seq", None)) + (P(),) * 9 + (split,)
    out_specs = (split,) * 3 + (P(),) * 9
    return jax.shard_map(
        functools.partial(local, dict(mesh.shape)), mesh=mesh, in_specs=in_specs, out_specs=out_specs, check_vma=False
    )
```

```python
import functools
import math

import jax
import jax.numpy as jnp
from jax import lax
from jax.experimental import pallas as pl
from jax.experimental.pallas import tpu as pltpu
from jax.sharding import PartitionSpec as P

EPSILON = 1e-05
NEGATIVE = -1e30
ROOM = (64 << 20) - (160 << 10)
LOG2E = 1.4426950408889634
GELU_C = math.sqrt(2.0 / math.pi)
GELU_A = 0.044715
F32 = jnp.float32
BF16 = jnp.bfloat16
NN = (((1,), (0,)), ((), ()))
NT = (((1,), (1,)), ((), ()))
TN = (((0,), (0,)), ((), ()))


def dot(left, right, dims=NN):
    return lax.dot_general(left, right, dims, preferred_element_type=F32)


def norm_parts(rows):
    center = rows - jnp.mean(rows, axis=-1, keepdims=True)
    spread = jnp.mean(center * center, axis=-1, keepdims=True)
    inverse = lax.rsqrt(spread + EPSILON)
    return center * inverse, inverse


def norm_back(d_normed, unit, inverse, gain):
    d_unit = d_normed * gain
    mean_d = jnp.mean(d_unit, axis=-1, keepdims=True)
    mean_p = jnp.mean(d_unit * unit, axis=-1, keepdims=True)
    return inverse * (d_unit - mean_d - unit * mean_p)


def vmem_call(kernel, name, outs, args, limit, scratch=(), smem=0):
    held = sum(math.prod(shape) * jnp.dtype(dtype).itemsize for shape, dtype in scratch)
    in_vmem = pl.BlockSpec(memory_space=pltpu.VMEM)
    in_smem = pl.BlockSpec(memory_space=pltpu.SMEM)
    return pl.pallas_call(
        kernel,
        in_specs=[in_smem] * smem + [in_vmem] * (len(args) - smem),
        out_specs=[in_vmem] * len(outs),
        out_shape=[jax.ShapeDtypeStruct(shape, dtype) for shape, dtype in outs],
        scratch_shapes=[pltpu.VMEM(shape, dtype) for shape, dtype in scratch],
        compiler_params=pltpu.CompilerParams(vmem_limit_bytes=(limit << 20) + held),
        cost_estimate=pl.CostEstimate(flops=0, bytes_accessed=0, transcendentals=0),
        name=name,
    )(*args)


class Flow:
    AHEAD = 64 << 20

    def __init__(self, loads, stores, semaphores):
        self.loads = loads
        self.stores = stores
        self.semaphores = semaphores
        self.started = 0
        self.waiting = set(range(len(loads)))
        self.begun = []
        self.whole = set()
        self.start_more(-1)

    def start_more(self, least):
        def size(j):
            held = self.loads[j][1]
            return math.prod(held.shape) * jnp.dtype(held.dtype).itemsize

        flying = sum(size(j) for j in self.waiting if j < self.started)
        while self.started < len(self.loads) and (self.started <= least or flying + size(self.started) <= self.AHEAD):
            flying += size(self.started)
            self.loads[self.started][2].start()
            self.started += 1

    def need(self, *refs):
        wanted = [j for j, load in enumerate(self.loads) if j in self.waiting and any(load[1] is r for r in refs)]
        for j in wanted:
            self.start_more(j)
        for j in wanted:
            self.waiting.discard(j)
            self.loads[j][2].wait()
        self.start_more(-1)

    def emit(self, ref, *where):
        for j, (out, held) in enumerate(self.stores):
            if held is ref:
                self.whole.add(j)
                source, target = (held.at[where], out.at[where]) if where else (held, out)
                copy = pltpu.make_async_copy(source, target, self.semaphores.at[len(self.begun)])
                copy.start()
                self.begun.append(copy)

    def close(self):
        self.need(*[held for _, held, _ in self.loads])
        for j, (_, held) in enumerate(self.stores):
            if j not in self.whole:
                self.emit(held)
        for copy in self.begun:
            copy.wait()


def hbm_call(kernel, name, outs, args, limit, scratch=(), smem=0, fixed_in=(), fixed_out=(), stores=None):
    arrays = args[smem:]
    moves_in = [j for j in range(len(arrays)) if j not in fixed_in]
    moves_out = [j for j in range(len(outs)) if j not in fixed_out]
    held = [(arrays[j].shape, arrays[j].dtype) for j in moves_in] + [outs[j] for j in moves_out] + list(scratch)
    size = sum(math.prod(shape) * jnp.dtype(dtype).itemsize for shape, dtype in held)

    resident = [(arrays[j].shape, arrays[j].dtype) for j in fixed_in] + [outs[j] for j in fixed_out]
    rest = sum(math.prod(shape) * jnp.dtype(dtype).itemsize for shape, dtype in resident)
    limit = max((limit << 20) + size, ROOM - rest)

    def body(*refs):
        scalars, refs = refs[:smem], refs[smem:]
        ins, refs = list(refs[: len(arrays)]), refs[len(arrays) :]
        results, refs = list(refs[: len(outs)]), refs[len(outs) :]
        *kept, load_sems, store_sems = refs
        loads, kept_out = [], []
        for n, j in enumerate(moves_in):
            loads.append((ins[j], kept[n], pltpu.make_async_copy(ins[j], kept[n], load_sems.at[n])))
            ins[j] = kept[n]
        kept = kept[len(moves_in) :]
        for n, j in enumerate(moves_out):
            kept_out.append((results[j], kept[n]))
            results[j] = kept[n]
        flow = Flow(loads, kept_out, store_sems)
        kernel(flow, *scalars, *ins, *results, *kept[len(moves_out) :])
        flow.close()

    def place(count, fixed):
        return [pl.BlockSpec(memory_space=pltpu.VMEM if j in fixed else pl.ANY) for j in range(count)]

    return pl.pallas_call(
        body,
        in_specs=[pl.BlockSpec(memory_space=pltpu.SMEM)] * smem + place(len(arrays), fixed_in),
        out_specs=place(len(outs), fixed_out),
        out_shape=[jax.ShapeDtypeStruct(shape, dtype) for shape, dtype in outs],
        scratch_shapes=[pltpu.VMEM(shape, dtype) for shape, dtype in held]
        + [pltpu.SemaphoreType.DMA((max(len(moves_in), 1),)), pltpu.SemaphoreType.DMA((max(stores or len(moves_out), 1),))],
        compiler_params=pltpu.CompilerParams(vmem_limit_bytes=min(limit, ROOM)),
        cost_estimate=pl.CostEstimate(flops=0, bytes_accessed=0, transcendentals=0),
        name=name,
    )(*args)


def cuts(size, step):
    return [(i, min(step, size - i)) for i in range(0, size, step)]


def fold(rows):
    return jnp.sum(rows.reshape(rows.shape[0] // 8, 8, rows.shape[1]), axis=0)


def column_of(row):
    return jnp.transpose(jnp.broadcast_to(row, (8, row.shape[1])))[:, :1]


def row_of(column):
    return jnp.transpose(jnp.broadcast_to(column, (column.shape[0], 128)))[:8, :]


def join(refs, whole_ref):
    part = refs[0].shape[0]
    for j, ref in enumerate(refs):
        whole_ref[pl.ds(j * part, part), :] = ref[...]


def line_store(ref, scenes, scene, start, value):
    part = ref.shape[0] // scenes
    size = min(part, value.shape[0])
    for first in range(0, value.shape[0], size):
        at = start + first
        place = (scene ^ (at // part)) * part + at % part
        ref[pl.ds(pl.multiple_of(place, 16), size), :] = value[first : first + size]


def part_store(refs, start, value):
    part = refs[0].shape[0]
    size = min(part, value.shape[0])
    for first in range(0, value.shape[0], size):
        at = start + first
        refs[at // part][pl.ds(at % part, size), :] = value[first : first + size]


def kv_kernel(flow, tok_ref, gain_ref, wk_ref, wv_ref, k_ref, v_ref):
    flow.need(tok_ref, gain_ref, wk_ref, wv_ref)
    for start, size in cuts(tok_ref.shape[0], 256):
        rows = pl.ds(start, size)
        unit, _ = norm_parts(tok_ref[rows, :].astype(F32))
        low = (unit * gain_ref[...]).astype(BF16)
        k_ref[rows, :] = dot(low, wk_ref[...]).astype(BF16)
        v_ref[rows, :] = dot(low, wv_ref[...]).astype(BF16)
    flow.emit(k_ref)
    flow.emit(v_ref)


def keys_values(tok, gain, w_key, w_value):
    return hbm_call(kv_kernel, "keys_values", [(tok.shape, BF16)] * 2, (tok, gain, w_key, w_value), 8)


def score_piece(info_ref, p, k_ref, s_ref, query, columns, top, scale):
    begin, end = info_ref[0], info_ref[1]
    for start, size in cuts(k_ref.shape[0], 512):
        s = dot(k_ref[pl.ds(start, size), :], query, NT) * (scale * LOG2E)
        place = info_ref[2 + p] + start + lax.broadcasted_iota(jnp.int32, (size, 1), 0)
        s = s + jnp.where((place >= begin) & (place < end), 0.0, NEGATIVE)
        s_ref[pl.ds(start, size), columns] = s
        top = jnp.maximum(top, jnp.max(s.reshape(size // 8, 8, s.shape[1]), axis=0))
    return top


def weigh_piece(v_ref, s_ref, w_ref, columns, top, total, acc):
    for start, size in cuts(v_ref.shape[0], 512):
        w = jnp.exp2(s_ref[pl.ds(start, size), columns] - top)
        total = total + fold(w)
        w_ref[pl.ds(start, size), columns] = w.astype(BF16)
    part = dot(w_ref[:, columns], v_ref[...], TN)
    return total, part if acc is None else acc + part


def attend_kernel(parts, fresh, count, scale, flow, info_ref, gl_ref, wq_ref, *refs):
    new, refs = refs[: 3 * bool(fresh) + fresh], refs[3 * bool(fresh) + fresh :]
    lat_refs, refs = refs[:parts], refs[parts:]
    given = count - fresh
    k_refs, v_refs, refs = refs[:given], refs[given : 2 * given], refs[2 * given :]
    q_ref, acc_ref, top_ref, tot_ref, lat_ref = refs[:5]
    refs = refs[5:]
    k_refs, v_refs, refs = refs[:fresh] + k_refs, refs[fresh : 2 * fresh] + v_refs, refs[2 * fresh :]
    w_refs, s_refs = refs[:count], refs[count:]
    flow.need(*lat_refs, gl_ref, wq_ref)
    join(lat_refs, lat_ref)
    for j in range(fresh):
        kv_kernel(flow, new[3 + j], *new[:3], k_refs[j], v_refs[j])
    for start, size in cuts(lat_ref.shape[0], 512):
        rows = columns = pl.ds(start, size)
        unit, _ = norm_parts(lat_ref[rows, :].astype(F32))
        query = dot((unit * gl_ref[...]).astype(BF16), wq_ref[...]).astype(BF16)
        q_ref[rows, :] = query
        flow.need(*k_refs)
        top = jnp.full((8, size), NEGATIVE, F32)
        for p in range(count):
            top = score_piece(info_ref, p, k_refs[p], s_refs[p], query, columns, top, scale)
        top = jnp.max(top, axis=0, keepdims=True)
        total, acc = jnp.zeros((8, size), F32), None
        flow.need(*v_refs)
        for p in range(count):
            total, acc = weigh_piece(v_refs[p], s_refs[p], w_refs[p], columns, top, total, acc)
        acc_ref[rows, :] = acc
        if start == 0:
            flow.emit(lat_ref)
        for p in range(count):
            flow.emit(w_refs[p], slice(None), columns)
        flow.emit(acc_ref, rows)
        top_ref[:, columns] = jnp.broadcast_to(top, (8, size))
        tot_ref[:, columns] = total


def attend(info, lats, gl, wq, fresh, gt, wk, wv, keys, values, scale):
    rows, width = len(lats) * lats[0].shape[0], lats[0].shape[1]
    made = [(t.shape, BF16) for t in fresh]
    pieces = [t.shape[0] for t in (*fresh, *keys)]
    outs = [((rows, width), BF16), ((rows, width), F32), ((8, rows), F32), ((8, rows), F32), ((rows, width), BF16)]
    outs += made * 2 + [((n, rows), BF16) for n in pieces]
    new = (gt, wk, wv, *fresh) if fresh else ()
    q, acc, top, total, lat, *rest = hbm_call(
        functools.partial(attend_kernel, len(lats), len(fresh), len(pieces), scale),
        "attend",
        outs,
        (info, gl, wq, *new, *lats, *keys, *values),
        12,
        [((n, rows), F32) for n in pieces],
        smem=1,
        stores=len(outs) + (len(cuts(rows, 512)) - 1) * (len(pieces) + 1),
    )
    more = len(fresh)
    return q, acc, top, total, lat, rest[2 * more :], (*rest[:more], *keys), (*rest[more : 2 * more], *values)


def finish_kernel(
    scale, flow, info_ref, tok_ref, gt_ref, wk_ref, wv_ref, top_ref, q_ref, tot_ref, acc_ref, lat_ref, gm_ref, wo_ref, wu_ref, wd_ref,
    k_ref, v_ref, w_ref, factor_ref, mixed_ref, mlp_ref, state_ref, inner_ref, slope_ref, *refs,
):
    *out_refs, s_ref = refs
    kv_kernel(flow, tok_ref, gt_ref, wk_ref, wv_ref, k_ref, v_ref)
    flow.need(top_ref, q_ref, tot_ref, acc_ref)
    hidden = wu_ref.shape[1]
    for start, size in cuts(lat_ref.shape[0], 512):
        rows = columns = pl.ds(start, size)
        old = top_ref[:1, columns]
        top = jnp.broadcast_to(old, (8, size))
        top = score_piece(info_ref, 0, k_ref, s_ref, q_ref[rows, :], columns, top, scale)
        top = jnp.max(top, axis=0, keepdims=True)
        total, acc = weigh_piece(v_ref, s_ref, w_ref, columns, top, jnp.zeros((8, size), F32), None)
        shrink = jnp.exp2(old - top)
        total = jnp.sum(total, axis=0, keepdims=True) + jnp.sum(tot_ref[:, columns], axis=0, keepdims=True) * shrink
        inverse = 1.0 / total
        late, early = column_of(inverse), column_of(shrink * inverse)
        lane = lax.broadcasted_iota(jnp.int32, (size, 128), 1)
        factor_ref[rows, :] = jnp.where(lane == 0, late, early)
        mixed_ref[rows, :] = (acc * late + acc_ref[rows, :] * early).astype(BF16)
    for ref in (w_ref, factor_ref, mixed_ref):
        flow.emit(ref)
    flow.need(lat_ref, wo_ref, gm_ref, wu_ref, wd_ref)
    for start, size in cuts(lat_ref.shape[0], 256):
        rows = pl.ds(start, size)
        state = lat_ref[rows, :].astype(F32) + dot(mixed_ref[rows, :], wo_ref[...])
        state_ref[rows, :] = state
        unit, _ = norm_parts(state)
        low = (unit * gm_ref[...]).astype(BF16)
        mlp_ref[rows, :] = low
        out = state
        for first, step in cuts(hidden, 512):
            some = pl.ds(first, step)
            u = dot(low, wu_ref[:, some])
            square = u * u
            t = jnp.tanh(u * (GELU_C + (GELU_C * GELU_A) * square))
            half = 0.5 + 0.5 * t
            inner = (u * half).astype(BF16)
            bend = u * ((0.5 * GELU_C) + (1.5 * GELU_C * GELU_A) * square)
            inner_ref[rows, some] = inner
            slope_ref[rows, some] = (half + bend * (1.0 - t * t)).astype(BF16)
            out = out + dot(inner, wd_ref[some, :])
        part_store(out_refs, start, out.astype(BF16))
        for ref in (state_ref, mlp_ref, inner_ref, slope_ref):
            flow.emit(ref, rows)


def finish(info, parts, lat, q, acc, top, total, tail, gt, wk, wv, gm, wo, wu, wd, scale):
    rows, width = lat.shape
    hidden = wu.shape[1]
    tall = (rows, width)
    outs = [(tail.shape, BF16)] * 2 + [((tail.shape[0], rows), BF16), ((rows, 128), F32), (tall, BF16), (tall, BF16), (tall, F32)]
    outs += [((rows, hidden), BF16)] * 2 + [((rows // parts, width), BF16)] * parts
    out = hbm_call(
        functools.partial(finish_kernel, scale),
        "finish",
        outs,
        (info, tail, gt, wk, wv, top, q, total, acc, lat, gm, wo, wu, wd),
        22,
        [((tail.shape[0], rows), F32)],
        smem=1,
        stores=len(outs) + 4 * (len(cuts(rows, 256)) - 1),
    )
    return out[:9], out[9:]


def mlp_back_kernel(
    parts, flow, info_ref, *refs,
):
    cot_refs, refs = refs[:parts], refs[parts:]
    wd_ref, slope_ref, wu_ref, state_ref, mixed_ref, factor_ref, gm_ref, wo_ref, inner_ref, mlp_ref, *refs = refs
    dstate_ref, late_ref, early_ref, dlate_ref, dearly_ref, keep_ref, send_ref, dwo_ref, dgain_ref = refs[:9]
    dpre_ref, dproj_ref, cot_ref = refs[9:]
    flow.need(*cot_refs, wd_ref, slope_ref)
    join(cot_refs, cot_ref)
    hidden, width = wd_ref.shape

    def pack(half, first, value):
        rows = pl.ds(first, value.shape[0])

        @pl.when(info_ref[0] == half)
        def _():
            keep_ref[rows, :] = value.astype(BF16)

        @pl.when(info_ref[0] != half)
        def _():
            send_ref[rows, :] = value.astype(BF16)

    total = jnp.zeros((8, width), F32)
    for start, size in cuts(cot_ref.shape[0], 256):
        rows = pl.ds(start, size)
        cot = cot_ref[rows, :]
        d_mlp = None
        for first, step in cuts(hidden, 512):
            some = pl.ds(first, step)
            d_inner = dot(cot, wd_ref[some, :], NT)
            d_pre = (slope_ref[rows, some].astype(F32) * d_inner).astype(BF16)
            dpre_ref[rows, some] = d_pre
            flow.need(wu_ref)
            part = dot(d_pre, wu_ref[:, some], NT)
            d_mlp = part if d_mlp is None else d_mlp + part
        flow.need(gm_ref, wo_ref, state_ref, mixed_ref, factor_ref)
        unit, inverse = norm_parts(state_ref[rows, :])
        total = total + fold(d_mlp * unit)
        d_state = cot.astype(F32) + norm_back(d_mlp, unit, inverse, gm_ref[...])
        dstate_ref[rows, :] = d_state
        d_proj = d_state.astype(BF16)
        dproj_ref[rows, :] = d_proj
        d_att = dot(d_proj, wo_ref[...], NT)
        mixed = mixed_ref[rows, :].astype(F32)
        for lane, part_ref, delta_ref in ((0, late_ref, dlate_ref), (1, early_ref, dearly_ref)):
            part = (d_att * factor_ref[rows, lane : lane + 1]).astype(BF16)
            part_ref[rows, :] = part
            delta = jnp.sum(part.astype(F32) * mixed, axis=-1, keepdims=True)
            delta_ref[:, rows] = row_of(delta)
    dgain_ref[...] = total
    for ref in (dstate_ref, late_ref, early_ref, dlate_ref, dearly_ref):
        flow.emit(ref)
    flow.need(inner_ref, mlp_ref)
    for first, step in cuts(hidden, 512):
        pack(0, first, dot(inner_ref[:, first : first + step], cot_ref[...], TN))
    for first, step in cuts(hidden, 512):
        pack(1, first, dot(mlp_ref[...], dpre_ref[:, first : first + step], TN))
    dwo_ref[...] = dot(mixed_ref[...], dproj_ref[...], TN).astype(BF16)


def mlp_back(info, cots, slope, state, mixed, mlp, inner, factor, gm, wo, wu, wd):
    rows, width = state.shape
    hidden = wu.shape[1]
    tall, flat = (rows, width), (8, rows)
    outs = [(tall, F32), (tall, BF16), (tall, BF16), (flat, F32), (flat, F32)]
    outs += [((hidden, width), BF16)] * 2 + [((width, width), BF16), ((8, width), F32)]
    return hbm_call(
        functools.partial(mlp_back_kernel, len(cots)),
        "mlp_back",
        outs,
        (info, *cots, wd, slope, wu, state, mixed, factor, gm, wo, inner, mlp),
        20,
        [((rows, hidden), BF16), (tall, BF16), (tall, BF16)],
        smem=1,
    )


def attention_back_kernel(count, start, parts, extra, scale, flow, info_ref, *refs):
    q_ref, wk_ref, wv_ref, gain_ref, *refs = refs
    datt_ref, delta_ref, *refs = refs
    v_refs, w_refs, t_refs, k_refs = (refs[j : 4 * count : 4] for j in range(4))
    refs = refs[4 * count :]
    sums, refs = refs[:start], refs[start:]
    if parts:
        lat_ref, gl_ref, wq_ref, dstate_ref, dwo_ref, dgmlp_ref, *refs = refs
    dtok_refs, refs = refs[:count], refs[count:]
    if parts:
        dlat_ref, *refs = refs
        keep_ref, send_ref, dq_ref, akey_ref, aval_ref, dgain_ref, latlow_ref, dquery_ref, *refs = refs
    else:
        dq_ref, akey_ref, aval_ref, dgain_ref, *refs = refs
    dscore_ref, low_ref, dkey_ref, dval_ref, part_ref = refs
    totals = (dq_ref, akey_ref, aval_ref, dgain_ref)
    flow.need(q_ref, wk_ref, wv_ref, gain_ref)
    for p in range(count):
        size = k_refs[p].shape[0]
        flow.need(datt_ref, delta_ref, v_refs[p], w_refs[p], t_refs[p], k_refs[p])
        begin, end, first_place = info_ref[1 + 3 * p], info_ref[2 + 3 * p], info_ref[3 + 3 * p]
        part_ref[...] = jnp.zeros_like(part_ref)
        for first, step in cuts(size, 256):
            rows = pl.ds(first, step)
            active = (first_place + first < end) & (first_place + first + step > begin)

            @pl.when(active)
            def _(p=p, rows=rows):
                d_prob = dot(v_refs[p][rows, :], datt_ref[...], NT)
                d_score = (w_refs[p][rows, :].astype(F32) * (d_prob - delta_ref[:1, :])).astype(BF16)
                dscore_ref[rows, :] = d_score
                d_key = (dot(d_score, q_ref[...]) * scale).astype(BF16)
                d_value = dot(w_refs[p][rows, :], datt_ref[...]).astype(BF16)
                dkey_ref[rows, :] = d_key
                dval_ref[rows, :] = d_value
                unit, _ = norm_parts(t_refs[p][rows, :].astype(F32))
                low_ref[rows, :] = (unit * gain_ref[...]).astype(BF16)
                d_tok = dot(d_key, wk_ref[...], NT) + dot(d_value, wv_ref[...], NT)
                dtok_refs[p][rows, :] = d_tok.astype(BF16)
                part_ref[...] += fold(d_tok * unit)

            @pl.when(jnp.logical_not(active))
            def _(p=p, rows=rows):
                for ref in (dscore_ref, dkey_ref, dval_ref, low_ref, dtok_refs[p]):
                    ref[rows, :] = jnp.zeros((rows.size, ref.shape[1]), BF16)

        flow.emit(dtok_refs[p])
        dgain = part_ref[...]
        here = pl.ds(0, size)
        news = (
            dot(dscore_ref[here, :], k_refs[p][...], TN),
            dot(low_ref[here, :], dkey_ref[here, :], TN),
            dot(low_ref[here, :], dval_ref[here, :], TN),
            dgain,
        )
        if p == 0:
            flow.need(*sums)
        for j, (ref, value) in enumerate(zip(totals, news)):
            if p == 0:
                ref[...] = value + sums[j][...] if sums else value
            else:
                ref[...] += value
    if not parts:
        return
    flow.need(lat_ref, gl_ref, wq_ref, dstate_ref, dwo_ref, dgmlp_ref)
    total = None
    width = wq_ref.shape[0]
    for first, size in cuts(lat_ref.shape[0], 256):
        rows = pl.ds(first, size)
        unit, inverse = norm_parts(lat_ref[rows, :].astype(F32))
        gain = gl_ref[...]
        latlow_ref[rows, :] = (unit * gain).astype(BF16)
        d_query = (dq_ref[rows, :] * scale).astype(BF16)
        dquery_ref[rows, :] = d_query
        d_low = dot(d_query, wq_ref[...], NT)
        line_store(dlat_ref, parts, info_ref[1 + 3 * count], first, (dstate_ref[rows, :] + norm_back(d_low, unit, inverse, gain)).astype(BF16))
        part = fold(d_low * unit)
        total = part if total is None else total + part
    flow.emit(dlat_ref)
    d_wq = dot(latlow_ref[...], dquery_ref[...], TN)
    gains = [jnp.sum(g, axis=0, keepdims=True) for g in (total, dgain_ref[...], dgmlp_ref[...])]
    line = lax.broadcasted_iota(jnp.int32, (extra, width), 0)
    block = jnp.where(line == 0, gains[0], jnp.where(line == 1, gains[1], jnp.where(line == 2, gains[2], 0.0)))
    halves = ((d_wq, akey_ref), (aval_ref, dwo_ref))
    for ref, core in ((keep_ref, info_ref[0]), (send_ref, 1 - info_ref[0])):
        ref[pl.ds(2 * width, extra), :] = block.astype(BF16)
        for h, half in enumerate(halves):

            @pl.when(core == h)
            def _(ref=ref, half=half):
                for j, piece in enumerate(half):
                    ref[pl.ds(j * width, width), :] = piece[...].astype(BF16)


def attention_back(info, q, wk, wv, gain, grads, values, weights, tokens, keys, sums, latents, parts, extra, scale):
    rows, width = q.shape
    square = ((width, width), F32)
    totals = [((rows, width), F32), square, square, ((8, width), F32)]
    most = max(k.shape[0] for k in keys)
    work = [((most, rows), BF16)] + [((most, width), BF16)] * 3 + [((8, width), F32)]
    outs = [(k.shape, BF16) for k in keys]
    by_piece = [a for piece in zip(values, weights, tokens, keys) for a in piece]
    args = (info, q, wk, wv, gain, *grads, *by_piece, *sums)
    if latents:
        args = (*args, *latents)
        outs += [((rows, width), BF16)] + [((2 * width + extra, width), BF16)] * 2
        work = totals + [((rows, width), BF16)] * 2 + work
    else:
        outs += totals
        parts = 0
    kernel = functools.partial(attention_back_kernel, len(keys), len(sums), parts, extra, scale)
    out = hbm_call(kernel, "attention_back", outs, args, 12, work, smem=1)
    return out[: len(keys)], out[len(keys) :]


def token_back_kernel(count, flow, tok_ref, gain_ref, *refs):
    flow.need(tok_ref, gain_ref, *refs[:count])
    for start, size in cuts(tok_ref.shape[0], 256):
        rows = pl.ds(start, size)
        unit, inverse = norm_parts(tok_ref[rows, :].astype(F32))
        total = refs[0][rows, :].astype(F32)
        for ref in refs[1:count]:
            total = total + ref[rows, :].astype(F32)
        refs[count][rows, :] = norm_back(total, unit, inverse, gain_ref[...])
        flow.emit(refs[count], rows)


def token_back(tok, gain, parts):
    args = (tok, gain, *parts)
    [out] = hbm_call(functools.partial(token_back_kernel, len(parts)), "token_back", [(tok.shape, F32)], args, 8, stores=len(cuts(tok.shape[0], 256)))
    return out


def picks(shape, scenes, scene, transposed=False):
    along = lax.broadcasted_iota(jnp.int32, shape, 1 if transposed else 0)
    across = lax.broadcasted_iota(jnp.int32, shape, 0 if transposed else 1)
    return jnp.where(across == along * scenes + scene, 1.0, 0.0).astype(BF16)


def sort_kernel(flow, info_ref, rows_ref, *out_refs):
    flow.need(rows_ref)
    for k, ref in enumerate(out_refs):
        scenes, some = len(out_refs), ref.shape[0] // len(out_refs)
        take = picks((some, some * scenes), scenes, info_ref[0] ^ k)
        for first in range(0, ref.shape[0], some):
            given = rows_ref[pl.ds(first * scenes, some * scenes), :]
            ref[pl.ds(first, some), :] = dot(take, given).astype(BF16)
        flow.emit(ref)


def sort_rows(info, value, scenes):
    rows, width = value.shape
    return hbm_call(sort_kernel, "sort_rows", [((rows // scenes, width), BF16)] * scenes, (info, value), 16, smem=1)


def unsort_kernel(scenes, flow, info_ref, *refs):
    *in_refs, out_ref = refs
    flow.need(*in_refs)
    if len(in_refs) == 1:
        size = out_ref.shape[0] // scenes
        in_refs = [in_refs[0].at[pl.ds(k * size, size)] for k in range(scenes)]
    rows, part = out_ref.shape[0], in_refs[0].shape[0]
    step = rows // scenes
    for start in range(0, rows, step):
        total = None
        for k, ref in enumerate(in_refs):
            some = part // scenes
            first = start // scenes
            put = picks((step, some), scenes, info_ref[0] ^ k, transposed=True)
            value = dot(put, ref[pl.ds(first, some), :])
            total = value if total is None else total + value
        out_ref[pl.ds(start, step), :] = total.astype(out_ref.dtype)
        flow.emit(out_ref, pl.ds(start, step))


def unsort_rows(info, parts, scenes, dtype):
    rows, width = sum(p.shape[0] for p in parts), parts[0].shape[1]
    kernel = functools.partial(unsort_kernel, scenes)
    [out] = hbm_call(kernel, "unsort_rows", [((rows, width), dtype)], (info, *parts), 16, smem=1, stores=scenes)
    return out


def split_kernel(count, place, extra, info_ref, *refs):
    in_refs, out_refs = refs[:count], refs[count:]
    rest = None
    if extra and out_refs[-1].shape[0] == extra and len(out_refs) == 2:
        *out_refs, rest = out_refs
    body = in_refs[0].shape[0] - extra
    step = body // len(out_refs)

    def total(start, rows):
        value = in_refs[0][pl.ds(start, rows), :].astype(F32)
        for ref in in_refs[1:]:
            value = value + ref[pl.ds(start, rows), :].astype(F32)
        return value.astype(BF16)

    shared = total(body, extra) if extra else None
    for k, ref in enumerate(out_refs):
        start = (info_ref[place] ^ k) * step if len(out_refs) > 1 else 0
        ref[pl.ds(0, step), :] = total(start if isinstance(start, int) else pl.multiple_of(start, 16), step)
        if extra and rest is None:
            ref[pl.ds(step, extra), :] = shared
    if rest is not None:
        rest[...] = shared


def split_sum(info, arrays, parts, place, extra):
    rows, width = arrays[0].shape
    step = (rows - extra) // parts
    if parts > 1:
        outs = [((step + extra, width), BF16)] * parts
    else:
        outs = [((step, width), BF16)] + ([((extra, width), BF16)] if extra else [])
    kernel = functools.partial(split_kernel, len(arrays), place, extra)
    return vmem_call(kernel, "split_sum", outs, (info, *arrays), 8, smem=1)


def unpack_kernel(width, count, crossed, info_ref, *refs):
    core, quad, line = info_ref[0], info_ref[1], info_ref[2]
    out_refs, (mine_ref, other_ref) = refs[2 * count : -2], refs[-2:]
    join(refs[:count], mine_ref)
    join(refs[count : 2 * count], other_ref)
    half = mine_ref.shape[0]
    lines = info_ref.shape[0] - 3
    block = half // (4 * lines)
    for h in range(2):
        for m in range(4):
            for z in range(lines):
                chip, spot = quad ^ m, line ^ z
                if crossed:
                    late = spot // (lines // 2)
                    chip = jnp.where(late == 0, chip, (chip % 2) * 2 + chip // 2)
                    spot = (late * 4 + chip) * (lines // 2) + spot % (lines // 2)
                else:
                    spot = chip * lines + spot
                rows = pl.ds(pl.multiple_of(spot * block, 16), block)
                value = jnp.where(core == h, mine_ref[rows, :].astype(F32), other_ref[rows, :].astype(F32))
                at = h * half + (m * lines + z) * block
                total = 0
                for ref in out_refs:
                    tall = ref.shape[0] * (ref.shape[1] // width)
                    if total <= at < total + tall:
                        inside = at - total
                        slab, row = inside // ref.shape[0], inside % ref.shape[0]
                        ref[pl.ds(row, block), pl.ds(slab * width, width)] = value
                    total += tall


class Sums:
    def __init__(self, seqs, blocks):
        self.seqs, self.blocks = seqs, blocks
        self.lines = blocks // 2
        seq, blk = lax.axis_index("seq"), lax.axis_index("blk")
        places = [seq % 2, (seq // 2) * 2 + blk % 2, blk // 2] + [seq * 0] * self.lines
        self.info = jnp.stack(places).astype(jnp.int32)

    def flip(self, value, seq_mask, blk_mask):
        pairs = [
            (s * self.blocks + b, (s ^ seq_mask) * self.blocks + (b ^ blk_mask))
            for s in range(self.seqs)
            for b in range(self.blocks)
        ]
        return lax.ppermute(value, ("seq", "blk"), pairs)

    def to_core(self, value):
        return self.flip(value, 1, 0)

    def to_quad(self, values):
        return [self.flip(v, 2 * (k // 2), k % 2) for k, v in enumerate(values, 1)]

    def to_line(self, values):
        return [self.flip(v, 0, 2 * k) for k, v in enumerate(values, 1)]

    def add_core(self, keep, received, extra=0):
        return split_sum(self.info, [keep, received], 4, 1, extra)

    def add_quad(self, keep, received, extra=0):
        return split_sum(self.info, [keep, *received], self.lines, 2, extra)

    def add_line(self, keep, received, extra=0):
        return split_sum(self.info, [keep, *received], 1, 0, extra)

    def unpack(self, mine, other, shapes, crossed=False):
        outs = [(shape, F32) for shape in shapes]
        rows, width = mine[0].shape
        kernel = functools.partial(unpack_kernel, width, len(mine), crossed)
        work = [((rows * len(mine), width), BF16)] * 2
        return vmem_call(kernel, "unpack", outs, (self.info, *mine, *other), 16, work, smem=1)


def after(value, *others):
    return lax.optimization_barrier((value, others))[0]


def local(
    sizes, latents, tokens, lengths, gain_lat, gain_tok, gain_mlp, w_query, w_key, w_value, w_out, w_up, w_down, d_out
):
    lat, tok, cot = latents[0], tokens[0], d_out[0]
    scene_lengths = lengths[0]
    scenes = scene_lengths.shape[0]
    seqs, blocks = sizes["seq"], sizes["blk"]
    group = blocks // scenes
    span, width = tok.shape
    hidden = w_up.shape[1]
    scale = width ** (-0.5)
    position = lax.axis_index("blk")
    scene, member = position // group, position % group
    scene_info = scene.astype(jnp.int32).reshape(1)
    gl, gt, gm = (g.reshape(1, width) for g in (gain_lat, gain_tok, gain_mlp))
    lines = [[m + group * k for k in range(scenes)] for m in range(group)]
    sums = Sums(seqs, blocks)

    def exchange(value, mask):
        return sums.flip(value, 0, mask)

    def across(values):
        return [exchange(v, group * k) if k else v for k, v in enumerate(values)]

    order = jnp.arange(scenes, dtype=jnp.int32)
    begin = jnp.sum(jnp.where(order < scene, scene_lengths, 0))
    end = begin + jnp.sum(jnp.where(order == scene, scene_lengths, 0))
    base = scene * group * span
    tail_rows = (scenes - 1) * group * span // 8
    starts = [base + (member ^ k) * span for k in [*range(1, group), 0]]
    main_info = jnp.stack([begin, end, *starts]).astype(jnp.int32)
    tail_info = jnp.stack([begin, end, base - tail_rows]).astype(jnp.int32)
    calls, size = [[0], []], 0
    for j in range(1, group + 1):
        if calls[-1] and size + span > 3 * span:
            calls.append([])
            size = 0
        calls[-1].append(j)
        size += span
    core = lax.axis_index("seq") % 2
    places = []
    for call in calls:
        spots = [v for j in call for v in (begin, end, (base - tail_rows, *starts)[j])]
        places.append(jnp.stack([core, *spots, scene]).astype(jnp.int32))

    lat_parts = sort_rows(scene_info, lat, scenes)
    others = [exchange(tok, k) for k in range(1, group)]
    lat_in = across(lat_parts)
    cot_parts = sort_rows(scene_info, after(cot, lat_parts), scenes)
    own_kv = keys_values(after(tok, cot_parts), gt, w_key, w_value)
    lat_in, others, cot_parts, own_kv, main_info, tail_info, places = lax.optimization_barrier(
        (lat_in, others, cot_parts, own_kv, main_info, tail_info, places)
    )
    cot_near = exchange(cot_parts[1], group)

    pieces = [tok, *others]
    lowest = (group * span - tail_rows) // span
    needed = []
    for owner in range(lowest, group):
        block = pieces[owner]
        for m in range(1, group):
            block = jnp.where(member == m, pieces[owner ^ m], block)
        needed.append(block)
    needed = jnp.concatenate(needed, axis=0) if len(needed) > 1 else needed[0]
    pairs = [(i, i + group) for i in range(blocks - group)]
    sent = needed[needed.shape[0] - tail_rows :]
    tail = lax.ppermute(sent, "blk", pairs)
    fresh = list(others) if group == 2 else []
    given = [own_kv] if fresh else [keys_values(piece, gt, w_key, w_value) for piece in others] + [own_kv]
    made_keys, made_values = zip(*given)
    query, acc, top, total, lat_set, weights, keys, values = attend(
        main_info, lat_in, gl, w_query, after(fresh, sent), gt, w_key, w_value, made_keys, made_values, scale
    )
    tail, query, cot_parts, cot_near = lax.optimization_barrier((tail, query, cot_parts, cot_near))

    cot_in = [cot_parts[0], cot_near, *[exchange(cot_parts[k], group * k) for k in range(2, scenes)]]
    saved, out_parts = finish(
        tail_info, scenes, lat_set, query, acc, top, total, tail, gt, w_key, w_value, gm, w_out, w_up, w_down, scale
    )
    tail_key, tail_value, tail_weight, factor, mixed, mlp, state, inner, slope = saved
    cot_in, out_parts, slope = lax.optimization_barrier((cot_in, out_parts, slope))
    out_back = across(out_parts)
    d_state, d_late, d_early, late, early_delta, keep, send, d_wo, dg_mlp = mlp_back(
        sums.info, cot_in, slope, state, mixed, mlp, inner, factor, gm, w_out, w_up, w_down
    )

    out_back, keep, send, d_early, d_late = lax.optimization_barrier((out_back, keep, send, d_early, d_late))
    received = sums.to_core(send)
    pieces = [(tail_value, tail_weight, tail, tail_key)]
    pieces += [(values[j], weights[j], piece, keys[j]) for j, piece in enumerate((*others, tok))]
    extra = 16
    d_toks, kept = [], []
    for j, call in enumerate(calls):
        some_values, some_weights, some_tokens, some_keys = zip(*[pieces[p] for p in call])
        latents = (lat_set, gl, w_query, d_state, d_wo, dg_mlp) if j == len(calls) - 1 else ()
        grads = (d_early, early_delta) if j else (d_late, late)
        some, kept = attention_back(
            places[j], query, w_key, w_value, gt, grads, some_values, some_weights, some_tokens, some_keys, kept,
            latents, scenes, extra, scale,
        )
        d_toks += some
        if j == 0:
            received, d_toks, kept = lax.optimization_barrier((received, d_toks, kept))
            keep, *sends = sums.add_core(keep, received)
            d_early = after(d_early, keep)
            received = sums.to_quad(sends)
            d_tail = lax.ppermute(d_toks[0], "blk", [(j, i) for i, j in pairs])
    received, d_tail, d_toks, kept = lax.optimization_barrier((received, d_tail, d_toks, kept))
    _, *returned, own = d_toks
    d_lat_set, small_keep, small_send = kept

    returned = dict(enumerate(returned, 1))
    own_tail = []
    for owner in range(lowest, group):
        start = owner * span - (group * span - tail_rows)
        chunk = d_tail[max(start, 0) : start + span]
        chunk = jnp.pad(chunk, ((span - chunk.shape[0], 0), (0, 0)))
        for k in range(1, group):
            returned[k] = returned[k] + jnp.where(member == owner ^ k, chunk, 0)
        own_tail.append(jnp.where(member == owner, chunk, 0))
    small_got = sums.to_core(small_send)
    keep, *sends = sums.add_quad(keep, received)
    received = sums.to_line(sends)
    returned = [exchange(after(returned[k], keep), k) for k in range(1, group)]
    output = unsort_rows(scene_info, after(out_back, keep), scenes, BF16)
    small_got, received, output = lax.optimization_barrier((small_got, received, output))
    [shard] = sums.add_line(keep, received)
    small_keep, *small_sends = sums.add_core(small_keep, small_got, extra)
    small_got = sums.to_quad(small_sends)
    block = shard
    for j in range(sums.lines.bit_length() - 1):
        far = sums.flip(block, 0, 2 << j)
        if j == sums.lines.bit_length() - 2:
            small_got, far = lax.optimization_barrier((small_got, far))
        block = jnp.concatenate([block, far], axis=0)
    half = block.shape[0] // 2
    near_a, near_b = block[:half], block[half:]
    far_a, far_b = sums.flip(near_a, 0, 1), sums.flip(near_b, 2, 0)
    small_keep, *small_sends = sums.add_quad(small_keep, small_got, extra)
    small_got = sums.to_line(small_sends)
    small_got, far_a, far_b, returned = lax.optimization_barrier((small_got, far_a, far_b, returned))
    two_a, two_b = jnp.concatenate([near_a, far_a], axis=0), jnp.concatenate([near_b, far_b], axis=0)
    last_a, last_b = sums.flip(two_a, 2, 0), sums.flip(two_b, 0, 1)
    small_shard, gains = sums.add_line(small_keep, small_got, extra)
    small_block = small_shard
    for j in range(sums.lines.bit_length() - 1):
        far = sums.flip(small_block, 0, 2 << j)
        if j == sums.lines.bit_length() - 2:
            d_tokens = token_back(tok, gt, [own, *own_tail, *after(returned, small_block)])
            far = after(far, d_tokens)
        small_block = jnp.concatenate([small_block, far], axis=0)
    other_a, other_b = sums.to_core(two_a), sums.to_core(two_b)
    last_a, last_b, small_block, other_a, other_b = lax.optimization_barrier(
        (last_a, last_b, small_block, other_a, other_b)
    )
    leaving = after(d_lat_set, small_block)
    d_lat_back = lax.all_to_all(leaving, "blk", 0, 0, axis_index_groups=lines, tiled=True)
    small_got = sums.to_quad([small_block] * 3)
    mine = [two_a, last_a, two_b, last_b]
    other = [other_a, sums.to_core(last_a), other_b, sums.to_core(last_b)]
    d_w_down, d_w_up = sums.unpack(mine, other, [(hidden, width), (width, hidden)], crossed=True)
    small_got = after(small_got, d_w_up)
    small_mine = [small_block, *small_got]
    small_other = [sums.to_core(v) for v in small_mine]
    squares = sums.unpack(small_mine, small_other, [(width, width)] * 4)
    d_latents = unsort_rows(0 * scene_info, [after(d_lat_back, *squares)], scenes, F32)
    gains = gains.astype(F32)
    return (output[None], d_latents[None], d_tokens[None], *squares, d_w_up, d_w_down, gains[0], gains[1], gains[2])


def solution(mesh):
    split = P("seq", "blk", None)
    in_specs = (split, split, P("seq", None)) + (P(),) * 9 + (split,)
    out_specs = (split,) * 3 + (P(),) * 9
    return jax.shard_map(
        functools.partial(local, dict(mesh.shape)), mesh=mesh, in_specs=in_specs, out_specs=out_specs, check_vma=False
    )
```

```python
import functools
import math

import jax
import jax.numpy as jnp
from jax import lax
from jax.experimental import pallas as pl
from jax.experimental.pallas import tpu as pltpu
from jax.sharding import PartitionSpec as P

EPSILON = 1e-05
NEGATIVE = -1e30
ROOM = (64 << 20) - (160 << 10)
LOG2E = 1.4426950408889634
GELU_C = math.sqrt(2.0 / math.pi)
GELU_A = 0.044715
F32 = jnp.float32
BF16 = jnp.bfloat16
NN = (((1,), (0,)), ((), ()))
NT = (((1,), (1,)), ((), ()))
TN = (((0,), (0,)), ((), ()))


def dot(left, right, dims=NN):
    return lax.dot_general(left, right, dims, preferred_element_type=F32)


def norm_parts(rows):
    center = rows - jnp.mean(rows, axis=-1, keepdims=True)
    spread = jnp.mean(center * center, axis=-1, keepdims=True)
    inverse = lax.rsqrt(spread + EPSILON)
    return center * inverse, inverse


def norm_back(d_normed, unit, inverse, gain):
    d_unit = d_normed * gain
    mean_d = jnp.mean(d_unit, axis=-1, keepdims=True)
    mean_p = jnp.mean(d_unit * unit, axis=-1, keepdims=True)
    return inverse * (d_unit - mean_d - unit * mean_p)


def vmem_call(kernel, name, outs, args, limit, scratch=(), smem=0):
    held = sum(math.prod(shape) * jnp.dtype(dtype).itemsize for shape, dtype in scratch)
    in_vmem = pl.BlockSpec(memory_space=pltpu.VMEM)
    in_smem = pl.BlockSpec(memory_space=pltpu.SMEM)
    return pl.pallas_call(
        kernel,
        in_specs=[in_smem] * smem + [in_vmem] * (len(args) - smem),
        out_specs=[in_vmem] * len(outs),
        out_shape=[jax.ShapeDtypeStruct(shape, dtype) for shape, dtype in outs],
        scratch_shapes=[pltpu.VMEM(shape, dtype) for shape, dtype in scratch],
        compiler_params=pltpu.CompilerParams(vmem_limit_bytes=(limit << 20) + held),
        cost_estimate=pl.CostEstimate(flops=0, bytes_accessed=0, transcendentals=0),
        name=name,
    )(*args)


class Flow:
    AHEAD = 64 << 20

    def __init__(self, loads, stores, semaphores):
        self.loads = loads
        self.stores = stores
        self.semaphores = semaphores
        self.started = 0
        self.waiting = set(range(len(loads)))
        self.begun = []
        self.whole = set()
        self.start_more(-1)

    def start_more(self, least):
        def size(j):
            held = self.loads[j][1]
            return math.prod(held.shape) * jnp.dtype(held.dtype).itemsize

        flying = sum(size(j) for j in self.waiting if j < self.started)
        while self.started < len(self.loads) and (self.started <= least or flying + size(self.started) <= self.AHEAD):
            flying += size(self.started)
            self.loads[self.started][2].start()
            self.started += 1

    def need(self, *refs):
        wanted = [j for j, load in enumerate(self.loads) if j in self.waiting and any(load[1] is r for r in refs)]
        for j in wanted:
            self.start_more(j)
        for j in wanted:
            self.waiting.discard(j)
            self.loads[j][2].wait()
        self.start_more(-1)

    def need_block(self, ref, number):
        j = [i for i, load in enumerate(self.loads) if load[1] is ref][number]
        self.start_more(j)
        if j in self.waiting:
            self.waiting.discard(j)
            self.loads[j][2].wait()

    def emit(self, ref, *where):
        for j, (out, held) in enumerate(self.stores):
            if held is ref:
                self.whole.add(j)
                source, target = (held.at[where], out.at[where]) if where else (held, out)
                copy = pltpu.make_async_copy(source, target, self.semaphores.at[len(self.begun)])
                copy.start()
                self.begun.append(copy)

    def close(self):
        self.need(*[held for _, held, _ in self.loads])
        for j, (_, held) in enumerate(self.stores):
            if j not in self.whole:
                self.emit(held)
        for copy in self.begun:
            copy.wait()


def hbm_call(kernel, name, outs, args, limit, scratch=(), smem=0, fixed_in=(), fixed_out=(), stores=None, blocks=()):
    arrays = args[smem:]
    moves_in = [j for j in range(len(arrays)) if j not in fixed_in]
    moves_out = [j for j in range(len(outs)) if j not in fixed_out]
    held = [(arrays[j].shape, arrays[j].dtype) for j in moves_in] + [outs[j] for j in moves_out] + list(scratch)
    size = sum(math.prod(shape) * jnp.dtype(dtype).itemsize for shape, dtype in held)

    resident = [(arrays[j].shape, arrays[j].dtype) for j in fixed_in] + [outs[j] for j in fixed_out]
    rest = sum(math.prod(shape) * jnp.dtype(dtype).itemsize for shape, dtype in resident)
    limit = max((limit << 20) + size, ROOM - rest)
    more = sum(len(cuts(arrays[j].shape[0], 256)) - 1 for j in blocks)

    def body(*refs):
        scalars, refs = refs[:smem], refs[smem:]
        ins, refs = list(refs[: len(arrays)]), refs[len(arrays) :]
        results, refs = list(refs[: len(outs)]), refs[len(outs) :]
        *kept, load_sems, store_sems = refs
        loads, kept_out = [], []
        for n, j in enumerate(moves_in):
            for first, rows in cuts(arrays[j].shape[0], 256 if j in blocks else arrays[j].shape[0]):
                source, target = ins[j], kept[n]
                if j in blocks:
                    source, target = source.at[pl.ds(first, rows)], target.at[pl.ds(first, rows)]
                copy = pltpu.make_async_copy(source, target, load_sems.at[len(loads)])
                loads.append((ins[j], kept[n], copy))
            ins[j] = kept[n]
        kept = kept[len(moves_in) :]
        for n, j in enumerate(moves_out):
            kept_out.append((results[j], kept[n]))
            results[j] = kept[n]
        flow = Flow(loads, kept_out, store_sems)
        kernel(flow, *scalars, *ins, *results, *kept[len(moves_out) :])
        flow.close()

    def place(count, fixed):
        return [pl.BlockSpec(memory_space=pltpu.VMEM if j in fixed else pl.ANY) for j in range(count)]

    return pl.pallas_call(
        body,
        in_specs=[pl.BlockSpec(memory_space=pltpu.SMEM)] * smem + place(len(arrays), fixed_in),
        out_specs=place(len(outs), fixed_out),
        out_shape=[jax.ShapeDtypeStruct(shape, dtype) for shape, dtype in outs],
        scratch_shapes=[pltpu.VMEM(shape, dtype) for shape, dtype in held]
        + [pltpu.SemaphoreType.DMA((max(len(moves_in) + more, 1),)), pltpu.SemaphoreType.DMA((max(stores or len(moves_out), 1),))],
        compiler_params=pltpu.CompilerParams(vmem_limit_bytes=min(limit, ROOM)),
        cost_estimate=pl.CostEstimate(flops=0, bytes_accessed=0, transcendentals=0),
        name=name,
    )(*args)


def cuts(size, step):
    return [(i, min(step, size - i)) for i in range(0, size, step)]


def fold(rows):
    return jnp.sum(rows.reshape(rows.shape[0] // 8, 8, rows.shape[1]), axis=0)


def column_of(row):
    return jnp.transpose(jnp.broadcast_to(row, (8, row.shape[1])))[:, :1]


def row_of(column):
    return jnp.transpose(jnp.broadcast_to(column, (column.shape[0], 128)))[:8, :]


def join(refs, whole_ref):
    part = refs[0].shape[0]
    for j, ref in enumerate(refs):
        whole_ref[pl.ds(j * part, part), :] = ref[...]


def line_store(ref, scenes, scene, start, value):
    part = ref.shape[0] // scenes
    size = min(part, value.shape[0])
    for first in range(0, value.shape[0], size):
        at = start + first
        place = (scene ^ (at // part)) * part + at % part
        ref[pl.ds(pl.multiple_of(place, 16), size), :] = value[first : first + size]


def part_store(refs, start, value):
    part = refs[0].shape[0]
    size = min(part, value.shape[0])
    for first in range(0, value.shape[0], size):
        at = start + first
        refs[at // part][pl.ds(at % part, size), :] = value[first : first + size]


def kv_kernel(flow, tok_ref, gain_ref, wk_ref, wv_ref, k_ref, v_ref):
    flow.need(tok_ref, gain_ref, wk_ref, wv_ref)
    for start, size in cuts(tok_ref.shape[0], 256):
        rows = pl.ds(start, size)
        unit, _ = norm_parts(tok_ref[rows, :].astype(F32))
        low = (unit * gain_ref[...]).astype(BF16)
        k_ref[rows, :] = dot(low, wk_ref[...]).astype(BF16)
        v_ref[rows, :] = dot(low, wv_ref[...]).astype(BF16)
    flow.emit(k_ref)
    flow.emit(v_ref)


def keys_values(tok, gain, w_key, w_value):
    return hbm_call(kv_kernel, "keys_values", [(tok.shape, BF16)] * 2, (tok, gain, w_key, w_value), 8)


def score_piece(info_ref, p, k_ref, s_ref, query, columns, top, scale):
    begin, end = info_ref[0], info_ref[1]
    for start, size in cuts(k_ref.shape[0], 512):
        s = dot(k_ref[pl.ds(start, size), :], query, NT) * (scale * LOG2E)
        place = info_ref[2 + p] + start + lax.broadcasted_iota(jnp.int32, (size, 1), 0)
        s = s + jnp.where((place >= begin) & (place < end), 0.0, NEGATIVE)
        s_ref[pl.ds(start, size), columns] = s
        top = jnp.maximum(top, jnp.max(s.reshape(size // 8, 8, s.shape[1]), axis=0))
    return top


def weigh_piece(v_ref, s_ref, w_ref, columns, top, total, acc):
    for start, size in cuts(v_ref.shape[0], 512):
        w = jnp.exp2(s_ref[pl.ds(start, size), columns] - top)
        total = total + fold(w)
        w_ref[pl.ds(start, size), columns] = w.astype(BF16)
    part = dot(w_ref[:, columns], v_ref[...], TN)
    return total, part if acc is None else acc + part


def attend_kernel(parts, fresh, count, scale, flow, info_ref, gl_ref, wq_ref, *refs):
    new, refs = refs[: 3 * bool(fresh) + fresh], refs[3 * bool(fresh) + fresh :]
    lat_refs, refs = refs[:parts], refs[parts:]
    given = count - fresh
    k_refs, v_refs, refs = refs[:given], refs[given : 2 * given], refs[2 * given :]
    q_ref, acc_ref, top_ref, tot_ref, lat_ref = refs[:5]
    refs = refs[5:]
    k_refs, v_refs, refs = refs[:fresh] + k_refs, refs[fresh : 2 * fresh] + v_refs, refs[2 * fresh :]
    w_refs, s_refs = refs[:count], refs[count:]
    flow.need(*lat_refs, gl_ref, wq_ref)
    join(lat_refs, lat_ref)
    for j in range(fresh):
        kv_kernel(flow, new[3 + j], *new[:3], k_refs[j], v_refs[j])
    for start, size in cuts(lat_ref.shape[0], 512):
        rows = columns = pl.ds(start, size)
        unit, _ = norm_parts(lat_ref[rows, :].astype(F32))
        query = dot((unit * gl_ref[...]).astype(BF16), wq_ref[...]).astype(BF16)
        q_ref[rows, :] = query
        flow.need(*k_refs)
        top = jnp.full((8, size), NEGATIVE, F32)
        for p in range(count):
            top = score_piece(info_ref, p, k_refs[p], s_refs[p], query, columns, top, scale)
        top = jnp.max(top, axis=0, keepdims=True)
        total, acc = jnp.zeros((8, size), F32), None
        flow.need(*v_refs)
        for p in range(count):
            total, acc = weigh_piece(v_refs[p], s_refs[p], w_refs[p], columns, top, total, acc)
        acc_ref[rows, :] = acc
        if start == 0:
            flow.emit(lat_ref)
        for p in range(count):
            flow.emit(w_refs[p], slice(None), columns)
        flow.emit(acc_ref, rows)
        top_ref[:, columns] = jnp.broadcast_to(top, (8, size))
        tot_ref[:, columns] = total


def attend(info, lats, gl, wq, fresh, gt, wk, wv, keys, values, scale):
    rows, width = len(lats) * lats[0].shape[0], lats[0].shape[1]
    made = [(t.shape, BF16) for t in fresh]
    pieces = [t.shape[0] for t in (*fresh, *keys)]
    outs = [((rows, width), BF16), ((rows, width), F32), ((8, rows), F32), ((8, rows), F32), ((rows, width), BF16)]
    outs += made * 2 + [((n, rows), BF16) for n in pieces]
    new = (gt, wk, wv, *fresh) if fresh else ()
    q, acc, top, total, lat, *rest = hbm_call(
        functools.partial(attend_kernel, len(lats), len(fresh), len(pieces), scale),
        "attend",
        outs,
        (info, gl, wq, *new, *lats, *keys, *values),
        12,
        [((n, rows), F32) for n in pieces],
        smem=1,
        stores=len(outs) + (len(cuts(rows, 512)) - 1) * (len(pieces) + 1),
    )
    more = len(fresh)
    return q, acc, top, total, lat, rest[2 * more :], (*rest[:more], *keys), (*rest[more : 2 * more], *values)


def finish_kernel(
    scale, flow, info_ref, tok_ref, gt_ref, wk_ref, wv_ref, top_ref, q_ref, tot_ref, acc_ref, lat_ref, gm_ref, wo_ref, wu_ref, wd_ref,
    k_ref, v_ref, w_ref, factor_ref, mixed_ref, mlp_ref, state_ref, inner_ref, slope_ref, *refs,
):
    *out_refs, s_ref = refs
    kv_kernel(flow, tok_ref, gt_ref, wk_ref, wv_ref, k_ref, v_ref)
    flow.need(top_ref, q_ref, tot_ref, acc_ref)
    hidden = wu_ref.shape[1]
    for start, size in cuts(lat_ref.shape[0], 512):
        rows = columns = pl.ds(start, size)
        old = top_ref[:1, columns]
        top = jnp.broadcast_to(old, (8, size))
        top = score_piece(info_ref, 0, k_ref, s_ref, q_ref[rows, :], columns, top, scale)
        top = jnp.max(top, axis=0, keepdims=True)
        total, acc = weigh_piece(v_ref, s_ref, w_ref, columns, top, jnp.zeros((8, size), F32), None)
        shrink = jnp.exp2(old - top)
        total = jnp.sum(total, axis=0, keepdims=True) + jnp.sum(tot_ref[:, columns], axis=0, keepdims=True) * shrink
        inverse = 1.0 / total
        late, early = column_of(inverse), column_of(shrink * inverse)
        lane = lax.broadcasted_iota(jnp.int32, (size, 128), 1)
        factor_ref[rows, :] = jnp.where(lane == 0, late, early)
        mixed_ref[rows, :] = (acc * late + acc_ref[rows, :] * early).astype(BF16)
    for ref in (w_ref, factor_ref, mixed_ref):
        flow.emit(ref)
    flow.need(lat_ref, wo_ref, gm_ref, wu_ref, wd_ref)
    for start, size in cuts(lat_ref.shape[0], 256):
        rows = pl.ds(start, size)
        state = lat_ref[rows, :].astype(F32) + dot(mixed_ref[rows, :], wo_ref[...])
        state_ref[rows, :] = state
        unit, _ = norm_parts(state)
        low = (unit * gm_ref[...]).astype(BF16)
        mlp_ref[rows, :] = low
        out = state
        for first, step in cuts(hidden, 512):
            some = pl.ds(first, step)
            u = dot(low, wu_ref[:, some])
            square = u * u
            t = jnp.tanh(u * (GELU_C + (GELU_C * GELU_A) * square))
            half = 0.5 + 0.5 * t
            inner = (u * half).astype(BF16)
            bend = u * ((0.5 * GELU_C) + (1.5 * GELU_C * GELU_A) * square)
            inner_ref[rows, some] = inner
            slope_ref[rows, some] = (half + bend * (1.0 - t * t)).astype(BF16)
            out = out + dot(inner, wd_ref[some, :])
        part_store(out_refs, start, out.astype(BF16))
        for ref in (state_ref, mlp_ref, inner_ref, slope_ref):
            flow.emit(ref, rows)


def finish(info, parts, lat, q, acc, top, total, tail, gt, wk, wv, gm, wo, wu, wd, scale):
    rows, width = lat.shape
    hidden = wu.shape[1]
    tall = (rows, width)
    outs = [(tail.shape, BF16)] * 2 + [((tail.shape[0], rows), BF16), ((rows, 128), F32), (tall, BF16), (tall, BF16), (tall, F32)]
    outs += [((rows, hidden), BF16)] * 2 + [((rows // parts, width), BF16)] * parts
    out = hbm_call(
        functools.partial(finish_kernel, scale),
        "finish",
        outs,
        (info, tail, gt, wk, wv, top, q, total, acc, lat, gm, wo, wu, wd),
        22,
        [((tail.shape[0], rows), F32)],
        smem=1,
        stores=len(outs) + 4 * (len(cuts(rows, 256)) - 1),
    )
    return out[:9], out[9:]


def mlp_back_kernel(
    parts, flow, info_ref, *refs,
):
    cot_refs, refs = refs[:parts], refs[parts:]
    wd_ref, wu_ref, slope_ref, state_ref, mixed_ref, factor_ref, gm_ref, wo_ref, inner_ref, mlp_ref, *refs = refs
    dstate_ref, late_ref, early_ref, dlate_ref, dearly_ref, keep_ref, send_ref, dwo_ref, dgain_ref = refs[:9]
    dpre_ref, dproj_ref, cot_ref = refs[9:]
    flow.need(*cot_refs, wd_ref)
    join(cot_refs, cot_ref)
    hidden, width = wd_ref.shape

    def pack(half, first, value):
        rows = pl.ds(first, value.shape[0])

        @pl.when(info_ref[0] == half)
        def _():
            keep_ref[rows, :] = value.astype(BF16)

        @pl.when(info_ref[0] != half)
        def _():
            send_ref[rows, :] = value.astype(BF16)

    total = jnp.zeros((8, width), F32)
    for start, size in cuts(cot_ref.shape[0], 256):
        rows = pl.ds(start, size)
        cot = cot_ref[rows, :]
        flow.need_block(slope_ref, start // 256)
        d_mlp = None
        for first, step in cuts(hidden, 512):
            some = pl.ds(first, step)
            d_inner = dot(cot, wd_ref[some, :], NT)
            d_pre = (slope_ref[rows, some].astype(F32) * d_inner).astype(BF16)
            dpre_ref[rows, some] = d_pre
            flow.need(wu_ref)
            part = dot(d_pre, wu_ref[:, some], NT)
            d_mlp = part if d_mlp is None else d_mlp + part
        flow.need(gm_ref, wo_ref, state_ref, mixed_ref, factor_ref)
        unit, inverse = norm_parts(state_ref[rows, :])
        total = total + fold(d_mlp * unit)
        d_state = cot.astype(F32) + norm_back(d_mlp, unit, inverse, gm_ref[...])
        dstate_ref[rows, :] = d_state
        d_proj = d_state.astype(BF16)
        dproj_ref[rows, :] = d_proj
        d_att = dot(d_proj, wo_ref[...], NT)
        mixed = mixed_ref[rows, :].astype(F32)
        for lane, part_ref, delta_ref in ((0, late_ref, dlate_ref), (1, early_ref, dearly_ref)):
            part = (d_att * factor_ref[rows, lane : lane + 1]).astype(BF16)
            part_ref[rows, :] = part
            delta = jnp.sum(part.astype(F32) * mixed, axis=-1, keepdims=True)
            delta_ref[:, rows] = row_of(delta)
    dgain_ref[...] = total
    for ref in (dstate_ref, late_ref, early_ref, dlate_ref, dearly_ref):
        flow.emit(ref)
    flow.need(inner_ref, mlp_ref)
    for first, step in cuts(hidden, 512):
        pack(0, first, dot(inner_ref[:, first : first + step], cot_ref[...], TN))
    for first, step in cuts(hidden, 512):
        pack(1, first, dot(mlp_ref[...], dpre_ref[:, first : first + step], TN))
    dwo_ref[...] = dot(mixed_ref[...], dproj_ref[...], TN).astype(BF16)


def mlp_back(info, cots, slope, state, mixed, mlp, inner, factor, gm, wo, wu, wd):
    rows, width = state.shape
    hidden = wu.shape[1]
    tall, flat = (rows, width), (8, rows)
    outs = [(tall, F32), (tall, BF16), (tall, BF16), (flat, F32), (flat, F32)]
    outs += [((hidden, width), BF16)] * 2 + [((width, width), BF16), ((8, width), F32)]
    return hbm_call(
        functools.partial(mlp_back_kernel, len(cots)),
        "mlp_back",
        outs,
        (info, *cots, wd, wu, slope, state, mixed, factor, gm, wo, inner, mlp),
        20,
        [((rows, hidden), BF16), (tall, BF16), (tall, BF16)],
        smem=1,
        blocks=(len(cots) + 2,),
    )


def attention_back_kernel(count, start, parts, extra, scale, flow, info_ref, *refs):
    q_ref, wk_ref, wv_ref, gain_ref, *refs = refs
    datt_ref, delta_ref, *refs = refs
    v_refs, w_refs, t_refs, k_refs = (refs[j : 4 * count : 4] for j in range(4))
    refs = refs[4 * count :]
    sums, refs = refs[:start], refs[start:]
    if parts:
        lat_ref, gl_ref, wq_ref, dstate_ref, dwo_ref, dgmlp_ref, *refs = refs
    dtok_refs, refs = refs[:count], refs[count:]
    if parts:
        dlat_ref, *refs = refs
        keep_ref, send_ref, dq_ref, akey_ref, aval_ref, dgain_ref, latlow_ref, dquery_ref, *refs = refs
    else:
        dq_ref, akey_ref, aval_ref, dgain_ref, *refs = refs
    dscore_ref, low_ref, dkey_ref, dval_ref, part_ref = refs
    totals = (dq_ref, akey_ref, aval_ref, dgain_ref)
    flow.need(q_ref, wk_ref, wv_ref, gain_ref)
    for p in range(count):
        size = k_refs[p].shape[0]
        flow.need(datt_ref, delta_ref, v_refs[p], w_refs[p], t_refs[p], k_refs[p])
        begin, end, first_place = info_ref[1 + 3 * p], info_ref[2 + 3 * p], info_ref[3 + 3 * p]
        part_ref[...] = jnp.zeros_like(part_ref)
        for first, step in cuts(size, 256):
            rows = pl.ds(first, step)
            active = (first_place + first < end) & (first_place + first + step > begin)

            @pl.when(active)
            def _(p=p, rows=rows):
                d_prob = dot(v_refs[p][rows, :], datt_ref[...], NT)
                d_score = (w_refs[p][rows, :].astype(F32) * (d_prob - delta_ref[:1, :])).astype(BF16)
                dscore_ref[rows, :] = d_score
                d_key = (dot(d_score, q_ref[...]) * scale).astype(BF16)
                d_value = dot(w_refs[p][rows, :], datt_ref[...]).astype(BF16)
                dkey_ref[rows, :] = d_key
                dval_ref[rows, :] = d_value
                unit, _ = norm_parts(t_refs[p][rows, :].astype(F32))
                low_ref[rows, :] = (unit * gain_ref[...]).astype(BF16)
                d_tok = dot(d_key, wk_ref[...], NT) + dot(d_value, wv_ref[...], NT)
                dtok_refs[p][rows, :] = d_tok.astype(BF16)
                part_ref[...] += fold(d_tok * unit)

            @pl.when(jnp.logical_not(active))
            def _(p=p, rows=rows):
                for ref in (dscore_ref, dkey_ref, dval_ref, low_ref, dtok_refs[p]):
                    ref[rows, :] = jnp.zeros((rows.size, ref.shape[1]), BF16)

        flow.emit(dtok_refs[p])
        dgain = part_ref[...]
        here = pl.ds(0, size)
        news = (
            dot(dscore_ref[here, :], k_refs[p][...], TN),
            dot(low_ref[here, :], dkey_ref[here, :], TN),
            dot(low_ref[here, :], dval_ref[here, :], TN),
            dgain,
        )
        if p == 0:
            flow.need(*sums)
        for j, (ref, value) in enumerate(zip(totals, news)):
            if p == 0:
                ref[...] = value + sums[j][...] if sums else value
            else:
                ref[...] += value
    if not parts:
        return
    flow.need(lat_ref, gl_ref, wq_ref, dstate_ref, dwo_ref, dgmlp_ref)
    total = None
    width = wq_ref.shape[0]
    for first, size in cuts(lat_ref.shape[0], 256):
        rows = pl.ds(first, size)
        unit, inverse = norm_parts(lat_ref[rows, :].astype(F32))
        gain = gl_ref[...]
        latlow_ref[rows, :] = (unit * gain).astype(BF16)
        d_query = (dq_ref[rows, :] * scale).astype(BF16)
        dquery_ref[rows, :] = d_query
        d_low = dot(d_query, wq_ref[...], NT)
        line_store(dlat_ref, parts, info_ref[1 + 3 * count], first, (dstate_ref[rows, :] + norm_back(d_low, unit, inverse, gain)).astype(BF16))
        part = fold(d_low * unit)
        total = part if total is None else total + part
    flow.emit(dlat_ref)
    d_wq = dot(latlow_ref[...], dquery_ref[...], TN)
    gains = [jnp.sum(g, axis=0, keepdims=True) for g in (total, dgain_ref[...], dgmlp_ref[...])]
    line = lax.broadcasted_iota(jnp.int32, (extra, width), 0)
    block = jnp.where(line == 0, gains[0], jnp.where(line == 1, gains[1], jnp.where(line == 2, gains[2], 0.0)))
    halves = ((d_wq, akey_ref), (aval_ref, dwo_ref))
    for ref, core in ((keep_ref, info_ref[0]), (send_ref, 1 - info_ref[0])):
        ref[pl.ds(2 * width, extra), :] = block.astype(BF16)
        for h, half in enumerate(halves):

            @pl.when(core == h)
            def _(ref=ref, half=half):
                for j, piece in enumerate(half):
                    ref[pl.ds(j * width, width), :] = piece[...].astype(BF16)


def attention_back(info, q, wk, wv, gain, grads, values, weights, tokens, keys, sums, latents, parts, extra, scale):
    rows, width = q.shape
    square = ((width, width), F32)
    totals = [((rows, width), F32), square, square, ((8, width), F32)]
    most = max(k.shape[0] for k in keys)
    work = [((most, rows), BF16)] + [((most, width), BF16)] * 3 + [((8, width), F32)]
    outs = [(k.shape, BF16) for k in keys]
    by_piece = [a for piece in zip(values, weights, tokens, keys) for a in piece]
    args = (info, q, wk, wv, gain, *grads, *by_piece, *sums)
    if latents:
        args = (*args, *latents)
        outs += [((rows, width), BF16)] + [((2 * width + extra, width), BF16)] * 2
        work = totals + [((rows, width), BF16)] * 2 + work
    else:
        outs += totals
        parts = 0
    kernel = functools.partial(attention_back_kernel, len(keys), len(sums), parts, extra, scale)
    out = hbm_call(kernel, "attention_back", outs, args, 12, work, smem=1)
    return out[: len(keys)], out[len(keys) :]


def token_back_kernel(count, flow, tok_ref, gain_ref, *refs):
    flow.need(tok_ref, gain_ref, *refs[:count])
    for start, size in cuts(tok_ref.shape[0], 256):
        rows = pl.ds(start, size)
        unit, inverse = norm_parts(tok_ref[rows, :].astype(F32))
        total = refs[0][rows, :].astype(F32)
        for ref in refs[1:count]:
            total = total + ref[rows, :].astype(F32)
        refs[count][rows, :] = norm_back(total, unit, inverse, gain_ref[...])
        flow.emit(refs[count], rows)


def token_back(tok, gain, parts):
    args = (tok, gain, *parts)
    [out] = hbm_call(functools.partial(token_back_kernel, len(parts)), "token_back", [(tok.shape, F32)], args, 8, stores=len(cuts(tok.shape[0], 256)))
    return out


def picks(shape, scenes, scene, transposed=False):
    along = lax.broadcasted_iota(jnp.int32, shape, 1 if transposed else 0)
    across = lax.broadcasted_iota(jnp.int32, shape, 0 if transposed else 1)
    return jnp.where(across == along * scenes + scene, 1.0, 0.0).astype(BF16)


def sort_kernel(flow, info_ref, rows_ref, *out_refs):
    flow.need(rows_ref)
    for k, ref in enumerate(out_refs):
        scenes, some = len(out_refs), ref.shape[0] // len(out_refs)
        take = picks((some, some * scenes), scenes, info_ref[0] ^ k)
        for first in range(0, ref.shape[0], some):
            given = rows_ref[pl.ds(first * scenes, some * scenes), :]
            ref[pl.ds(first, some), :] = dot(take, given).astype(BF16)
        flow.emit(ref)


def sort_rows(info, value, scenes):
    rows, width = value.shape
    return hbm_call(sort_kernel, "sort_rows", [((rows // scenes, width), BF16)] * scenes, (info, value), 16, smem=1)


def unsort_kernel(scenes, flow, info_ref, *refs):
    *in_refs, out_ref = refs
    flow.need(*in_refs)
    if len(in_refs) == 1:
        size = out_ref.shape[0] // scenes
        in_refs = [in_refs[0].at[pl.ds(k * size, size)] for k in range(scenes)]
    rows, part = out_ref.shape[0], in_refs[0].shape[0]
    step = rows // scenes
    for start in range(0, rows, step):
        total = None
        for k, ref in enumerate(in_refs):
            some = part // scenes
            first = start // scenes
            put = picks((step, some), scenes, info_ref[0] ^ k, transposed=True)
            value = dot(put, ref[pl.ds(first, some), :])
            total = value if total is None else total + value
        out_ref[pl.ds(start, step), :] = total.astype(out_ref.dtype)
        flow.emit(out_ref, pl.ds(start, step))


def unsort_rows(info, parts, scenes, dtype):
    rows, width = sum(p.shape[0] for p in parts), parts[0].shape[1]
    kernel = functools.partial(unsort_kernel, scenes)
    [out] = hbm_call(kernel, "unsort_rows", [((rows, width), dtype)], (info, *parts), 16, smem=1, stores=scenes)
    return out


def split_kernel(count, place, extra, info_ref, *refs):
    in_refs, out_refs = refs[:count], refs[count:]
    rest = None
    if extra and out_refs[-1].shape[0] == extra and len(out_refs) == 2:
        *out_refs, rest = out_refs
    body = in_refs[0].shape[0] - extra
    step = body // len(out_refs)

    def total(start, rows):
        value = in_refs[0][pl.ds(start, rows), :].astype(F32)
        for ref in in_refs[1:]:
            value = value + ref[pl.ds(start, rows), :].astype(F32)
        return value.astype(BF16)

    shared = total(body, extra) if extra else None
    for k, ref in enumerate(out_refs):
        start = (info_ref[place] ^ k) * step if len(out_refs) > 1 else 0
        ref[pl.ds(0, step), :] = total(start if isinstance(start, int) else pl.multiple_of(start, 16), step)
        if extra and rest is None:
            ref[pl.ds(step, extra), :] = shared
    if rest is not None:
        rest[...] = shared


def split_sum(info, arrays, parts, place, extra):
    rows, width = arrays[0].shape
    step = (rows - extra) // parts
    if parts > 1:
        outs = [((step + extra, width), BF16)] * parts
    else:
        outs = [((step, width), BF16)] + ([((extra, width), BF16)] if extra else [])
    kernel = functools.partial(split_kernel, len(arrays), place, extra)
    return vmem_call(kernel, "split_sum", outs, (info, *arrays), 8, smem=1)


def unpack_kernel(width, count, crossed, info_ref, *refs):
    core, quad, line = info_ref[0], info_ref[1], info_ref[2]
    out_refs, (mine_ref, other_ref) = refs[2 * count : -2], refs[-2:]
    join(refs[:count], mine_ref)
    join(refs[count : 2 * count], other_ref)
    half = mine_ref.shape[0]
    lines = info_ref.shape[0] - 3
    block = half // (4 * lines)
    for h in range(2):
        for m in range(4):
            for z in range(lines):
                chip, spot = quad ^ m, line ^ z
                if crossed:
                    late = spot // (lines // 2)
                    chip = jnp.where(late == 0, chip, (chip % 2) * 2 + chip // 2)
                    spot = (late * 4 + chip) * (lines // 2) + spot % (lines // 2)
                else:
                    spot = chip * lines + spot
                rows = pl.ds(pl.multiple_of(spot * block, 16), block)
                value = jnp.where(core == h, mine_ref[rows, :].astype(F32), other_ref[rows, :].astype(F32))
                at = h * half + (m * lines + z) * block
                total = 0
                for ref in out_refs:
                    tall = ref.shape[0] * (ref.shape[1] // width)
                    if total <= at < total + tall:
                        inside = at - total
                        slab, row = inside // ref.shape[0], inside % ref.shape[0]
                        ref[pl.ds(row, block), pl.ds(slab * width, width)] = value
                    total += tall


class Sums:
    def __init__(self, seqs, blocks):
        self.seqs, self.blocks = seqs, blocks
        self.lines = blocks // 2
        seq, blk = lax.axis_index("seq"), lax.axis_index("blk")
        places = [seq % 2, (seq // 2) * 2 + blk % 2, blk // 2] + [seq * 0] * self.lines
        self.info = jnp.stack(places).astype(jnp.int32)

    def flip(self, value, seq_mask, blk_mask):
        pairs = [
            (s * self.blocks + b, (s ^ seq_mask) * self.blocks + (b ^ blk_mask))
            for s in range(self.seqs)
            for b in range(self.blocks)
        ]
        return lax.ppermute(value, ("seq", "blk"), pairs)

    def to_core(self, value):
        return self.flip(value, 1, 0)

    def to_quad(self, values):
        return [self.flip(v, 2 * (k // 2), k % 2) for k, v in enumerate(values, 1)]

    def to_line(self, values):
        return [self.flip(v, 0, 2 * k) for k, v in enumerate(values, 1)]

    def add_core(self, keep, received, extra=0):
        return split_sum(self.info, [keep, received], 4, 1, extra)

    def add_quad(self, keep, received, extra=0):
        return split_sum(self.info, [keep, *received], self.lines, 2, extra)

    def add_line(self, keep, received, extra=0):
        return split_sum(self.info, [keep, *received], 1, 0, extra)

    def unpack(self, mine, other, shapes, crossed=False):
        outs = [(shape, F32) for shape in shapes]
        rows, width = mine[0].shape
        kernel = functools.partial(unpack_kernel, width, len(mine), crossed)
        work = [((rows * len(mine), width), BF16)] * 2
        return vmem_call(kernel, "unpack", outs, (self.info, *mine, *other), 16, work, smem=1)


def after(value, *others):
    return lax.optimization_barrier((value, others))[0]


def local(
    sizes, latents, tokens, lengths, gain_lat, gain_tok, gain_mlp, w_query, w_key, w_value, w_out, w_up, w_down, d_out
):
    lat, tok, cot = latents[0], tokens[0], d_out[0]
    scene_lengths = lengths[0]
    scenes = scene_lengths.shape[0]
    seqs, blocks = sizes["seq"], sizes["blk"]
    group = blocks // scenes
    span, width = tok.shape
    hidden = w_up.shape[1]
    scale = width ** (-0.5)
    position = lax.axis_index("blk")
    scene, member = position // group, position % group
    scene_info = scene.astype(jnp.int32).reshape(1)
    gl, gt, gm = (g.reshape(1, width) for g in (gain_lat, gain_tok, gain_mlp))
    lines = [[m + group * k for k in range(scenes)] for m in range(group)]
    sums = Sums(seqs, blocks)

    def exchange(value, mask):
        return sums.flip(value, 0, mask)

    def across(values):
        return [exchange(v, group * k) if k else v for k, v in enumerate(values)]

    order = jnp.arange(scenes, dtype=jnp.int32)
    begin = jnp.sum(jnp.where(order < scene, scene_lengths, 0))
    end = begin + jnp.sum(jnp.where(order == scene, scene_lengths, 0))
    base = scene * group * span
    tail_rows = (scenes - 1) * group * span // 8
    starts = [base + (member ^ k) * span for k in [*range(1, group), 0]]
    main_info = jnp.stack([begin, end, *starts]).astype(jnp.int32)
    tail_info = jnp.stack([begin, end, base - tail_rows]).astype(jnp.int32)
    calls, size = [[0], []], 0
    for j in range(1, group + 1):
        if calls[-1] and size + span > 3 * span:
            calls.append([])
            size = 0
        calls[-1].append(j)
        size += span
    core = lax.axis_index("seq") % 2
    places = []
    for call in calls:
        spots = [v for j in call for v in (begin, end, (base - tail_rows, *starts)[j])]
        places.append(jnp.stack([core, *spots, scene]).astype(jnp.int32))

    lat_parts = sort_rows(scene_info, lat, scenes)
    others = [exchange(tok, k) for k in range(1, group)]
    lat_in = across(lat_parts)
    cot_parts = sort_rows(scene_info, after(cot, lat_parts), scenes)
    own_kv = keys_values(after(tok, cot_parts), gt, w_key, w_value)
    lat_in, others, cot_parts, own_kv, main_info, tail_info, places = lax.optimization_barrier(
        (lat_in, others, cot_parts, own_kv, main_info, tail_info, places)
    )
    cot_near = exchange(cot_parts[1], group)

    pieces = [tok, *others]
    lowest = (group * span - tail_rows) // span
    needed = []
    for owner in range(lowest, group):
        block = pieces[owner]
        for m in range(1, group):
            block = jnp.where(member == m, pieces[owner ^ m], block)
        needed.append(block)
    needed = jnp.concatenate(needed, axis=0) if len(needed) > 1 else needed[0]
    pairs = [(i, i + group) for i in range(blocks - group)]
    sent = needed[needed.shape[0] - tail_rows :]
    tail = lax.ppermute(sent, "blk", pairs)
    fresh = list(others) if group == 2 else []
    given = [own_kv] if fresh else [keys_values(piece, gt, w_key, w_value) for piece in others] + [own_kv]
    made_keys, made_values = zip(*given)
    query, acc, top, total, lat_set, weights, keys, values = attend(
        main_info, lat_in, gl, w_query, after(fresh, sent), gt, w_key, w_value, made_keys, made_values, scale
    )
    tail, query, cot_parts, cot_near = lax.optimization_barrier((tail, query, cot_parts, cot_near))

    cot_in = [cot_parts[0], cot_near, *[exchange(cot_parts[k], group * k) for k in range(2, scenes)]]
    saved, out_parts = finish(
        tail_info, scenes, lat_set, query, acc, top, total, tail, gt, w_key, w_value, gm, w_out, w_up, w_down, scale
    )
    tail_key, tail_value, tail_weight, factor, mixed, mlp, state, inner, slope = saved
    cot_in, out_parts, slope = lax.optimization_barrier((cot_in, out_parts, slope))
    out_back = across(out_parts)
    d_state, d_late, d_early, late, early_delta, keep, send, d_wo, dg_mlp = mlp_back(
        sums.info, cot_in, slope, state, mixed, mlp, inner, factor, gm, w_out, w_up, w_down
    )

    out_back, keep, send, d_early, d_late = lax.optimization_barrier((out_back, keep, send, d_early, d_late))
    received = sums.to_core(send)
    pieces = [(tail_value, tail_weight, tail, tail_key)]
    pieces += [(values[j], weights[j], piece, keys[j]) for j, piece in enumerate((*others, tok))]
    extra = 16
    d_toks, kept = [], []
    for j, call in enumerate(calls):
        some_values, some_weights, some_tokens, some_keys = zip(*[pieces[p] for p in call])
        latents = (lat_set, gl, w_query, d_state, d_wo, dg_mlp) if j == len(calls) - 1 else ()
        grads = (d_early, early_delta) if j else (d_late, late)
        some, kept = attention_back(
            places[j], query, w_key, w_value, gt, grads, some_values, some_weights, some_tokens, some_keys, kept,
            latents, scenes, extra, scale,
        )
        d_toks += some
        if j == 0:
            received, d_toks, kept = lax.optimization_barrier((received, d_toks, kept))
            keep, *sends = sums.add_core(keep, received)
            d_early = after(d_early, keep)
            received = sums.to_quad(sends)
            d_tail = lax.ppermute(d_toks[0], "blk", [(j, i) for i, j in pairs])
    received, d_tail, d_toks, kept = lax.optimization_barrier((received, d_tail, d_toks, kept))
    _, *returned, own = d_toks
    d_lat_set, small_keep, small_send = kept

    returned = dict(enumerate(returned, 1))
    own_tail = []
    for owner in range(lowest, group):
        start = owner * span - (group * span - tail_rows)
        chunk = d_tail[max(start, 0) : start + span]
        chunk = jnp.pad(chunk, ((span - chunk.shape[0], 0), (0, 0)))
        for k in range(1, group):
            returned[k] = returned[k] + jnp.where(member == owner ^ k, chunk, 0)
        own_tail.append(jnp.where(member == owner, chunk, 0))
    small_got = sums.to_core(small_send)
    keep, *sends = sums.add_quad(keep, received)
    received = sums.to_line(sends)
    returned = [exchange(after(returned[k], keep), k) for k in range(1, group)]
    output = unsort_rows(scene_info, after(out_back, keep), scenes, BF16)
    small_got, received, output = lax.optimization_barrier((small_got, received, output))
    [shard] = sums.add_line(keep, received)
    small_keep, *small_sends = sums.add_core(small_keep, small_got, extra)
    small_got = sums.to_quad(small_sends)
    block = shard
    for j in range(sums.lines.bit_length() - 1):
        far = sums.flip(block, 0, 2 << j)
        if j == sums.lines.bit_length() - 2:
            small_got, far = lax.optimization_barrier((small_got, far))
        block = jnp.concatenate([block, far], axis=0)
    half = block.shape[0] // 2
    near_a, near_b = block[:half], block[half:]
    far_a, far_b = sums.flip(near_a, 0, 1), sums.flip(near_b, 2, 0)
    small_keep, *small_sends = sums.add_quad(small_keep, small_got, extra)
    small_got = sums.to_line(small_sends)
    small_got, far_a, far_b, returned = lax.optimization_barrier((small_got, far_a, far_b, returned))
    two_a, two_b = jnp.concatenate([near_a, far_a], axis=0), jnp.concatenate([near_b, far_b], axis=0)
    last_a, last_b = sums.flip(two_a, 2, 0), sums.flip(two_b, 0, 1)
    small_shard, gains = sums.add_line(small_keep, small_got, extra)
    small_block = small_shard
    for j in range(sums.lines.bit_length() - 1):
        far = sums.flip(small_block, 0, 2 << j)
        if j == sums.lines.bit_length() - 2:
            d_tokens = token_back(tok, gt, [own, *own_tail, *after(returned, small_block)])
            far = after(far, d_tokens)
        small_block = jnp.concatenate([small_block, far], axis=0)
    other_a, other_b = sums.to_core(two_a), sums.to_core(two_b)
    last_a, last_b, small_block, other_a, other_b = lax.optimization_barrier(
        (last_a, last_b, small_block, other_a, other_b)
    )
    leaving = after(d_lat_set, small_block)
    d_lat_back = lax.all_to_all(leaving, "blk", 0, 0, axis_index_groups=lines, tiled=True)
    small_got = sums.to_quad([small_block] * 3)
    mine = [two_a, last_a, two_b, last_b]
    other = [other_a, sums.to_core(last_a), other_b, sums.to_core(last_b)]
    d_w_down, d_w_up = sums.unpack(mine, other, [(hidden, width), (width, hidden)], crossed=True)
    small_got = after(small_got, d_w_up)
    small_mine = [small_block, *small_got]
    small_other = [sums.to_core(v) for v in small_mine]
    squares = sums.unpack(small_mine, small_other, [(width, width)] * 4)
    d_latents = unsort_rows(0 * scene_info, [after(d_lat_back, *squares)], scenes, F32)
    gains = gains.astype(F32)
    return (output[None], d_latents[None], d_tokens[None], *squares, d_w_up, d_w_down, gains[0], gains[1], gains[2])


def solution(mesh):
    split = P("seq", "blk", None)
    in_specs = (split, split, P("seq", None)) + (P(),) * 9 + (split,)
    out_specs = (split,) * 3 + (P(),) * 9
    return jax.shard_map(
        functools.partial(local, dict(mesh.shape)), mesh=mesh, in_specs=in_specs, out_specs=out_specs, check_vma=False
    )
```
